32 devices in a mesh: rep: 4 (over x, core), shard: 8 (over z, y).
Axes of the slice: x: 2, y: 2, z: 4, core: 2. Of those that a mesh axis runs over, the one named last changes fastest.
Arguments:
- tokens: bfloat16 [64, 1024, 768], P(('rep', 'shard')), may hold values from -6 to 6
- cotangent: bfloat16 [64, 1024, 768], P(('rep', 'shard')), may hold values from -6 to 6
- lengths: int32 [64], P(('rep', 'shard')), may hold values from 256 to 1024, as said below
- widen_weight: bfloat16 [768, 3328], P('shard'), may hold values from -0.21875 to 0.21875
- timestep_weight: bfloat16 [768, 48], P('shard'), may hold values from -0.21875 to 0.21875
- narrow_weight: bfloat16 [1536, 768], P('shard'), may hold values from -0.15625 to 0.15625
- filter_weight: bfloat16 [4, 1792], P(None, 'shard'), may hold values from -3 to 3
- filter_offset: bfloat16 [1792], P('shard'), may hold values from -3 to 3
- prenorm_gain: bfloat16 [768], P('shard'), may hold values from 0.099609375 to 1.8984375
- postnorm_gain: bfloat16 [1536], P('shard'), may hold values from 0.099609375 to 1.8984375
- timestep_bias: float32 [48], replicated, may hold values from -7 to -2.3
- decay_log: float32 [24], replicated, may hold values from 0 to 2.77
- skip_gain: float32 [24], replicated, may hold values from 0.5 to 1.5
Outputs:
- result: bfloat16 [64, 1024, 768], P(('rep', 'shard'))
- tokens_gradient: bfloat16 [64, 1024, 768], P(('rep', 'shard'))
- widen_gradient: float32 [768, 3328], P('shard')
- timestep_gradient: float32 [768, 48], P('shard')
- narrow_gradient: float32 [1536, 768], P('shard')
- filter_gradient: float32 [4, 1792], P(None, 'shard')
- offset_gradient: float32 [1792], P('shard')
- prenorm_gradient: float32 [768], P('shard')
- postnorm_gradient: float32 [1536], P('shard')
- bias_gradient: float32 [48], replicated
- decay_gradient: float32 [24], replicated
- skip_gradient: float32 [24], replicated
The draws below stay inside these ranges and needn't reach their ends.
Inputs may be any that keep to these rules, and one draw needn't show every extreme that they name: `lengths`: each length lies between a quarter of 1024 and 1024; some sequence has exactly 1024.
All inputs are finite; a program needn't handle non-finite values.
Results may differ from the reference program's by a relative error of at most 0.0082.
Values may be sent and summed in bfloat16 or wider, within the bound.
A program may use at most 384 MiB of HBM per device.

```python
from functools import partial
import jax
import jax.numpy as jnp
from jax import lax

D = 768
HEADS = 24
HEADDIM = 64
STATE = 64
CONV = 4
SEQ = 1024
INNER = 1536
CHANNELS = 1792
SEQS = 64


def draw_lengths(key, part):
    first, second = jax.random.split(jax.random.fold_in(key, 17))
    values = jax.random.randint(first, (SEQS,), SEQ // 4, SEQ + 1)
    spot = jax.random.randint(second, (), 0, SEQS)
    return values.at[spot].set(SEQ).astype(jnp.int32)


def block_scale(key, extent, pieces, least, high):
    loudness = 1.0
    for position, shards_of in pieces:
        steps = jax.random.uniform(jax.random.fold_in(jax.random.fold_in(key, 6), position), (shards_of,), jnp.float32, least / len(pieces), high / len(pieces))
        loudness = loudness * jnp.repeat(jnp.exp(steps), extent[position] // shards_of).reshape((-1,) + (1,) * (len(extent) - 1 - position))
    return loudness


def normal_values(stream_key, shape, scale, limit, cuts=(), kind=jnp.bfloat16):
    result = scale * jax.random.normal(stream_key, shape, jnp.float32)
    if cuts:
        result = result * block_scale(stream_key, shape, cuts, -0.22, 0.18)
    return jnp.clip(result, -limit, limit).astype(kind)


def setup_inputs(seed: int = 0) -> dict:
    seeds = jax.random.split(jax.random.key(seed), 14)
    return {
        "tokens": normal_values(seeds[0], (SEQS, SEQ, D), 1.0, 6.0, ((0, 32),)),
        "cotangent": normal_values(seeds[1], (SEQS, SEQ, D), 1.0, 6.0, ((0, 32),)),
        "lengths": draw_lengths(jax.random.fold_in(seeds[13], 71), 0),
        "widen_weight": normal_values(seeds[3], (D, INNER + CHANNELS), D ** -0.5, 0.21875, ((0, 8),)),
        "timestep_weight": normal_values(seeds[4], (D, 2 * HEADS), D ** -0.5, 0.21875, ((0, 8),)),
        "narrow_weight": normal_values(seeds[5], (INNER, D), INNER ** -0.5, 0.15625, ((0, 8),)),
        "filter_weight": normal_values(seeds[6], (CONV, CHANNELS), CONV ** -0.5, 3.0, ((1, 8),)),
        "filter_offset": normal_values(seeds[7], (CHANNELS,), 0.5, 3.0, ((0, 8),)),
        "prenorm_gain": jnp.clip(1.0 + 0.18 * jax.random.normal(seeds[8], (D,), jnp.float32), 0.099609375, 1.8984375).astype(jnp.bfloat16),
        "postnorm_gain": jnp.clip(1.0 + 0.18 * jax.random.normal(seeds[9], (INNER,), jnp.float32), 0.099609375, 1.8984375).astype(jnp.bfloat16),
        "timestep_bias": jnp.clip(jax.random.uniform(seeds[10], (2 * HEADS,), jnp.float32, -7.0, -2.3), -7.0, -2.3),
        "decay_log": jnp.clip(jax.random.uniform(seeds[11], (HEADS,), jnp.float32, 0.0, 2.77), 0.0, 2.77),
        "skip_gain": jnp.clip(jax.random.uniform(seeds[12], (HEADS,), jnp.float32, 0.5, 1.5), 0.5, 1.5),
    }


@jax.custom_vjp
def low(v):
    return lax.optimization_barrier(v.astype(jnp.bfloat16)).astype(jnp.float32)

@jax.custom_vjp
def low_back(v):
    return v

def low_keep(v):
    return (low(v), None)

def low_pass(kept, grad):
    return (grad,)

def back_keep(v):
    return (v, None)

def back_low(kept, grad):
    return (low(grad),)
low.defvjp(low_keep, low_pass)
low_back.defvjp(back_keep, back_low)
epsilon = 1e-05
precise = lax.Precision.HIGHEST

def normalize(values, gain):
    return values * lax.rsqrt(lax.optimization_barrier(jnp.mean(values * values, axis=-1, keepdims=True)) + epsilon) * gain

def direction(values, steps, rate, inputs_b, outputs_c):
    length = values.shape[0]
    cums = jnp.cumsum(steps * rate, axis=0).T
    lower = lax.broadcasted_iota(jnp.int32, (length, length), 0) > lax.broadcasted_iota(jnp.int32, (length, length), 1)
    spread = cums[:, :, None] - cums[:, None, :]
    decay = jnp.where(lower, jnp.exp(jnp.where(lower, spread, 0.0)), 0.0)
    scores = jnp.dot(outputs_c, inputs_b.T, precision=precise)
    weights = decay * scores[None] * steps.T[:, None, :]
    return jnp.einsum('hts,shp->thp', weights, values, precision=precise)

def mixer_block(projected, raw_steps, filter_weight, filter_offset, timestep_bias, decay_log, skip_gain, postnorm_gain, mask, scanner):
    length = projected.shape[0]
    gate = projected[:, :INNER]
    filter_input = projected[:, INNER:]
    padded = jnp.pad(filter_input, ((CONV - 1, 0), (0, 0)))
    filtered = filter_offset + jnp.zeros_like(filter_input)
    for place in range(CONV):
        filtered = filtered + filter_weight[place] * padded[place:place + length]
    active = jax.nn.silu(filtered)
    values = (active[:, :INNER] * mask).reshape(length, HEADS, HEADDIM)
    forward_in = active[:, INNER:INNER + STATE]
    forward_out = active[:, INNER + STATE:INNER + 2 * STATE]
    reverse_in = active[:, INNER + 2 * STATE:INNER + 3 * STATE]
    reverse_out = active[:, INNER + 3 * STATE:]
    steps = jax.nn.softplus(raw_steps + timestep_bias)
    rate = -jnp.exp(decay_log)
    ahead = scanner(values, steps[:, :HEADS], rate, forward_in, forward_out)
    behind = jnp.flip(scanner(jnp.flip(values, 0), jnp.flip(steps[:, HEADS:], 0), rate, jnp.flip(reverse_in, 0), jnp.flip(reverse_out, 0)), 0)
    mixed = (ahead + behind + skip_gain[:, None] * values).reshape(length, INNER)
    return normalize(mixed * jax.nn.silu(gate), postnorm_gain)

def reference(tokens, cotangent, lengths, widen_weight, timestep_weight, narrow_weight, filter_weight, filter_offset, prenorm_gain, postnorm_gain, timestep_bias, decay_log, skip_gain):
    params = (widen_weight.astype(jnp.float32), timestep_weight.astype(jnp.float32), narrow_weight.astype(jnp.float32), filter_weight.astype(jnp.float32), filter_offset.astype(jnp.float32), prenorm_gain.astype(jnp.float32), postnorm_gain.astype(jnp.float32), timestep_bias, decay_log, skip_gain)
    scanner = jax.checkpoint(direction)

    def layer(mask, row, widen, timestep, narrow, smoother, shifter, prenorm, postnorm, biasing, decaying, skipping):
        normed = low(normalize(row, prenorm))
        projected = low_back(jnp.dot(normed, widen, precision=precise))
        raw_steps = low_back(jnp.dot(normed, timestep, precision=precise))
        gnormed = low(mixer_block(projected, raw_steps, smoother, shifter, biasing, decaying, skipping, postnorm, mask, scanner))
        branch = low_back(jnp.dot(gnormed, narrow, precision=precise))
        return row + mask * branch

    def visit(totals, inputs):
        row, slope, length = inputs
        mask = (lax.iota(jnp.int32, SEQ) < length).astype(jnp.float32)[:, None]
        result_row, pullback = jax.vjp(partial(layer, mask), row.astype(jnp.float32), *params)
        grads = pullback(slope.astype(jnp.float32))
        totals = tuple((total + grad for total, grad in zip(totals, grads[1:])))
        return (totals, (result_row.astype(jnp.bfloat16), grads[0].astype(jnp.bfloat16)))
    zeros = tuple((jnp.zeros(parameter.shape, jnp.float32) for parameter in params))
    totals, outputs = lax.scan(visit, zeros, (tokens, cotangent, lengths))
    return (outputs[0], outputs[1], totals[0], totals[1], totals[2], totals[3], totals[4], totals[5], totals[6], totals[7], totals[8], totals[9])
```

```python
from functools import partial

import jax
import jax.numpy as jnp
from jax import lax
from jax.experimental import pallas as pl
from jax.experimental.pallas import tpu as pltpu
from jax.sharding import PartitionSpec as P

HEADS = 24
HEADDIM = 64
STATE = 64
CONV = 4
INNER = 1536
CHANNELS = 1792
D = 768
WIDE = INNER + CHANNELS
SPAN = 128
BLOCK = 256
SUBS = BLOCK // SPAN
EPS = 1e-05
LOG2E = 1.4426950408889634
TINY = 1.2e-38
f32 = jnp.float32
bf16 = jnp.bfloat16
precise = lax.Precision.HIGHEST
VMEM_LIMIT = 60 * 1024 * 1024


def mm(a, b, precision=None):
    return lax.dot_general(
        a, b, (((1,), (0,)), ((), ())), precision=precision, preferred_element_type=f32
    )


def mm_nt(a, b):
    return lax.dot_general(a, b, (((1,), (1,)), ((), ())), preferred_element_type=f32)


def mm_tn(a, b):
    return lax.dot_general(a, b, (((0,), (0,)), ((), ())), preferred_element_type=f32)


def sigmoid(v):
    return 0.5 * jnp.tanh(0.5 * v) + 0.5


def iotas(shape):
    return (
        lax.broadcasted_iota(jnp.int32, shape, 0),
        lax.broadcasted_iota(jnp.int32, shape, 1),
    )


def step_sums(x, rate):
    rows, cols = iotas((SPAN, SPAN))
    steps = jnp.maximum(x, 0.0) + jnp.log1p(jnp.exp(-jnp.abs(x)))
    scaled = steps * rate
    fcum = mm(scaled[:HEADS], (rows <= cols).astype(f32), precise)
    rcum = mm(scaled[HEADS:], (rows >= cols).astype(f32), precise)
    return steps, fcum, rcum


def span_tails(steps, fcum, rcum):
    tail_f = jnp.exp2(fcum[:, SPAN - 1 :] - fcum) * steps[:HEADS]
    tail_r = jnp.exp2(rcum[:, :1] - rcum) * steps[HEADS:]
    return tail_f, tail_r


def enter_kernel(
    len_ref,
    tok_ref,
    wide_ref,
    time_ref,
    pre_ref,
    taps_ref,
    bias_ref,
    rate_ref,
    gate_o,
    fin_o,
    filt_o,
    act_o,
    x_o,
    state_o,
    proj_s,
    run_s,
):
    seq = pl.program_id(0)
    block = pl.program_id(1)
    length = len_ref[seq]

    @pl.when(block == 0)
    def _():
        proj_s[:, BLOCK:] = jnp.zeros((CHANNELS, SPAN), f32)
        run_s[...] = jnp.zeros_like(run_s)

    @pl.when(block * BLOCK < length)
    def _():
        tok = tok_ref[0].astype(f32)
        scale = lax.rsqrt(jnp.mean(tok * tok, axis=-1, keepdims=True) + EPS)
        normed = (tok * scale * pre_ref[...]).astype(bf16)
        x_o[0] = mm_nt(time_ref[...], normed) + bias_ref[...]
        proj_s[:, :SPAN] = proj_s[:, BLOCK:]
        for i in range(INNER // 256):
            gate_o[0, i * 256 : (i + 1) * 256, :] = mm_nt(
                wide_ref[i * 256 : (i + 1) * 256, :], normed
            ).astype(bf16)
        for i in range(CHANNELS // 256):
            proj_s[i * 256 : (i + 1) * 256, SPAN:] = mm_nt(
                wide_ref[INNER + i * 256 : INNER + (i + 1) * 256, :], normed
            )
        place = block * BLOCK + lax.broadcasted_iota(jnp.int32, (1, BLOCK), 1)
        mask = (place < length).astype(f32)

        def filter_rows(i, masked):
            r = pl.ds(pl.multiple_of(i * 32, 32), 32)
            w = proj_s[r, :]
            taps = taps_ref[r, :]
            acc = taps[:, 4:5] + taps[:, 3:4] * w[:, SPAN:]
            for lag in range(1, CONV):
                moved = pltpu.roll(w, lag, 1)[:, SPAN:]
                acc = acc + taps[:, 3 - lag : 4 - lag] * moved
            fin_o[0, r, :] = w[:, SPAN:].astype(bf16)
            filt_o[0, r, :] = acc.astype(bf16)
            act = acc * sigmoid(acc)
            if masked:
                act = act * mask
            act_o[0, r, :] = act.astype(bf16)

        lax.fori_loop(0, INNER // 32, lambda i, _: filter_rows(i, True), None)
        lax.fori_loop(INNER // 32, CHANNELS // 32, lambda i, _: filter_rows(i, False), None)

        lane = lax.broadcasted_iota(jnp.int32, (1, SPAN), 1)

        def span(sub, _):
            cols = pl.ds(pl.multiple_of(sub * SPAN, SPAN), SPAN)
            steps, fcum, rcum = step_sums(x_o[0, :, cols], rate_ref[...])
            tail_f, tail_r = span_tails(steps, fcum, rcum)
            decay = jnp.exp2(fcum[:, SPAN - 1 :])
            ins_f = act_o[0, INNER : INNER + 64, cols].astype(f32)
            ins_r = act_o[0, INNER + 128 : INNER + 192, cols].astype(f32)
            for h in range(HEADS):
                rows = slice(h * 64, (h + 1) * 64)
                weighted = jnp.concatenate(
                    [
                        (ins_f * tail_f[h : h + 1]).astype(bf16),
                        (ins_r * tail_r[h : h + 1]).astype(bf16),
                    ],
                    axis=0,
                )
                fresh = mm_nt(act_o[0, rows, cols], weighted)
                run = run_s[rows, :]
                state_o[0, sub, rows, :] = jnp.where(lane < 64, run, fresh)
                run_s[rows, :] = run * decay[h : h + 1] + fresh
            return None

        lax.fori_loop(0, SUBS, span, None)


def middle_kernel(
    len_ref,
    skip_ref,
    tok_ref,
    cot_ref,
    gate_ref,
    act_ref,
    x_ref,
    state_ref,
    narrow_ref,
    turned_ref,
    post_ref,
    rate_ref,
    result_o,
    dgate_o,
    dval_o,
    dio_o,
    sums_o,
    dstate_o,
    rstate_o,
    narrow_o,
    post_o,
    skip_o,
    run_s,
    grun_s,
    mixed_s,
    gated_s,
    dgn_s,
    spread_s,
    matrix_s,
    held_s,
):
    seq = pl.program_id(0)
    step = pl.program_id(1)
    block = pl.num_programs(1) - 1 - step
    length = len_ref[seq]

    @pl.when((seq == 0) & (step == 0))
    def _():
        narrow_o[...] = jnp.zeros_like(narrow_o)
        post_o[...] = jnp.zeros_like(post_o)
        skip_o[...] = jnp.zeros_like(skip_o)

    @pl.when(step == 0)
    def _():
        run_s[...] = jnp.zeros_like(run_s)
        grun_s[...] = jnp.zeros_like(grun_s)

    @pl.when(block * BLOCK >= length)
    def _():
        result_o[...] = tok_ref[...]

    @pl.when(block * BLOCK < length)
    def _():
        rows_i, cols_i = iotas((SPAN, SPAN))
        lower = rows_i < cols_i
        upper = rows_i > cols_i
        lane = lax.broadcasted_iota(jnp.int32, (1, SPAN), 1)

        def span_scores(cols):
            fi = act_ref[0, INNER : INNER + 64, cols]
            fo = act_ref[0, INNER + 64 : INNER + 128, cols]
            ri = act_ref[0, INNER + 128 : INNER + 192, cols]
            ro = act_ref[0, INNER + 192 : INNER + 256, cols]
            ahead = mm_tn(fi, fo)
            behind = mm_tn(ri, ro)
            scores = jnp.where(lower, ahead, jnp.where(upper, behind, 0.0))
            return fi, fo, ri, ro, scores

        def forward_span(back, _):
            sub = SUBS - 1 - back
            cols = pl.ds(pl.multiple_of(sub * SPAN, SPAN), SPAN)
            steps, fcum, rcum = step_sums(x_ref[0, :, cols], rate_ref[...])
            least = jnp.log2(jnp.maximum(steps, TINY))
            columns = jnp.concatenate(
                [fcum - least[:HEADS], rcum - least[HEADS:], jnp.zeros((SPAN - 48, SPAN), f32)],
                axis=0,
            ).T
            out_f = jnp.exp2(fcum)
            out_r = jnp.exp2(rcum)
            decay = jnp.exp2(rcum[:, :1])
            fi, fo, ri, ro, scores = span_scores(cols)
            fo = fo.astype(f32)
            ro = ro.astype(f32)
            for h in range(HEADS):
                rows = slice(h * 64, (h + 1) * 64)
                power = jnp.where(
                    lower,
                    fcum[h : h + 1] - columns[:, h : h + 1],
                    rcum[h : h + 1] - columns[:, HEADS + h : HEADS + h + 1],
                )
                spread = jnp.exp2(power)
                spread_s[sub, h] = spread.astype(bf16)
                matrix = jnp.concatenate(
                    [
                        (spread * scores).astype(bf16),
                        (fo * out_f[h : h + 1]).astype(bf16),
                        (ro * out_r[h : h + 1]).astype(bf16),
                    ],
                    axis=0,
                )
                matrix_s[sub, h] = matrix
                state = state_ref[0, sub, rows, :]
                run = run_s[rows, :]
                rstate_o[0, sub, rows, :] = run
                held = jnp.where(lane < 64, state, run).astype(bf16)
                held_s[sub, rows, :] = held
                run_s[rows, :] = run * decay[h : h + 1] + state
                values = act_ref[0, rows, cols]
                both = jnp.concatenate([values, held], axis=1)
                mixed_s[rows, cols] = mm(both, matrix) + skip_ref[h] * values.astype(f32)
            return None

        lax.fori_loop(0, SUBS, forward_span, None)

        def gate_rows(i, total):
            r = pl.ds(pl.multiple_of(i * 32, 32), 32)
            gate = gate_ref[0, r, :].astype(f32)
            gated = mixed_s[r, :] * (gate * sigmoid(gate))
            gated_s[r, :] = gated
            return total + jnp.sum((gated * gated).reshape(4, 8, BLOCK), axis=0)

        squares = lax.fori_loop(0, INNER // 32, gate_rows, jnp.zeros((8, BLOCK), f32))
        rs = lax.rsqrt(jnp.sum(squares, axis=0, keepdims=True) * (1.0 / INNER) + EPS)

        def norm_rows(i, _):
            r = pl.ds(pl.multiple_of(i * 32, 32), 32)
            held_gn = gated_s[r, :] * rs * post_ref[r, :1]
            dgate_o[0, r, :] = held_gn.astype(bf16)
            return None

        lax.fori_loop(0, INNER // 32, norm_rows, None)
        gnormed = dgate_o[0]
        place = block * BLOCK + lax.broadcasted_iota(jnp.int32, (BLOCK, 1), 0)
        inside = place < length
        branch = mm(turned_ref[...], gnormed)
        result_o[0] = (tok_ref[0].astype(f32) + jnp.where(inside, branch.T, 0.0)).astype(bf16)
        slope = jnp.where(inside, cot_ref[0].astype(f32), 0.0).astype(bf16)
        for i in range(3):
            rows = slice(i * 512, (i + 1) * 512)
            narrow_o[rows, :] += mm(gnormed[rows], slope)
            dgn_s[rows, :] = mm_nt(narrow_ref[rows, :], slope)

        def dot_rows(i, total):
            r = pl.ds(pl.multiple_of(i * 32, 32), 32)
            product = dgn_s[r, :] * gated_s[r, :]
            kept = product * rs
            post_o[r, :] += kept[:, :SPAN] + kept[:, SPAN:]
            weighted = product * post_ref[r, :1]
            return total + jnp.sum(weighted.reshape(4, 8, BLOCK), axis=0)

        dots = lax.fori_loop(0, INNER // 32, dot_rows, jnp.zeros((8, BLOCK), f32))
        mean = jnp.sum(dots, axis=0, keepdims=True) * (1.0 / INNER)
        pull = rs * rs * rs * mean

        def grad_rows(i, _):
            r = pl.ds(pl.multiple_of(i * 32, 32), 32)
            gate = gate_ref[0, r, :].astype(f32)
            sig = sigmoid(gate)
            dgated = rs * post_ref[r, :1] * dgn_s[r, :] - gated_s[r, :] * pull
            dmixed = dgated * (gate * sig)
            dgate = dgated * mixed_s[r, :] * (sig * (1.0 + gate * (1.0 - sig)))
            dgate_o[0, r, :] = dgate.astype(bf16)
            dgn_s[r, :] = dmixed
            product = dmixed * act_ref[0, r, :].astype(f32)
            skip_o[r, :] += product[:, :SPAN] + product[:, SPAN:]
            return None

        lax.fori_loop(0, INNER // 32, grad_rows, None)

        ones_row = (lax.broadcasted_iota(jnp.int32, (8, 2 * SPAN), 1) // SPAN) == (
            lax.broadcasted_iota(jnp.int32, (8, 2 * SPAN), 0)
        )
        ones_row = ones_row.astype(bf16)
        ones_flat = jnp.ones((8, SPAN), bf16)

        def backward_span(back, _):
            sub = SUBS - 1 - back
            cols = pl.ds(pl.multiple_of(sub * SPAN, SPAN), SPAN)
            steps, fcum, rcum = step_sums(x_ref[0, :, cols], rate_ref[...])
            out_f = jnp.exp2(fcum)
            out_r = jnp.exp2(rcum)
            decay = jnp.exp2(fcum[:, SPAN - 1 :])
            fi, fo, ri, ro, scores = span_scores(cols)
            fo32 = fo.astype(f32)
            ro32 = ro.astype(f32)
            dscores = jnp.zeros((SPAN, SPAN), f32)
            dfo = jnp.zeros((64, SPAN), f32)
            dro = jnp.zeros((64, SPAN), f32)
            for h in range(HEADS):
                rows = slice(h * 64, (h + 1) * 64)
                dmixed = dgn_s[rows, cols]
                dm = dmixed.astype(bf16)
                values = act_ref[0, rows, cols]
                held = held_s[sub, rows, :]
                both = jnp.concatenate([values, held], axis=1)
                grad = mm_tn(both, dm)
                matrix = matrix_s[sub, h]
                first = grad[:SPAN] * spread_s[sub, h].astype(f32)
                dscores = dscores + first
                pairs = first * scores
                pairs_low = jnp.where(lower, pairs, 0.0).astype(bf16)
                stack = jnp.concatenate([pairs_low, pairs.astype(bf16)], axis=0)
                by_row = mm(ones_row, stack)
                by_col = mm_nt(ones_flat, stack)
                part_f = grad[SPAN : SPAN + 64] * out_f[h : h + 1]
                part_r = grad[SPAN + 64 :] * out_r[h : h + 1]
                dfo = dfo + part_f
                dro = dro + part_r
                carried_f = jnp.sum(part_f * fo32, axis=0, keepdims=True)
                carried_r = jnp.sum(part_r * ro32, axis=0, keepdims=True)
                col_f = by_col[:1, :SPAN]
                sums_o[0, h : h + 1, cols] = by_row[:1] + carried_f
                sums_o[0, HEADS + h : HEADS + h + 1, cols] = (
                    by_row[1:2] - by_row[:1] + carried_r
                )
                sums_o[0, 2 * HEADS + h : 2 * HEADS + h + 1, cols] = col_f
                sums_o[0, 3 * HEADS + h : 3 * HEADS + h + 1, cols] = by_col[:1, SPAN:] - col_f
                dboth = mm_nt(dm, matrix)
                dval_o[0, rows, cols] = (dboth[:, :SPAN] + skip_ref[h] * dmixed).astype(bf16)
                dheld = dboth[:, SPAN:]
                run = grun_s[rows, :]
                dstate_o[0, sub, rows, :] = jnp.where(lane < 64, run, dheld)
                sums_o[0, 4 * HEADS + h : 4 * HEADS + h + 1, cols] = decay[h : h + 1] * jnp.sum(
                    jnp.where(lane < 64, run * held.astype(f32), 0.0), axis=0, keepdims=True
                )
                grun_s[rows, :] = run * decay[h : h + 1] + dheld
            low = jnp.where(lower, dscores, 0.0).astype(bf16)
            high = jnp.where(upper, dscores, 0.0).astype(bf16)
            dio_o[0, 0:64, cols] = mm_nt(fo, low)
            dio_o[0, 64:128, cols] = dfo + mm(fi, low)
            dio_o[0, 128:192, cols] = mm_nt(ro, high)
            dio_o[0, 192:256, cols] = dro + mm(ri, high)
            return None

        lax.fori_loop(0, SUBS, backward_span, None)


def leave_kernel(
    len_ref,
    filt_ref,
    act_ref,
    fin_ref,
    x_ref,
    dval_ref,
    dio_ref,
    sums_ref,
    dstate_ref,
    rstate_ref,
    rate_ref,
    dfilt_o,
    draw_o,
    offset_o,
    taps_o,
    bias_o,
    decay_o,
    grun_s,
    near_s,
    dact_s,
    last_s,
):
    seq = pl.program_id(0)
    block = pl.program_id(1)
    length = len_ref[seq]

    @pl.when((seq == 0) & (block == 0))
    def _():
        offset_o[...] = jnp.zeros_like(offset_o)
        taps_o[...] = jnp.zeros_like(taps_o)
        bias_o[...] = jnp.zeros_like(bias_o)
        decay_o[...] = jnp.zeros_like(decay_o)

    @pl.when(block == 0)
    def _():
        grun_s[...] = jnp.zeros_like(grun_s)
        last_s[...] = jnp.zeros_like(last_s)

    @pl.when(block * BLOCK < length)
    def _():
        rows_i, cols_i = iotas((SPAN, SPAN))
        lane = lax.broadcasted_iota(jnp.int32, (1, SPAN), 1)

        def span(sub, _):
            cols = pl.ds(pl.multiple_of(sub * SPAN, SPAN), SPAN)
            x = x_ref[0, :, cols]
            steps, fcum, rcum = step_sums(x, rate_ref[...])
            tail_f, tail_r = span_tails(steps, fcum, rcum)
            decay = jnp.exp2(rcum[:, :1])
            fi = act_ref[0, INNER : INNER + 64, cols].astype(f32)
            ri = act_ref[0, INNER + 128 : INNER + 192, cols].astype(f32)
            dfi = jnp.zeros((64, SPAN), f32)
            dri = jnp.zeros((64, SPAN), f32)
            ends_f = []
            ends_r = []
            for h in range(HEADS):
                rows = slice(h * 64, (h + 1) * 64)
                weighted = jnp.concatenate(
                    [
                        (fi * tail_f[h : h + 1]).astype(bf16),
                        (ri * tail_r[h : h + 1]).astype(bf16),
                    ],
                    axis=0,
                )
                dstate = dstate_ref[0, sub, rows, :]
                run = grun_s[rows, :]
                dfresh = jnp.where(lane < 64, dstate, run).astype(bf16)
                near_s[h : h + 1, :] = decay[h : h + 1] * jnp.sum(
                    jnp.where(lane < 64, 0.0, run * rstate_ref[0, sub, rows, :]),
                    axis=0,
                    keepdims=True,
                )
                grun_s[rows, :] = run * decay[h : h + 1] + dstate
                values = act_ref[0, rows, cols]
                dact_s[rows, cols] = dval_ref[0, rows, cols].astype(f32) + mm(dfresh, weighted)
                dweighted = mm_tn(dfresh, values)
                part_f = dweighted[:64] * tail_f[h : h + 1]
                part_r = dweighted[64:] * tail_r[h : h + 1]
                dfi = dfi + part_f
                dri = dri + part_r
                ends_f.append(jnp.sum(part_f * fi, axis=0, keepdims=True))
                ends_r.append(jnp.sum(part_r * ri, axis=0, keepdims=True))
            dact_s[INNER : INNER + 64, cols] = dio_ref[0, 0:64, cols] + dfi
            dact_s[INNER + 64 : INNER + 128, cols] = dio_ref[0, 64:128, cols]
            dact_s[INNER + 128 : INNER + 192, cols] = dio_ref[0, 128:192, cols] + dri
            dact_s[INNER + 192 : INNER + 256, cols] = dio_ref[0, 192:256, cols]
            ends_f = jnp.concatenate(ends_f, axis=0)
            ends_r = jnp.concatenate(ends_r, axis=0)
            col_f = sums_ref[0, 2 * HEADS : 3 * HEADS, cols]
            col_r = sums_ref[0, 3 * HEADS : 4 * HEADS, cols]
            far_f = jnp.sum(sums_ref[0, 4 * HEADS :, cols], axis=1, keepdims=True)
            far_r = jnp.sum(near_s[...], axis=1, keepdims=True)
            dfa = mm(sums_ref[0, :HEADS, cols] - col_f, (rows_i >= cols_i).astype(f32), precise)
            dra = mm(
                sums_ref[0, HEADS : 2 * HEADS, cols] - col_r,
                (rows_i <= cols_i).astype(f32),
                precise,
            )
            dfa = dfa + far_f + mm(ends_f, (rows_i < cols_i).astype(f32), precise)
            dra = dra + far_r + mm(ends_r, (rows_i > cols_i).astype(f32), precise)
            sig = jax.nn.sigmoid(x)
            rate = rate_ref[...] * (1.0 / LOG2E)
            share = sig / jnp.maximum(steps, TINY)
            span_d = jnp.concatenate([dfa, dra], axis=0)
            draw = jnp.concatenate([col_f + ends_f, col_r + ends_r], axis=0) * share + span_d * (rate * sig)
            draw_o[0, :, cols] = draw.astype(bf16)
            bias_o[...] += draw
            decay_o[...] += span_d * steps * rate
            return None

        lax.fori_loop(0, SUBS, span, None)
        place = block * BLOCK + lax.broadcasted_iota(jnp.int32, (1, BLOCK), 1)
        mask = (place < length).astype(f32)

        def filter_rows(i, masked):
            r = pl.ds(pl.multiple_of(i * 32, 32), 32)
            filt = filt_ref[0, r, :].astype(f32)
            sig = sigmoid(filt)
            dact = dact_s[r, :]
            if masked:
                dact = dact * mask
            dfilt = dact * (sig * (1.0 + filt * (1.0 - sig)))
            dfilt_o[0, r, :] = dfilt.astype(bf16)
            offset_o[r, :] += dfilt[:, :SPAN] + dfilt[:, SPAN:]
            fin = fin_ref[0, r, :].astype(f32)
            w = jnp.concatenate([last_s[r, :], fin], axis=1)
            last_s[r, :] = fin[:, SPAN:]
            product = dfilt * fin
            taps_o[3, r, :] += product[:, :SPAN] + product[:, SPAN:]
            for lag in range(1, CONV):
                product = dfilt * pltpu.roll(w, lag, 1)[:, SPAN:]
                taps_o[3 - lag, r, :] += product[:, :SPAN] + product[:, SPAN:]
            return None

        lax.fori_loop(0, INNER // 32, lambda i, _: filter_rows(i, True), None)
        lax.fori_loop(INNER // 32, CHANNELS // 32, lambda i, _: filter_rows(i, False), None)


def widen_kernel(
    len_ref,
    tok_ref,
    cot_ref,
    dgate_ref,
    dfilt_ref,
    next_ref,
    draw_ref,
    wide_ref,
    time_ref,
    pre_ref,
    taps_ref,
    slope_o,
    wide_o,
    time_o,
    pre_o,
    dproj_s,
):
    seq = pl.program_id(0)
    block = pl.program_id(1)
    length = len_ref[seq]

    @pl.when((seq == 0) & (block == 0))
    def _():
        wide_o[...] = jnp.zeros_like(wide_o)
        time_o[...] = jnp.zeros_like(time_o)
        pre_o[...] = jnp.zeros_like(pre_o)

    @pl.when(block * BLOCK >= length)
    def _():
        slope_o[...] = cot_ref[...]

    @pl.when(block * BLOCK < length)
    def _():
        tok = tok_ref[0].astype(f32)
        scale = lax.rsqrt(jnp.mean(tok * tok, axis=-1, keepdims=True) + EPS)
        normed = (tok * scale * pre_ref[...]).astype(bf16)
        normed_t = normed.T
        dproj_s[:INNER, :] = dgate_ref[0]
        beyond = (block + 1) * BLOCK < length

        def filter_rows(i, _):
            r = pl.ds(pl.multiple_of(i * 32, 32), 32)
            following = jnp.where(beyond, next_ref[0, r, :].astype(f32), 0.0)
            w = jnp.concatenate([dfilt_ref[0, r, :].astype(f32), following], axis=1)
            taps = taps_ref[r, :]
            acc = taps[:, 3:4] * w[:, :BLOCK]
            for lag in range(1, CONV):
                moved = pltpu.roll(w, BLOCK + SPAN - lag, 1)[:, :BLOCK]
                acc = acc + taps[:, 3 - lag : 4 - lag] * moved
            dproj_s[pl.ds(pl.multiple_of(INNER + i * 32, 32), 32), :] = acc.astype(bf16)
            return None

        lax.fori_loop(0, CHANNELS // 32, filter_rows, None)
        for i in range(WIDE // 256):
            rows = slice(i * 256, (i + 1) * 256)
            wide_o[:, rows] += mm_nt(normed_t, dproj_s[rows, :])
        draw = draw_ref[0]
        time_o[...] += mm_nt(normed_t, draw)
        dnormed = (mm(wide_ref[...], dproj_s[...]) + mm(time_ref[...], draw)).T
        product = dnormed * tok
        pre_o[...] += jnp.sum((product * scale).reshape(BLOCK // 8, 8, D), axis=0)
        gain = pre_ref[...]
        mean = jnp.mean(product * gain, axis=-1, keepdims=True)
        grad = scale * (gain * dnormed) - tok * (scale * scale * scale * mean)
        slope_o[0] = (cot_ref[0].astype(f32) + grad).astype(bf16)


def whole(shape):
    return pl.BlockSpec(shape, lambda s, c, *_: (0,) * len(shape))


def layer(
    tokens, cotangent, lengths, wide, time, narrow, taps, offset, prenorm, postnorm,
    timestep_bias, decay_log, skip_gain,
):
    count, length = tokens.shape[:2]
    blocks = length // BLOCK
    spans = length // SPAN
    wide_t = wide.T
    time_t = time.T
    narrow_t = narrow.T
    pre = prenorm.astype(f32)[None]
    post = jnp.pad(postnorm.astype(f32)[:, None], ((0, 0), (0, 7)))
    cols = jnp.concatenate([taps, offset[None], jnp.zeros((3, CHANNELS), bf16)], axis=0).astype(f32).T
    bias = timestep_bias[:, None]
    rate = -jnp.exp(decay_log) * LOG2E
    rate = jnp.concatenate([rate, rate])[:, None]
    grid = (count, blocks)
    sds = jax.ShapeDtypeStruct

    def ahead(rows, width=BLOCK):
        return pl.BlockSpec((1, rows, width), lambda s, c, *_: (s, 0, c))

    def back(rows, width=BLOCK):
        return pl.BlockSpec((1, rows, width), lambda s, c, *_: (s, 0, blocks - 1 - c))

    def tall(reverse):
        if reverse:
            return pl.BlockSpec((1, BLOCK, D), lambda s, c, *_: (s, blocks - 1 - c, 0))
        return pl.BlockSpec((1, BLOCK, D), lambda s, c, *_: (s, c, 0))

    def states(reverse):
        if reverse:
            return pl.BlockSpec((1, SUBS, INNER, SPAN), lambda s, c, *_: (s, blocks - 1 - c, 0, 0))
        return pl.BlockSpec((1, SUBS, INNER, SPAN), lambda s, c, *_: (s, c, 0, 0))

    params = pltpu.CompilerParams(
        dimension_semantics=("arbitrary", "arbitrary"), vmem_limit_bytes=VMEM_LIMIT
    )
    state_shape = sds((count, spans, INNER, SPAN), f32)
    gate, fin, filt, act, x, state = pl.pallas_call(
        enter_kernel,
        grid_spec=pltpu.PrefetchScalarGridSpec(
            num_scalar_prefetch=1,
            grid=grid,
            in_specs=[
                tall(False), whole((WIDE, D)), whole((48, D)), whole((1, D)),
                whole((CHANNELS, 8)), whole((48, 1)), whole((48, 1)),
            ],
            out_specs=[
                ahead(INNER), ahead(CHANNELS), ahead(CHANNELS), ahead(CHANNELS), ahead(48), states(False),
            ],
            scratch_shapes=[
                pltpu.VMEM((CHANNELS, BLOCK + SPAN), f32),
                pltpu.VMEM((INNER, SPAN), f32),
            ],
        ),
        out_shape=[
            sds((count, INNER, length), bf16),
            sds((count, CHANNELS, length), bf16),
            sds((count, CHANNELS, length), bf16),
            sds((count, CHANNELS, length), bf16),
            sds((count, 48, length), f32),
            state_shape,
        ],
        compiler_params=params,
        name="enter",
    )(lengths, tokens, wide_t, time_t, pre, cols, bias, rate)

    result, dgate, dval, dio, sums, dstate, rstate, narrow_grad, post_grad, skip_grad = pl.pallas_call(
        middle_kernel,
        grid_spec=pltpu.PrefetchScalarGridSpec(
            num_scalar_prefetch=1,
            grid=grid,
            in_specs=[
                pl.BlockSpec(memory_space=pltpu.SMEM),
                tall(True), tall(True), back(INNER), back(CHANNELS), back(48), states(True),
                whole((INNER, D)), whole((D, INNER)), whole((INNER, 8)), whole((48, 1)),
            ],
            out_specs=[
                tall(True), back(INNER), back(INNER), back(256), back(120), states(True), states(True),
                whole((INNER, D)), whole((INNER, SPAN)), whole((INNER, SPAN)),
            ],
            scratch_shapes=[
                pltpu.VMEM((INNER, SPAN), f32),
                pltpu.VMEM((INNER, SPAN), f32),
                pltpu.VMEM((INNER, BLOCK), f32),
                pltpu.VMEM((INNER, BLOCK), f32),
                pltpu.VMEM((INNER, BLOCK), f32),
                pltpu.VMEM((SUBS, HEADS, SPAN, SPAN), bf16),
                pltpu.VMEM((SUBS, HEADS, 2 * SPAN, SPAN), bf16),
                pltpu.VMEM((SUBS, INNER, SPAN), bf16),
            ],
        ),
        out_shape=[
            sds((count, length, D), bf16),
            sds((count, INNER, length), bf16),
            sds((count, INNER, length), bf16),
            sds((count, 256, length), f32),
            sds((count, 120, length), f32),
            state_shape,
            state_shape,
            sds((INNER, D), f32),
            sds((INNER, SPAN), f32),
            sds((INNER, SPAN), f32),
        ],
        compiler_params=params,
        name="middle",
    )(lengths, skip_gain, tokens, cotangent, gate, act, x, state, narrow, narrow_t, post, rate)

    dfilt, draw, offset_grad, taps_grad, bias_grad, decay_grad = pl.pallas_call(
        leave_kernel,
        grid_spec=pltpu.PrefetchScalarGridSpec(
            num_scalar_prefetch=1,
            grid=grid,
            in_specs=[
                ahead(CHANNELS), ahead(CHANNELS), ahead(CHANNELS), ahead(48), ahead(INNER), ahead(256), ahead(120),
                states(False), states(False), whole((48, 1)),
            ],
            out_specs=[
                ahead(CHANNELS), ahead(48),
                whole((CHANNELS, SPAN)), whole((CONV, CHANNELS, SPAN)),
                whole((48, SPAN)), whole((48, SPAN)),
            ],
            scratch_shapes=[
                pltpu.VMEM((INNER, SPAN), f32),
                pltpu.VMEM((HEADS, SPAN), f32),
                pltpu.VMEM((CHANNELS, BLOCK), f32),
                pltpu.VMEM((CHANNELS, SPAN), f32),
            ],
        ),
        out_shape=[
            sds((count, CHANNELS, length), bf16),
            sds((count, 48, length), bf16),
            sds((CHANNELS, SPAN), f32),
            sds((CONV, CHANNELS, SPAN), f32),
            sds((48, SPAN), f32),
            sds((48, SPAN), f32),
        ],
        compiler_params=params,
        name="leave",
    )(lengths, filt, act, fin, x, dval, dio, sums, dstate, rstate, rate)

    slope, wide_grad, time_grad, pre_grad = pl.pallas_call(
        widen_kernel,
        grid_spec=pltpu.PrefetchScalarGridSpec(
            num_scalar_prefetch=1,
            grid=grid,
            in_specs=[
                tall(False), tall(False), ahead(INNER), ahead(CHANNELS),
                pl.BlockSpec(
                    (1, CHANNELS, SPAN),
                    lambda s, c, *_: (s, 0, jnp.minimum(SUBS * (c + 1), spans - 1)),
                ),
                ahead(48),
                whole((D, WIDE)), whole((D, 48)), whole((1, D)), whole((CHANNELS, 8)),
            ],
            out_specs=[tall(False), whole((D, WIDE)), whole((D, 48)), whole((8, D))],
            scratch_shapes=[pltpu.VMEM((WIDE, BLOCK), bf16)],
        ),
        out_shape=[
            sds((count, length, D), bf16),
            sds((D, WIDE), f32),
            sds((D, 48), f32),
            sds((8, D), f32),
        ],
        compiler_params=params,
        name="widen",
    )(lengths, tokens, cotangent, dgate, dfilt, dfilt, draw, wide, time, pre, cols)

    decay_rows = jnp.sum(decay_grad, axis=1)
    return (
        result,
        slope,
        wide_grad,
        time_grad,
        narrow_grad,
        jnp.sum(taps_grad, axis=2),
        jnp.sum(offset_grad, axis=1),
        jnp.sum(pre_grad, axis=0),
        jnp.sum(post_grad, axis=1),
        jnp.sum(bias_grad, axis=1),
        decay_rows[:HEADS] + decay_rows[HEADS:],
        jnp.sum(skip_grad.reshape(HEADS, HEADDIM * SPAN), axis=1),
    )


def small_sizes(timestep_weight, filter_weight, filter_offset, prenorm_gain, postnorm_gain):
    sizes = [
        timestep_weight.size,
        filter_weight.size,
        filter_offset.size,
        prenorm_gain.size,
        postnorm_gain.size,
    ]
    used = sum(sizes)
    width = (used + 127) // 128 * 128
    return (sizes, used, width)


def pack_own(timestep_weight, filter_weight, filter_offset, prenorm_gain, postnorm_gain, width):
    joined = jnp.concatenate(
        [
            timestep_weight.reshape(-1),
            filter_weight.reshape(-1),
            filter_offset,
            prenorm_gain,
            postnorm_gain,
        ]
    )
    return jnp.pad(joined, (0, width - joined.shape[0]))


def unpack_rows(rows, sizes, conv_taps):
    count = rows.shape[0]
    starts = [0]
    for amount in sizes:
        starts.append(starts[-1] + amount)
    timestep = rows[:, starts[0] : starts[1]].reshape(-1, 2 * HEADS)
    filter_piece = rows[:, starts[1] : starts[2]].reshape(count, conv_taps, -1)
    smoother = jnp.transpose(filter_piece, (1, 0, 2)).reshape(conv_taps, -1)
    shifter = rows[:, starts[2] : starts[3]].reshape(-1)
    prenorm = rows[:, starts[3] : starts[4]].reshape(-1)
    postnorm = rows[:, starts[4] : starts[5]].reshape(-1)
    return (timestep, smoother, shifter, prenorm, postnorm)


def pack_grads(
    timestep_grad, smoother_grad, shifter_grad, prenorm_grad, postnorm_grad, count, width
):
    conv_taps = smoother_grad.shape[0]
    filter_rows = jnp.transpose(smoother_grad.reshape(conv_taps, count, -1), (1, 0, 2)).reshape(
        count, -1
    )
    joined = jnp.concatenate(
        [
            timestep_grad.reshape(count, -1),
            filter_rows,
            shifter_grad.reshape(count, -1),
            prenorm_grad.reshape(count, -1),
            postnorm_grad.reshape(count, -1),
        ],
        axis=1,
    )
    return jnp.pad(joined, ((0, 0), (0, width - joined.shape[1])))


def local(
    tokens,
    cotangent,
    lengths,
    widen_weight,
    timestep_weight,
    narrow_weight,
    filter_weight,
    filter_offset,
    prenorm_gain,
    postnorm_gain,
    timestep_bias,
    decay_log,
    skip_gain,
):
    count = lax.axis_size("shard")
    sizes, used, width = small_sizes(
        timestep_weight, filter_weight, filter_offset, prenorm_gain, postnorm_gain
    )
    own_small = pack_own(
        timestep_weight, filter_weight, filter_offset, prenorm_gain, postnorm_gain, width
    )
    widen = lax.all_gather(widen_weight, "shard", axis=0, tiled=True)
    narrow = lax.all_gather(narrow_weight, "shard", axis=0, tiled=True)
    small = lax.all_gather(own_small, "shard", axis=0, tiled=True)
    timestep, smoother, shifter, prenorm, postnorm = unpack_rows(
        small.reshape(count, width), sizes, CONV
    )
    (
        result, slope, widen_grad, timestep_grad, narrow_grad, smoother_grad, shifter_grad,
        prenorm_grad, postnorm_grad, bias_grad, decay_grad, skip_grad,
    ) = layer(
        tokens, cotangent, lengths, widen, timestep, narrow, smoother, shifter, prenorm, postnorm,
        timestep_bias, decay_log, skip_gain,
    )
    small_grad = pack_grads(
        timestep_grad, smoother_grad, shifter_grad, prenorm_grad, postnorm_grad, count, width
    )
    shares = (
        lax.psum_scatter(widen_grad, "shard", scatter_dimension=0, tiled=True),
        lax.psum_scatter(narrow_grad, "shard", scatter_dimension=0, tiled=True),
        lax.psum_scatter(small_grad, "shard", scatter_dimension=0, tiled=True),
    )
    summed = lax.psum(shares, "rep")
    heads_summed = lax.psum((bias_grad, decay_grad, skip_grad), ("rep", "shard"))
    timestep_out, filter_out, offset_out, prenorm_out, postnorm_out = unpack_rows(
        summed[2], sizes, CONV
    )
    return (
        result, slope, summed[0], timestep_out, summed[1], filter_out, offset_out, prenorm_out,
        postnorm_out, *heads_summed,
    )


def solution(mesh):
    placed = (
        P(("rep", "shard"), None, None),
        P(("rep", "shard"), None, None),
        P(("rep", "shard")),
        P("shard", None),
        P("shard", None),
        P("shard", None),
        P(None, "shard"),
        P("shard"),
        P("shard"),
        P("shard"),
        P(),
        P(),
        P(),
    )
    return jax.shard_map(
        local,
        mesh=mesh,
        in_specs=placed,
        out_specs=(
            P(("rep", "shard"), None, None),
            P(("rep", "shard"), None, None),
            P("shard", None),
            P("shard", None),
            P("shard", None),
            P(None, "shard"),
            P("shard"),
            P("shard"),
            P("shard"),
            P(),
            P(),
            P(),
        ),
        check_vma=False,
    )
```

```python
from functools import partial

import jax
import jax.numpy as jnp
from jax import lax
from jax.experimental import pallas as pl
from jax.experimental.pallas import tpu as pltpu
from jax.sharding import PartitionSpec as P

HEADS = 24
HEADDIM = 64
STATE = 64
CONV = 4
INNER = 1536
CHANNELS = 1792
D = 768
WIDE = INNER + CHANNELS
SPAN = 128
BLOCK = 256
SUBS = BLOCK // SPAN
EPS = 1e-05
LOG2E = 1.4426950408889634
TINY = 1.2e-38
f32 = jnp.float32
bf16 = jnp.bfloat16
precise = lax.Precision.HIGHEST
VMEM_LIMIT = 60 * 1024 * 1024


def mm(a, b, precision=None):
    return lax.dot_general(
        a, b, (((1,), (0,)), ((), ())), precision=precision, preferred_element_type=f32
    )


def mm_nt(a, b):
    return lax.dot_general(a, b, (((1,), (1,)), ((), ())), preferred_element_type=f32)


def mm_tn(a, b):
    return lax.dot_general(a, b, (((0,), (0,)), ((), ())), preferred_element_type=f32)


def sigmoid(v):
    return 0.5 * jnp.tanh(0.5 * v) + 0.5


def iotas(shape):
    return (
        lax.broadcasted_iota(jnp.int32, shape, 0),
        lax.broadcasted_iota(jnp.int32, shape, 1),
    )


def step_sums(x, rate):
    rows, cols = iotas((SPAN, SPAN))
    steps = jnp.maximum(x, 0.0) + jnp.log1p(jnp.exp(-jnp.abs(x)))
    scaled = steps * rate
    fcum = mm(scaled[:HEADS], (rows <= cols).astype(f32), precise)
    rcum = mm(scaled[HEADS:], (rows >= cols).astype(f32), precise)
    return steps, fcum, rcum


def span_tails(steps, fcum, rcum):
    tail_f = jnp.exp2(fcum[:, SPAN - 1 :] - fcum) * steps[:HEADS]
    tail_r = jnp.exp2(rcum[:, :1] - rcum) * steps[HEADS:]
    return tail_f, tail_r


def enter_kernel(
    len_ref,
    tok_ref,
    wide_ref,
    time_ref,
    pre_ref,
    taps_ref,
    bias_ref,
    rate_ref,
    gate_o,
    fin_o,
    filt_o,
    act_o,
    x_o,
    state_o,
    last_s,
    run_s,
    taps_s,
):
    seq = pl.program_id(0)
    block = pl.program_id(1)
    length = len_ref[seq]

    @pl.when((seq == 0) & (block == 0))
    def _():
        for k in range(CONV + 1):
            taps_s[k] = jnp.broadcast_to(taps_ref[:, k : k + 1], (CHANNELS, SPAN))

    @pl.when(block == 0)
    def _():
        last_s[...] = jnp.zeros_like(last_s)
        run_s[...] = jnp.zeros_like(run_s)

    @pl.when(block * BLOCK < length)
    def _():
        tok = tok_ref[0].astype(f32)
        scale = lax.rsqrt(jnp.mean(tok * tok, axis=-1, keepdims=True) + EPS)
        normed = (tok * scale * pre_ref[...]).astype(bf16)
        x_o[0] = mm_nt(time_ref[...], normed) + bias_ref[...]
        place = block * BLOCK + lax.broadcasted_iota(jnp.int32, (1, BLOCK), 1)
        mask = (place < length).astype(f32)

        def project(i):
            fin_o[0, i * 256 : (i + 1) * 256, :] = mm_nt(
                wide_ref[INNER + i * 256 : INNER + (i + 1) * 256, :], normed
            ).astype(bf16)

        def filter_rows(i):
            r = slice(i * 32, (i + 1) * 32)
            now = fin_o[0, r, :]
            w = jnp.concatenate([last_s[r, :], now], axis=1)
            last_s[r, :] = now[:, SPAN:]
            twice = lambda k: jnp.concatenate([taps_s[k, r, :]] * 2, axis=1)
            acc = twice(4) + twice(3) * now.astype(f32)
            for lag in range(1, CONV):
                moved = pltpu.roll(w, lag, 1)[:, SPAN:].astype(f32)
                acc = acc + twice(3 - lag) * moved
            filt_o[0, r, :] = acc.astype(bf16)
            act = acc * sigmoid(acc)
            if i < INNER // 32:
                act = act * mask
            act_o[0, r, :] = act.astype(bf16)

        for i in range(CHANNELS // 256):
            project(i)
            if i:
                for j in range(8):
                    filter_rows((i - 1) * 8 + j)
        for i in range(INNER // 256):
            gate_o[0, i * 256 : (i + 1) * 256, :] = mm_nt(
                wide_ref[i * 256 : (i + 1) * 256, :], normed
            ).astype(bf16)
            if i == 0:
                for j in range(8):
                    filter_rows((CHANNELS // 256 - 1) * 8 + j)

        lane = lax.broadcasted_iota(jnp.int32, (1, SPAN), 1)

        def span(sub, _):
            cols = pl.ds(pl.multiple_of(sub * SPAN, SPAN), SPAN)
            steps, fcum, rcum = step_sums(x_o[0, :, cols], rate_ref[...])
            tail_f, tail_r = span_tails(steps, fcum, rcum)
            decay = jnp.exp2(fcum[:, SPAN - 1 :])
            ins_f = act_o[0, INNER : INNER + 64, cols].astype(f32)
            ins_r = act_o[0, INNER + 128 : INNER + 192, cols].astype(f32)
            for h in range(HEADS):
                rows = slice(h * 64, (h + 1) * 64)
                weighted = jnp.concatenate(
                    [
                        (ins_f * tail_f[h : h + 1]).astype(bf16),
                        (ins_r * tail_r[h : h + 1]).astype(bf16),
                    ],
                    axis=0,
                )
                fresh = mm_nt(act_o[0, rows, cols], weighted)
                run = run_s[rows, :]
                state_o[0, sub, rows, :] = jnp.where(lane < 64, run, fresh)
                run_s[rows, :] = run * decay[h : h + 1] + fresh
            return None

        lax.fori_loop(0, SUBS, span, None)


def middle_kernel(
    len_ref,
    skip_ref,
    tok_ref,
    cot_ref,
    gate_ref,
    act_ref,
    x_ref,
    state_ref,
    narrow_ref,
    turned_ref,
    post_ref,
    rate_ref,
    result_o,
    dgate_o,
    dval_o,
    dio_o,
    sums_o,
    dstate_o,
    rstate_o,
    narrow_o,
    post_o,
    skip_o,
    run_s,
    grun_s,
    ahead_s,
    behind_s,
    gated_s,
    dgn_s,
    spread_s,
    matrix_s,
    held_s,
    slope_s,
    norm_s,
    gain_s,
):
    seq = pl.program_id(0)
    step = pl.program_id(1)
    block = pl.num_programs(1) - 1 - step
    length = len_ref[seq]

    @pl.when((seq == 0) & (step == 0))
    def _():
        narrow_o[...] = jnp.zeros_like(narrow_o)
        post_o[...] = jnp.zeros_like(post_o)
        skip_o[...] = jnp.zeros_like(skip_o)
        gain_s[...] = jnp.broadcast_to(post_ref[:, :1], (INNER, SPAN))

    @pl.when(step == 0)
    def _():
        run_s[...] = jnp.zeros_like(run_s)
        grun_s[...] = jnp.zeros_like(grun_s)

    @pl.when(block * BLOCK >= length)
    def _():
        result_o[...] = tok_ref[...]

    @pl.when(block * BLOCK < length)
    def _():
        rows_i, cols_i = iotas((SPAN, SPAN))
        lower = rows_i < cols_i
        upper = rows_i > cols_i
        lane = lax.broadcasted_iota(jnp.int32, (1, SPAN), 1)
        place = block * BLOCK + lax.broadcasted_iota(jnp.int32, (BLOCK, 1), 0)
        inside = place < length
        slope_s[...] = jnp.where(inside, cot_ref[0].astype(f32), 0.0).astype(bf16)
        for i in range(3):
            rows = slice(i * 512, (i + 1) * 512)
            dgn_s[rows, :] = mm_nt(narrow_ref[rows, :], slope_s[...])
        zero = jnp.zeros((64, SPAN), bf16)

        def span_scores(cols):
            fi = act_ref[0, INNER : INNER + 64, cols]
            fo = act_ref[0, INNER + 64 : INNER + 128, cols]
            ri = act_ref[0, INNER + 128 : INNER + 192, cols]
            ro = act_ref[0, INNER + 192 : INNER + 256, cols]
            return fi, fo, ri, ro

        def fold(value):
            return jnp.sum(value.reshape(8, 8, SPAN), axis=0)

        def forward_span(back, _):
            sub = SUBS - 1 - back
            cols = pl.ds(pl.multiple_of(sub * SPAN, SPAN), SPAN)
            steps, fcum, rcum = step_sums(x_ref[0, :, cols], rate_ref[...])
            least = jnp.log2(jnp.maximum(steps, TINY))
            columns = jnp.concatenate(
                [fcum - least[:HEADS], rcum - least[HEADS:], jnp.zeros((SPAN - 48, SPAN), f32)],
                axis=0,
            ).T
            out_f = jnp.exp2(fcum)
            out_r = jnp.exp2(rcum)
            decay = jnp.exp2(rcum[:, :1])
            fi, fo, ri, ro = span_scores(cols)
            ahead_scores = jnp.where(lower, mm_tn(fi, fo), 0.0)
            behind_scores = jnp.where(upper, mm_tn(ri, ro), 0.0)
            fo = fo.astype(f32)
            ro = ro.astype(f32)
            squares = jnp.zeros((8, SPAN), f32)
            dots = jnp.zeros((8, SPAN), f32)
            for h in range(HEADS):
                rows = slice(h * 64, (h + 1) * 64)
                power = jnp.where(
                    lower,
                    fcum[h : h + 1] - columns[:, h : h + 1],
                    rcum[h : h + 1] - columns[:, HEADS + h : HEADS + h + 1],
                )
                spread = jnp.exp2(power)
                spread_s[sub, h] = spread.astype(bf16)
                low = (spread * ahead_scores).astype(bf16)
                high = (spread * behind_scores).astype(bf16)
                out_low = (fo * out_f[h : h + 1]).astype(bf16)
                out_high = (ro * out_r[h : h + 1]).astype(bf16)
                matrix_s[sub, h, :SPAN] = low
                matrix_s[sub, h, SPAN : 2 * SPAN] = high
                matrix_s[sub, h, 2 * SPAN : 2 * SPAN + 64] = out_low
                matrix_s[sub, h, 2 * SPAN + 64 :] = out_high
                matrix = jnp.concatenate(
                    [
                        jnp.concatenate([low, out_low, zero], axis=0),
                        jnp.concatenate([high, zero, out_high], axis=0),
                    ],
                    axis=1,
                )
                state = state_ref[0, sub, rows, :]
                run = run_s[rows, :]
                rstate_o[0, sub, rows, :] = run
                held = jnp.where(lane < 64, state, run).astype(bf16)
                held_s[sub, rows, :] = held
                run_s[rows, :] = run * decay[h : h + 1] + state
                values = act_ref[0, rows, cols]
                pair = mm(jnp.concatenate([values, held], axis=1), matrix)
                ahead = pair[:, :SPAN]
                behind = pair[:, SPAN:]
                ahead_s[rows, cols] = ahead
                behind_s[rows, cols] = behind
                mixed = ahead + behind + skip_ref[h] * values.astype(f32)
                gate = gate_ref[0, rows, cols].astype(f32)
                gated = mixed * (gate * sigmoid(gate))
                gated_s[rows, cols] = gated
                squares = squares + fold(gated * gated)
                dots = dots + fold(gated * gain_s[rows, :] * dgn_s[rows, cols])
            rs = lax.rsqrt(jnp.sum(squares, axis=0, keepdims=True) * (1.0 / INNER) + EPS)
            pull = rs * rs * rs * (jnp.sum(dots, axis=0, keepdims=True) * (1.0 / INNER))
            norm_s[:1, cols] = rs
            norm_s[1:2, cols] = pull
            return None

        lax.fori_loop(0, SUBS, forward_span, None)
        rs = norm_s[:1, :]

        def norm_rows(i, _):
            r = pl.ds(pl.multiple_of(i * 32, 32), 32)
            kept = gated_s[r, :] * rs
            gain = gain_s[r, :]
            dgate_o[0, r, :] = (kept * jnp.concatenate([gain, gain], axis=1)).astype(bf16)
            product = kept * dgn_s[r, :]
            post_o[r, :] += product[:, :SPAN] + product[:, SPAN:]
            return None

        lax.fori_loop(0, INNER // 32, norm_rows, None, unroll=8)
        gnormed = dgate_o[0]
        branch = mm(turned_ref[...], gnormed)
        result_o[0] = (tok_ref[0].astype(f32) + jnp.where(inside, branch.T, 0.0)).astype(bf16)
        for i in range(3):
            rows = slice(i * 512, (i + 1) * 512)
            narrow_o[rows, :] += mm(gnormed[rows], slope_s[...])

        def backward_span(back, _):
            sub = SUBS - 1 - back
            cols = pl.ds(pl.multiple_of(sub * SPAN, SPAN), SPAN)
            steps, fcum, rcum = step_sums(x_ref[0, :, cols], rate_ref[...])
            out_f = jnp.exp2(fcum)
            out_r = jnp.exp2(rcum)
            decay = jnp.exp2(fcum[:, SPAN - 1 :])
            fi, fo, ri, ro = span_scores(cols)
            rs = norm_s[:1, cols]
            pull = norm_s[1:2, cols]
            dscores = jnp.zeros((SPAN, SPAN), f32)
            dfo = jnp.zeros((64, SPAN), f32)
            dro = jnp.zeros((64, SPAN), f32)

            def down(value):
                return jnp.sum(value, axis=0, keepdims=True)

            for h in range(HEADS):
                rows = slice(h * 64, (h + 1) * 64)
                gate = gate_ref[0, rows, cols].astype(f32)
                sig = sigmoid(gate)
                values = act_ref[0, rows, cols]
                values32 = values.astype(f32)
                ahead = ahead_s[rows, cols]
                behind = behind_s[rows, cols]
                mixed = ahead + behind + skip_ref[h] * values32
                dgated = rs * (gain_s[rows, :] * dgn_s[rows, cols]) - gated_s[rows, cols] * pull
                dmixed = dgated * (gate * sig)
                dgate = dgated * mixed * (sig * (1.0 + gate * (1.0 - sig)))
                dgate_o[0, rows, cols] = dgate.astype(bf16)
                skip_o[h * 8 : h * 8 + 8, :] += fold(dmixed * values32)
                dm = dmixed.astype(bf16)
                dm32 = dm.astype(f32)
                held = held_s[sub, rows, :]
                grad = mm_tn(jnp.concatenate([values, held], axis=1), dm)
                dscores = dscores + grad[:SPAN] * spread_s[sub, h].astype(f32)
                dfo = dfo + grad[SPAN : SPAN + 64] * out_f[h : h + 1]
                dro = dro + grad[SPAN + 64 :] * out_r[h : h + 1]
                dall = mm_nt(dm, matrix_s[sub, h])
                dlow = dall[:, :SPAN]
                dhigh = dall[:, SPAN : 2 * SPAN]
                dheld = dall[:, 2 * SPAN :]
                dval_o[0, rows, cols] = (dlow + dhigh + skip_ref[h] * dmixed).astype(bf16)
                run = grun_s[rows, :]
                dstate_o[0, sub, rows, :] = jnp.where(lane < 64, run, dheld)
                grun_s[rows, :] = run * decay[h : h + 1] + dheld
                sums_o[0, h : h + 1, cols] = down(dm32 * ahead)
                sums_o[0, HEADS + h : HEADS + h + 1, cols] = down(dm32 * behind)
                sums_o[0, 2 * HEADS + h : 2 * HEADS + h + 1, cols] = down(values32 * dlow)
                sums_o[0, 3 * HEADS + h : 3 * HEADS + h + 1, cols] = down(values32 * dhigh)
                sums_o[0, 4 * HEADS + h : 4 * HEADS + h + 1, cols] = decay[h : h + 1] * down(
                    jnp.where(lane < 64, run * held.astype(f32), 0.0)
                )
            low = jnp.where(lower, dscores, 0.0).astype(bf16)
            high = jnp.where(upper, dscores, 0.0).astype(bf16)
            dio_o[0, 0:64, cols] = mm_nt(fo, low)
            dio_o[0, 64:128, cols] = dfo + mm(fi, low)
            dio_o[0, 128:192, cols] = mm_nt(ro, high)
            dio_o[0, 192:256, cols] = dro + mm(ri, high)
            return None

        lax.fori_loop(0, SUBS, backward_span, None)


def leave_kernel(
    len_ref,
    filt_ref,
    act_ref,
    fin_ref,
    x_ref,
    dval_ref,
    dio_ref,
    sums_ref,
    dstate_ref,
    rstate_ref,
    rate_ref,
    dfilt_o,
    draw_o,
    offset_o,
    taps_o,
    bias_o,
    decay_o,
    grun_s,
    near_s,
    dact_s,
    last_s,
):
    seq = pl.program_id(0)
    block = pl.program_id(1)
    length = len_ref[seq]

    @pl.when((seq == 0) & (block == 0))
    def _():
        offset_o[...] = jnp.zeros_like(offset_o)
        taps_o[...] = jnp.zeros_like(taps_o)
        bias_o[...] = jnp.zeros_like(bias_o)
        decay_o[...] = jnp.zeros_like(decay_o)

    @pl.when(block == 0)
    def _():
        grun_s[...] = jnp.zeros_like(grun_s)
        last_s[...] = jnp.zeros_like(last_s)

    @pl.when(block * BLOCK < length)
    def _():
        rows_i, cols_i = iotas((SPAN, SPAN))
        lane = lax.broadcasted_iota(jnp.int32, (1, SPAN), 1)

        def span(sub, _):
            cols = pl.ds(pl.multiple_of(sub * SPAN, SPAN), SPAN)
            x = x_ref[0, :, cols]
            steps, fcum, rcum = step_sums(x, rate_ref[...])
            tail_f, tail_r = span_tails(steps, fcum, rcum)
            decay = jnp.exp2(rcum[:, :1])
            fi = act_ref[0, INNER : INNER + 64, cols].astype(f32)
            ri = act_ref[0, INNER + 128 : INNER + 192, cols].astype(f32)
            dfi = jnp.zeros((64, SPAN), f32)
            dri = jnp.zeros((64, SPAN), f32)
            ends_f = []
            ends_r = []
            for h in range(HEADS):
                rows = slice(h * 64, (h + 1) * 64)
                weighted = jnp.concatenate(
                    [
                        (fi * tail_f[h : h + 1]).astype(bf16),
                        (ri * tail_r[h : h + 1]).astype(bf16),
                    ],
                    axis=0,
                )
                dstate = dstate_ref[0, sub, rows, :]
                run = grun_s[rows, :]
                dfresh = jnp.where(lane < 64, dstate, run).astype(bf16)
                near_s[h : h + 1, :] = decay[h : h + 1] * jnp.sum(
                    jnp.where(lane < 64, 0.0, run * rstate_ref[0, sub, rows, :]),
                    axis=0,
                    keepdims=True,
                )
                grun_s[rows, :] = run * decay[h : h + 1] + dstate
                values = act_ref[0, rows, cols]
                dact_s[rows, cols] = dval_ref[0, rows, cols].astype(f32) + mm(dfresh, weighted)
                dweighted = mm_tn(dfresh, values)
                part_f = dweighted[:64] * tail_f[h : h + 1]
                part_r = dweighted[64:] * tail_r[h : h + 1]
                dfi = dfi + part_f
                dri = dri + part_r
                ends_f.append(jnp.sum(part_f * fi, axis=0, keepdims=True))
                ends_r.append(jnp.sum(part_r * ri, axis=0, keepdims=True))
            dact_s[INNER : INNER + 64, cols] = dio_ref[0, 0:64, cols] + dfi
            dact_s[INNER + 64 : INNER + 128, cols] = dio_ref[0, 64:128, cols]
            dact_s[INNER + 128 : INNER + 192, cols] = dio_ref[0, 128:192, cols] + dri
            dact_s[INNER + 192 : INNER + 256, cols] = dio_ref[0, 192:256, cols]
            ends_f = jnp.concatenate(ends_f, axis=0)
            ends_r = jnp.concatenate(ends_r, axis=0)
            col_f = sums_ref[0, 2 * HEADS : 3 * HEADS, cols]
            col_r = sums_ref[0, 3 * HEADS : 4 * HEADS, cols]
            far_f = jnp.sum(sums_ref[0, 4 * HEADS :, cols], axis=1, keepdims=True)
            far_r = jnp.sum(near_s[...], axis=1, keepdims=True)
            dfa = mm(sums_ref[0, :HEADS, cols] - col_f, (rows_i >= cols_i).astype(f32), precise)
            dra = mm(
                sums_ref[0, HEADS : 2 * HEADS, cols] - col_r,
                (rows_i <= cols_i).astype(f32),
                precise,
            )
            dfa = dfa + far_f + mm(ends_f, (rows_i < cols_i).astype(f32), precise)
            dra = dra + far_r + mm(ends_r, (rows_i > cols_i).astype(f32), precise)
            sig = jax.nn.sigmoid(x)
            rate = rate_ref[...] * (1.0 / LOG2E)
            share = sig / jnp.maximum(steps, TINY)
            span_d = jnp.concatenate([dfa, dra], axis=0)
            draw = jnp.concatenate([col_f + ends_f, col_r + ends_r], axis=0) * share + span_d * (rate * sig)
            draw_o[0, :, cols] = draw.astype(bf16)
            bias_o[...] += draw
            decay_o[...] += span_d * steps * rate
            return None

        lax.fori_loop(0, SUBS, span, None)
        place = block * BLOCK + lax.broadcasted_iota(jnp.int32, (1, BLOCK), 1)
        mask = (place < length).astype(f32)

        def filter_rows(i, masked):
            r = pl.ds(pl.multiple_of(i * 32, 32), 32)
            filt = filt_ref[0, r, :].astype(f32)
            sig = sigmoid(filt)
            dact = dact_s[r, :]
            if masked:
                dact = dact * mask
            dfilt = dact * (sig * (1.0 + filt * (1.0 - sig)))
            dfilt_o[0, r, :] = dfilt.astype(bf16)
            offset_o[r, :] += dfilt[:, :SPAN] + dfilt[:, SPAN:]
            fin = fin_ref[0, r, :]
            w = jnp.concatenate([last_s[r, :], fin], axis=1)
            last_s[r, :] = fin[:, SPAN:]
            product = dfilt * fin.astype(f32)
            taps_o[3, r, :] += product[:, :SPAN] + product[:, SPAN:]
            for lag in range(1, CONV):
                product = dfilt * pltpu.roll(w, lag, 1)[:, SPAN:].astype(f32)
                taps_o[3 - lag, r, :] += product[:, :SPAN] + product[:, SPAN:]
            return None

        lax.fori_loop(0, INNER // 32, lambda i, _: filter_rows(i, True), None, unroll=8)
        lax.fori_loop(INNER // 32, CHANNELS // 32, lambda i, _: filter_rows(i, False), None, unroll=8)


def widen_kernel(
    len_ref,
    tok_ref,
    cot_ref,
    dgate_ref,
    dfilt_ref,
    next_ref,
    draw_ref,
    wide_ref,
    time_ref,
    pre_ref,
    taps_ref,
    slope_o,
    wide_o,
    time_o,
    pre_o,
    dproj_s,
    taps_s,
):
    seq = pl.program_id(0)
    block = pl.program_id(1)
    length = len_ref[seq]

    @pl.when((seq == 0) & (block == 0))
    def _():
        wide_o[...] = jnp.zeros_like(wide_o)
        time_o[...] = jnp.zeros_like(time_o)
        pre_o[...] = jnp.zeros_like(pre_o)
        for k in range(CONV):
            taps_s[k] = jnp.broadcast_to(taps_ref[:, k : k + 1], (CHANNELS, SPAN))

    @pl.when(block * BLOCK >= length)
    def _():
        slope_o[...] = cot_ref[...]

    @pl.when(block * BLOCK < length)
    def _():
        tok = tok_ref[0].astype(f32)
        scale = lax.rsqrt(jnp.mean(tok * tok, axis=-1, keepdims=True) + EPS)
        normed = (tok * scale * pre_ref[...]).astype(bf16)
        normed_t = normed.T
        dproj_s[:INNER, :] = dgate_ref[0]
        beyond = (block + 1) * BLOCK < length

        def filter_rows(i, _):
            r = pl.ds(pl.multiple_of(i * 32, 32), 32)
            following = jnp.where(beyond, next_ref[0, r, :].astype(f32), 0.0).astype(bf16)
            now = dfilt_ref[0, r, :]
            w = jnp.concatenate([now, following], axis=1)
            twice = lambda k: jnp.concatenate([taps_s[k, r, :]] * 2, axis=1)
            acc = twice(3) * now.astype(f32)
            for lag in range(1, CONV):
                moved = pltpu.roll(w, BLOCK + SPAN - lag, 1)[:, :BLOCK].astype(f32)
                acc = acc + twice(3 - lag) * moved
            dproj_s[pl.ds(pl.multiple_of(INNER + i * 32, 32), 32), :] = acc.astype(bf16)
            return None

        lax.fori_loop(0, CHANNELS // 32, filter_rows, None, unroll=8)
        for i in range(WIDE // 256):
            rows = slice(i * 256, (i + 1) * 256)
            wide_o[:, rows] += mm_nt(normed_t, dproj_s[rows, :])
        draw = draw_ref[0]
        time_o[...] += mm_nt(normed_t, draw)
        dnormed = (mm(wide_ref[...], dproj_s[...]) + mm(time_ref[...], draw)).T
        product = dnormed * tok
        pre_o[...] += jnp.sum((product * scale).reshape(BLOCK // 8, 8, D), axis=0)
        gain = pre_ref[...]
        mean = jnp.mean(product * gain, axis=-1, keepdims=True)
        grad = scale * (gain * dnormed) - tok * (scale * scale * scale * mean)
        slope_o[0] = (cot_ref[0].astype(f32) + grad).astype(bf16)


def whole(shape):
    return pl.BlockSpec(shape, lambda s, c, *_: (0,) * len(shape))


def layer(
    tokens, cotangent, lengths, wide, time, narrow, taps, offset, prenorm, postnorm,
    timestep_bias, decay_log, skip_gain,
):
    count, length = tokens.shape[:2]
    blocks = length // BLOCK
    spans = length // SPAN
    wide_t = wide.T
    time_t = time.T
    narrow_t = narrow.T
    pre = prenorm.astype(f32)[None]
    post = jnp.pad(postnorm.astype(f32)[:, None], ((0, 0), (0, 7)))
    cols = jnp.concatenate([taps, offset[None], jnp.zeros((3, CHANNELS), bf16)], axis=0).astype(f32).T
    bias = timestep_bias[:, None]
    rate = -jnp.exp(decay_log) * LOG2E
    rate = jnp.concatenate([rate, rate])[:, None]
    grid = (count, blocks)
    sds = jax.ShapeDtypeStruct

    def ahead(rows, width=BLOCK):
        return pl.BlockSpec((1, rows, width), lambda s, c, *_: (s, 0, c))

    def back(rows, width=BLOCK):
        return pl.BlockSpec((1, rows, width), lambda s, c, *_: (s, 0, blocks - 1 - c))

    def tall(reverse):
        if reverse:
            return pl.BlockSpec((1, BLOCK, D), lambda s, c, *_: (s, blocks - 1 - c, 0))
        return pl.BlockSpec((1, BLOCK, D), lambda s, c, *_: (s, c, 0))

    def states(reverse):
        if reverse:
            return pl.BlockSpec((1, SUBS, INNER, SPAN), lambda s, c, *_: (s, blocks - 1 - c, 0, 0))
        return pl.BlockSpec((1, SUBS, INNER, SPAN), lambda s, c, *_: (s, c, 0, 0))

    params = pltpu.CompilerParams(
        dimension_semantics=("arbitrary", "arbitrary"), vmem_limit_bytes=VMEM_LIMIT
    )
    state_shape = sds((count, spans, INNER, SPAN), f32)
    gate, fin, filt, act, x, state = pl.pallas_call(
        enter_kernel,
        grid_spec=pltpu.PrefetchScalarGridSpec(
            num_scalar_prefetch=1,
            grid=grid,
            in_specs=[
                tall(False), whole((WIDE, D)), whole((48, D)), whole((1, D)),
                whole((CHANNELS, 8)), whole((48, 1)), whole((48, 1)),
            ],
            out_specs=[
                ahead(INNER), ahead(CHANNELS), ahead(CHANNELS), ahead(CHANNELS), ahead(48), states(False),
            ],
            scratch_shapes=[
                pltpu.VMEM((CHANNELS, SPAN), bf16),
                pltpu.VMEM((INNER, SPAN), f32),
                pltpu.VMEM((CONV + 1, CHANNELS, SPAN), f32),
            ],
        ),
        out_shape=[
            sds((count, INNER, length), bf16),
            sds((count, CHANNELS, length), bf16),
            sds((count, CHANNELS, length), bf16),
            sds((count, CHANNELS, length), bf16),
            sds((count, 48, length), f32),
            state_shape,
        ],
        compiler_params=params,
        name="enter",
    )(lengths, tokens, wide_t, time_t, pre, cols, bias, rate)

    result, dgate, dval, dio, sums, dstate, rstate, narrow_grad, post_grad, skip_grad = pl.pallas_call(
        middle_kernel,
        grid_spec=pltpu.PrefetchScalarGridSpec(
            num_scalar_prefetch=1,
            grid=grid,
            in_specs=[
                pl.BlockSpec(memory_space=pltpu.SMEM),
                tall(True), tall(True), back(INNER), back(CHANNELS), back(48), states(True),
                whole((INNER, D)), whole((D, INNER)), whole((INNER, 8)), whole((48, 1)),
            ],
            out_specs=[
                tall(True), back(INNER), back(INNER), back(256), back(120), states(True), states(True),
                whole((INNER, D)), whole((INNER, SPAN)), whole((8 * HEADS, SPAN)),
            ],
            scratch_shapes=[
                pltpu.VMEM((INNER, SPAN), f32),
                pltpu.VMEM((INNER, SPAN), f32),
                pltpu.VMEM((INNER, BLOCK), f32),
                pltpu.VMEM((INNER, BLOCK), f32),
                pltpu.VMEM((INNER, BLOCK), f32),
                pltpu.VMEM((INNER, BLOCK), f32),
                pltpu.VMEM((SUBS, HEADS, SPAN, SPAN), bf16),
                pltpu.VMEM((SUBS, HEADS, 3 * SPAN, SPAN), bf16),
                pltpu.VMEM((SUBS, INNER, SPAN), bf16),
                pltpu.VMEM((BLOCK, D), bf16),
                pltpu.VMEM((8, BLOCK), f32),
                pltpu.VMEM((INNER, SPAN), f32),
            ],
        ),
        out_shape=[
            sds((count, length, D), bf16),
            sds((count, INNER, length), bf16),
            sds((count, INNER, length), bf16),
            sds((count, 256, length), f32),
            sds((count, 120, length), f32),
            state_shape,
            state_shape,
            sds((INNER, D), f32),
            sds((INNER, SPAN), f32),
            sds((8 * HEADS, SPAN), f32),
        ],
        compiler_params=params,
        name="middle",
    )(lengths, skip_gain, tokens, cotangent, gate, act, x, state, narrow, narrow_t, post, rate)

    dfilt, draw, offset_grad, taps_grad, bias_grad, decay_grad = pl.pallas_call(
        leave_kernel,
        grid_spec=pltpu.PrefetchScalarGridSpec(
            num_scalar_prefetch=1,
            grid=grid,
            in_specs=[
                ahead(CHANNELS), ahead(CHANNELS), ahead(CHANNELS), ahead(48), ahead(INNER), ahead(256), ahead(120),
                states(False), states(False), whole((48, 1)),
            ],
            out_specs=[
                ahead(CHANNELS), ahead(48),
                whole((CHANNELS, SPAN)), whole((CONV, CHANNELS, SPAN)),
                whole((48, SPAN)), whole((48, SPAN)),
            ],
            scratch_shapes=[
                pltpu.VMEM((INNER, SPAN), f32),
                pltpu.VMEM((HEADS, SPAN), f32),
                pltpu.VMEM((CHANNELS, BLOCK), f32),
                pltpu.VMEM((CHANNELS, SPAN), bf16),
            ],
        ),
        out_shape=[
            sds((count, CHANNELS, length), bf16),
            sds((count, 48, length), bf16),
            sds((CHANNELS, SPAN), f32),
            sds((CONV, CHANNELS, SPAN), f32),
            sds((48, SPAN), f32),
            sds((48, SPAN), f32),
        ],
        compiler_params=params,
        name="leave",
    )(lengths, filt, act, fin, x, dval, dio, sums, dstate, rstate, rate)

    slope, wide_grad, time_grad, pre_grad = pl.pallas_call(
        widen_kernel,
        grid_spec=pltpu.PrefetchScalarGridSpec(
            num_scalar_prefetch=1,
            grid=grid,
            in_specs=[
                tall(False), tall(False), ahead(INNER), ahead(CHANNELS),
                pl.BlockSpec(
                    (1, CHANNELS, SPAN),
                    lambda s, c, *_: (s, 0, jnp.minimum(SUBS * (c + 1), spans - 1)),
                ),
                ahead(48),
                whole((D, WIDE)), whole((D, 48)), whole((1, D)), whole((CHANNELS, 8)),
            ],
            out_specs=[tall(False), whole((D, WIDE)), whole((D, 48)), whole((8, D))],
            scratch_shapes=[
                pltpu.VMEM((WIDE, BLOCK), bf16),
                pltpu.VMEM((CONV, CHANNELS, SPAN), f32),
            ],
        ),
        out_shape=[
            sds((count, length, D), bf16),
            sds((D, WIDE), f32),
            sds((D, 48), f32),
            sds((8, D), f32),
        ],
        compiler_params=params,
        name="widen",
    )(lengths, tokens, cotangent, dgate, dfilt, dfilt, draw, wide, time, pre, cols)

    decay_rows = jnp.sum(decay_grad, axis=1)
    return (
        result,
        slope,
        wide_grad,
        time_grad,
        narrow_grad,
        jnp.sum(taps_grad, axis=2),
        jnp.sum(offset_grad, axis=1),
        jnp.sum(pre_grad, axis=0),
        jnp.sum(post_grad, axis=1),
        jnp.sum(bias_grad, axis=1),
        decay_rows[:HEADS] + decay_rows[HEADS:],
        jnp.sum(skip_grad.reshape(HEADS, 8 * SPAN), axis=1),
    )


def peer(rep, shard):
    return {"rep": rep, "shard": shard}


def remote(src, dst, send, recv, device):
    return pltpu.make_async_remote_copy(
        src_ref=src, dst_ref=dst, send_sem=send, recv_sem=recv,
        device_id=device, device_id_type=pl.DeviceIdType.MESH,
    )


def greet(devices):
    barrier = pltpu.get_barrier_semaphore()
    for device in devices:
        pl.semaphore_signal(barrier, inc=1, device_id=device, device_id_type=pl.DeviceIdType.MESH)
    pl.semaphore_wait(barrier, len(devices))


def reduce_kernel(
    lines, wide,
    wide_ref, narrow_ref, small_ref, heads_ref, out_ref, heads_out_ref,
    grads_s, near_s, sum_s, p1_s, q1_s, t0_s, t1_s, p2_s, q2_s, r_s, z_s,
    hc_s, hx_s, hy_s, hz_s,
    send_sem, recv_sem, hsend_sem, hrecv_sem,
):
    piece, rows = grads_s.shape[-3:-1]
    shards = 2 * lines
    tiles_wide = wide_ref.shape[1] // 128
    tiles_narrow = narrow_ref.shape[1] // 128
    rep = lax.axis_index("rep")
    shard = lax.axis_index("shard")
    core, x = lax.rem(rep, 2), lax.div(rep, 2)
    y, z = lax.rem(shard, 2), lax.div(shard, 2)
    sibling = peer(rep + 1 - 2 * core, shard)
    partner = peer(rep, shard + 1 - 2 * y)
    across = [peer(lax.rem(x + k, wide) * 2 + core, shard) for k in range(1, wide)]
    along = [peer(rep, lax.rem(z + k, lines) * 2 + y) for k in range(1, lines)]
    greet([sibling, partner, *across, *along])
    started = []
    used = [0]

    def launch(src, dst, device):
        i = used[0]
        used[0] += 1
        copy = remote(src, dst, send_sem.at[i], recv_sem.at[i], device)
        copy.start()
        started.append(copy)
        return copy

    hused = [0]

    def launch_small(src, dst, device):
        i = hused[0]
        hused[0] += 1
        copy = remote(src, dst, hsend_sem.at[i], hrecv_sem.at[i], device)
        copy.start()
        started.append(copy)
        return copy

    def add(dst, *srcs):
        flat = 1
        for extent in dst.shape[:-3]:
            flat *= extent
        shape = dst.shape[:-3]

        def body(i, _):
            where = []
            rest = i
            for extent in reversed(shape):
                where.append(lax.rem(rest, extent))
                rest = lax.div(rest, extent)
            where = tuple(reversed(where))
            for unit in range(dst.shape[-3]):
                place = (*where, unit)
                total = srcs[0][place].astype(f32)
                for src in srcs[1:]:
                    total = total + src[place].astype(f32)
                dst[place] = total.astype(dst.dtype)
            return None

        lax.fori_loop(0, flat, body, None)

    def pack(half, order):
        def body(index, _):
            start = pl.multiple_of(index * rows, 8)
            for position in range(wide):
                for i in range(piece):
                    unit = ((half * wide + position) * 2 + order) * piece + i
                    if unit < tiles_wide:
                        value = wide_ref[pl.ds(start, rows), unit * 128 : unit * 128 + 128]
                    elif unit < tiles_wide + 2 * tiles_narrow:
                        lower, tile = divmod(unit - tiles_wide, tiles_narrow)
                        begin = pl.multiple_of(2 * start + lower * rows, 8)
                        value = narrow_ref[pl.ds(begin, rows), tile * 128 : tile * 128 + 128]
                    elif unit == tiles_wide + 2 * tiles_narrow:
                        value = small_ref[index]
                    else:
                        value = jnp.zeros((rows, 128), f32)
                    where = (half, order, position, lax.rem(index, 2), lax.div(index, 2), i)
                    grads_s[where] = value.astype(bf16)
            return None

        lax.fori_loop(0, shards, body, None)

    def pack_half(mine, order):
        pl.when(core == (0 if mine else 1))(lambda: pack(0, order))
        pl.when(core == (1 if mine else 0))(lambda: pack(1, order))

    hc_s[core] = heads_ref[...]
    head = launch_small(hc_s.at[core], hc_s.at[core], sibling)
    near = []
    for order in range(2):
        pack_half(False, order)
        near.append(launch(grads_s.at[1 - core, order], near_s.at[order], sibling))
    for order in range(2):
        pack_half(True, order)
    near[0].wait_recv()
    add(sum_s.at[0], grads_s.at[core, 0], near_s.at[0])
    p1 = [
        launch(sum_s.at[0, lax.rem(x + k, wide)], p1_s.at[k - 1], across[k - 1])
        for k in range(1, wide)
    ]
    near[1].wait_recv()
    add(sum_s.at[1], grads_s.at[core, 1], near_s.at[1])
    q1 = launch(sum_s.at[1, :, 1 - y], q1_s, partner)
    head.wait_recv()
    hx_s[x] = hc_s[0] + hc_s[1]
    heads = [launch_small(hx_s.at[x], hx_s.at[x], device) for device in across]
    for copy in p1:
        copy.wait_recv()
    add(t0_s, sum_s.at[0, x], *[p1_s.at[k] for k in range(wide - 1)])
    p2 = launch(t0_s.at[1 - y], p2_s, partner)
    q1.wait_recv()
    add(t1_s, sum_s.at[1, :, y], q1_s)
    q2 = [
        launch(t1_s.at[lax.rem(x + k, wide)], q2_s.at[k - 1], across[k - 1])
        for k in range(1, wide)
    ]
    for copy in heads:
        copy.wait_recv()
    total = hx_s[0]
    for k in range(1, wide):
        total = total + hx_s[k]
    hy_s[y] = total
    head = launch_small(hy_s.at[y], hy_s.at[y], partner)
    p2.wait_recv()
    add(r_s.at[0], t0_s.at[y], p2_s)
    z0 = [launch(r_s.at[0, lax.rem(z + k, lines)], z_s.at[0, k - 1], along[k - 1]) for k in range(1, lines)]
    for copy in q2:
        copy.wait_recv()
    add(r_s.at[1], t1_s.at[x], *[q2_s.at[k] for k in range(wide - 1)])
    z1 = [launch(r_s.at[1, lax.rem(z + k, lines)], z_s.at[1, k - 1], along[k - 1]) for k in range(1, lines)]
    head.wait_recv()
    hz_s[z] = hy_s[0] + hy_s[1]
    heads = [launch_small(hz_s.at[z], hz_s.at[z], device) for device in along]
    for order, copies in ((0, z0), (1, z1)):
        for copy in copies:
            copy.wait_recv()
        add(out_ref.at[core, x, order], r_s.at[order, z], *[z_s.at[order, k] for k in range(lines - 1)])
    shares = [launch(out_ref.at[core, x], out_ref.at[core, x], device) for device in across]
    for copy in heads:
        copy.wait_recv()
    total = hz_s[0]
    for k in range(1, lines):
        total = total + hz_s[k]
    heads_out_ref[...] = total
    for copy in shares:
        copy.wait_recv()
    last = launch(out_ref.at[core], out_ref.at[core], sibling)
    last.wait_recv()
    for copy in started:
        copy.wait_send()


def unit_count(wide_columns, narrow_columns, wide):
    used = wide_columns // 128 + 2 * (narrow_columns // 128) + 1
    return -(-used // (4 * wide)) * 4 * wide


def reduce_units(wide_grad, narrow_grad, small_grad, heads, wide, lines):
    rows = small_grad.shape[1]
    unit = unit_count(wide_grad.shape[1], narrow_grad.shape[1], wide) // (4 * wide)
    piece = (unit, rows, 128)
    copies = 2 + (wide - 1) * 3 + 2 + 2 * (lines - 1) + 1
    small = 1 + (wide - 1) + 1 + (lines - 1)
    vmem = pl.BlockSpec(memory_space=pltpu.VMEM)
    return pl.pallas_call(
        partial(reduce_kernel, lines, wide),
        in_specs=[vmem] * 4,
        out_specs=[vmem, vmem],
        out_shape=[
            jax.ShapeDtypeStruct((2, wide, 2, *piece), bf16),
            jax.ShapeDtypeStruct((8, 128), f32),
        ],
        scratch_shapes=[
            pltpu.VMEM((2, 2, wide, 2, lines, *piece), bf16),
            pltpu.VMEM((2, wide, 2, lines, *piece), bf16),
            pltpu.VMEM((2, wide, 2, lines, *piece), bf16),
            pltpu.VMEM((max(wide - 1, 1), 2, lines, *piece), bf16),
            pltpu.VMEM((wide, lines, *piece), bf16),
            pltpu.VMEM((2, lines, *piece), bf16),
            pltpu.VMEM((wide, lines, *piece), bf16),
            pltpu.VMEM((lines, *piece), bf16),
            pltpu.VMEM((max(wide - 1, 1), lines, *piece), bf16),
            pltpu.VMEM((2, lines, *piece), bf16),
            pltpu.VMEM((2, lines - 1, *piece), bf16),
            pltpu.VMEM((2, 8, 128), f32),
            pltpu.VMEM((wide, 8, 128), f32),
            pltpu.VMEM((2, 8, 128), f32),
            pltpu.VMEM((lines, 8, 128), f32),
            pltpu.SemaphoreType.DMA((copies,)),
            pltpu.SemaphoreType.DMA((copies,)),
            pltpu.SemaphoreType.DMA((small,)),
            pltpu.SemaphoreType.DMA((small,)),
        ],
        compiler_params=pltpu.CompilerParams(
            collective_id=1, has_side_effects=True, vmem_limit_bytes=VMEM_LIMIT
        ),
        name="reduce",
    )(wide_grad, narrow_grad, small_grad, heads)


def gather_kernel(lines, cuts, wide_ref, small_ref, wide_o, small_o, send_sem, recv_sem, own_sem):
    rep = lax.axis_index("rep")
    shard = lax.axis_index("shard")
    core = lax.rem(rep, 2)
    y, z = lax.rem(shard, 2), lax.div(shard, 2)
    half = sum(cuts)
    sibling = peer(rep + 1 - 2 * core, shard)
    partner = peer(rep, shard + 1 - 2 * y)
    has_up, has_down = z < lines - 1, z > 0
    up = peer(rep, jnp.minimum(z + 1, lines - 1) * 2 + y)
    down = peer(rep, jnp.maximum(z - 1, 0) * 2 + y)
    barrier = pltpu.get_barrier_semaphore()

    def hello(device):
        pl.semaphore_signal(barrier, inc=1, device_id=device, device_id_type=pl.DeviceIdType.MESH)

    hello(sibling)
    hello(partner)
    pl.when(has_up)(lambda: hello(up))
    pl.when(has_down)(lambda: hello(down))
    pl.semaphore_wait(barrier, 2 + has_up.astype(jnp.int32) + has_down.astype(jnp.int32))

    own = [
        pltpu.make_async_copy(wide_ref, wide_o.at[shard], own_sem.at[0]),
        pltpu.make_async_copy(small_ref, small_o.at[shard], own_sem.at[1]),
    ]
    for copy in own:
        copy.start()

    def place(order, part, ref, index, side):
        if part:
            return ref.at[side] if index is None else ref.at[index, side]
        start = pl.multiple_of(side * half + (cuts[0] if order else 0), 128)
        columns = pl.ds(start, cuts[order])
        return ref.at[:, columns] if index is None else ref.at[index, :, columns]

    def parts(order):
        return (0, 1) if order == 0 else (0,)

    def copies(way, order, index, device, mine=False, side=None):
        side = core if side is None else side
        made = []
        for part in parts(order):
            out = (wide_o, small_o)[part]
            src = (wide_ref, small_ref)[part] if mine else out
            made.append(
                remote(
                    place(order, part, src, None if mine else index, side),
                    place(order, part, out, index, side),
                    send_sem.at[way, order, part, index],
                    recv_sem.at[way, order, part, index],
                    device,
                )
            )
        return made

    def start(*args, **kw):
        for copy in copies(*args, **kw):
            copy.start()

    def arrive(*args, **kw):
        for copy in copies(*args, **kw):
            copy.wait_recv()

    def sent(*args, **kw):
        for copy in copies(*args, **kw):
            copy.wait_send()

    other = shard + 1 - 2 * y

    def index_of(line, side):
        return line * 2 + side

    start(0, 1, shard, partner, mine=True)
    pl.when(has_up)(lambda: start(1, 0, shard, up, mine=True))
    pl.when(has_down)(lambda: start(2, 0, shard, down, mine=True))
    pl.when(has_up)(lambda: start(1, 1, shard, up, mine=True))
    pl.when(has_down)(lambda: start(2, 1, shard, down, mine=True))
    start(0, 0, shard, partner, mine=True)
    arrive(0, 1, other, partner)
    pl.when(has_up)(lambda: start(1, 1, other, up))
    pl.when(has_down)(lambda: start(2, 1, other, down))
    start(3, 1, other, sibling)

    def line_step(k, order, side):
        def from_below():
            index = index_of(z - k, side)
            arrive(1, order, index, down)
            pl.when(has_up)(lambda: start(1, order, index, up))
            start(3, order, index, sibling)
            if order == 0:
                start(0, 0, index, partner)

        def from_above():
            index = index_of(z + k, side)
            arrive(2, order, index, up)
            pl.when(has_down)(lambda: start(2, order, index, down))
            start(3, order, index, sibling)
            if order == 0:
                start(0, 0, index, partner)

        pl.when(z - k >= 0)(from_below)
        pl.when(z + k < lines)(from_above)

    for k in range(1, lines):
        line_step(k, 0, y)
        line_step(k, 1, y)
        line_step(k, 1, 1 - y)
    for k in range(lines):
        def below(k=k):
            index = index_of(z - k, 1 - y)
            arrive(0, 0, index, partner)
            start(3, 0, index, sibling)

        def above(k=k):
            index = index_of(z + k, 1 - y)
            arrive(0, 0, index, partner)
            start(3, 0, index, sibling)

        pl.when(z - k >= 0)(below)
        if k:
            pl.when(z + k < lines)(above)
    for line in range(lines):
        for side in range(2):
            index = line * 2 + side

            @pl.when(index != shard)
            def _(index=index):
                for order in range(2):
                    arrive(3, order, index, sibling, side=1 - core)
                    sent(3, order, index, sibling)

    for line in range(lines):
        index = index_of(line, y)
        sent(0, 0, index, partner)
    sent(0, 1, shard, partner)
    for line in range(lines):
        for order, side in ((0, y), (1, y), (1, 1 - y)):
            index = index_of(line, side)

            @pl.when((line <= z) & has_up)
            def _(order=order, index=index):
                sent(1, order, index, up)

            @pl.when((line >= z) & has_down)
            def _(order=order, index=index):
                sent(2, order, index, down)

    for copy in own:
        copy.wait()


def gather_weights(wide, small, lines, cuts):
    shards = 2 * lines
    hbm = pl.BlockSpec(memory_space=pl.ANY)
    return pl.pallas_call(
        partial(gather_kernel, lines, cuts),
        in_specs=[hbm, hbm],
        out_specs=[hbm, hbm],
        out_shape=[
            jax.ShapeDtypeStruct((shards, *wide.shape), wide.dtype),
            jax.ShapeDtypeStruct((shards, *small.shape), small.dtype),
        ],
        scratch_shapes=[
            pltpu.SemaphoreType.DMA((4, 2, 2, shards)),
            pltpu.SemaphoreType.DMA((4, 2, 2, shards)),
            pltpu.SemaphoreType.DMA((2,)),
        ],
        compiler_params=pltpu.CompilerParams(collective_id=0, has_side_effects=True),
        name="gather",
    )(wide, small)


def pack_rows(pieces, width):
    joined = jnp.concatenate(pieces, axis=1)
    return jnp.pad(joined, ((0, 0), (0, width - joined.shape[1])))


def split_rows(rows, sizes):
    starts = [0]
    for amount in sizes:
        starts.append(starts[-1] + amount)
    return [rows[:, starts[i] : starts[i + 1]] for i in range(len(sizes))]


def local(
    tokens,
    cotangent,
    lengths,
    widen_weight,
    timestep_weight,
    narrow_weight,
    filter_weight,
    filter_offset,
    prenorm_gain,
    postnorm_gain,
    timestep_bias,
    decay_log,
    skip_gain,
):
    count = lax.axis_size("shard")
    lines = count // 2
    wide = lax.axis_size("rep") // 2
    rows = widen_weight.shape[0]
    own = [timestep_weight, filter_weight, filter_offset, prenorm_gain, postnorm_gain]
    sizes = [piece.size for piece in own]
    width = -(-sum(sizes) // 4096) * 4096
    own_small = pack_rows([piece.reshape(1, -1) for piece in own], width)
    half = WIDE // 2
    first = half * 5 // 8 // 128 * 128
    widen, small = gather_weights(
        widen_weight, own_small.reshape(2, -1, 128), lines, (first, half - first)
    )
    widen = widen.reshape(D, WIDE)
    narrow_weight, small = lax.optimization_barrier((narrow_weight, small))
    narrow = lax.all_gather(narrow_weight, "shard", axis=0, tiled=True)
    timestep, smoother, shifter, prenorm, postnorm = split_rows(small.reshape(count, width), sizes)
    (
        result, slope, widen_grad, timestep_grad, narrow_grad, smoother_grad, shifter_grad,
        prenorm_grad, postnorm_grad, bias_grad, decay_grad, skip_grad,
    ) = layer(
        tokens, cotangent, lengths, widen, timestep.reshape(D, 2 * HEADS), narrow,
        jnp.transpose(smoother.reshape(count, CONV, -1), (1, 0, 2)).reshape(CONV, CHANNELS),
        shifter.reshape(-1), prenorm.reshape(-1), postnorm.reshape(-1),
        timestep_bias, decay_log, skip_gain,
    )
    small_grad = pack_rows(
        [
            timestep_grad.reshape(count, -1),
            jnp.transpose(smoother_grad.reshape(CONV, count, -1), (1, 0, 2)).reshape(count, -1),
            shifter_grad.reshape(count, -1),
            prenorm_grad.reshape(count, -1),
            postnorm_grad.reshape(count, -1),
        ],
        rows * 128,
    ).reshape(count, rows, 128)
    heads = pack_rows([bias_grad[None], decay_grad[None], skip_grad[None]], 1024).reshape(8, 128)
    summed, heads_summed = reduce_units(widen_grad, narrow_grad, small_grad, heads, wide, lines)
    summed = summed.reshape(-1, rows, 128)
    tiles = WIDE // 128
    across = D // 128
    widen_out = jnp.transpose(summed[:tiles], (1, 0, 2)).reshape(rows, WIDE)
    narrow_out = jnp.transpose(
        summed[tiles : tiles + 2 * across].reshape(2, across, rows, 128), (0, 2, 1, 3)
    ).reshape(2 * rows, D)
    timestep_out, filter_out, offset_out, prenorm_out, postnorm_out = split_rows(
        summed[tiles + 2 * across].reshape(1, -1).astype(f32), sizes
    )
    heads_row = heads_summed.reshape(-1)
    return (
        result,
        slope,
        widen_out.astype(f32),
        timestep_out.reshape(rows, -1),
        narrow_out.astype(f32),
        filter_out.reshape(CONV, -1),
        offset_out.reshape(-1),
        prenorm_out.reshape(-1),
        postnorm_out.reshape(-1),
        heads_row[: 2 * HEADS],
        heads_row[2 * HEADS : 3 * HEADS],
        heads_row[3 * HEADS : 4 * HEADS],
    )


def solution(mesh):
    placed = (
        P(("rep", "shard"), None, None),
        P(("rep", "shard"), None, None),
        P(("rep", "shard")),
        P("shard", None),
        P("shard", None),
        P("shard", None),
        P(None, "shard"),
        P("shard"),
        P("shard"),
        P("shard"),
        P(),
        P(),
        P(),
    )
    return jax.shard_map(
        local,
        mesh=mesh,
        in_specs=placed,
        out_specs=(
            P(("rep", "shard"), None, None),
            P(("rep", "shard"), None, None),
            P("shard", None),
            P("shard", None),
            P("shard", None),
            P(None, "shard"),
            P("shard"),
            P("shard"),
            P("shard"),
            P(),
            P(),
            P(),
        ),
        check_vma=False,
    )
```

```python
from functools import partial

import jax
import jax.numpy as jnp
from jax import lax
from jax.experimental import pallas as pl
from jax.experimental.pallas import tpu as pltpu
from jax.sharding import PartitionSpec as P

HEADS = 24
HEADDIM = 64
STATE = 64
CONV = 4
INNER = 1536
CHANNELS = 1792
D = 768
WIDE = INNER + CHANNELS
SPAN = 128
BLOCK = 256
SUBS = BLOCK // SPAN
EPS = 1e-05
LOG2E = 1.4426950408889634
TINY = 1.2e-38
f32 = jnp.float32
bf16 = jnp.bfloat16
precise = lax.Precision.HIGHEST
VMEM_LIMIT = 60 * 1024 * 1024


def mm(a, b, precision=None):
    return lax.dot_general(
        a, b, (((1,), (0,)), ((), ())), precision=precision, preferred_element_type=f32
    )


def mm_nt(a, b):
    return lax.dot_general(a, b, (((1,), (1,)), ((), ())), preferred_element_type=f32)


def mm_tn(a, b):
    return lax.dot_general(a, b, (((0,), (0,)), ((), ())), preferred_element_type=f32)


def mm_tn_precise(a, b):
    return lax.dot_general(
        a, b, (((0,), (0,)), ((), ())), precision=precise, preferred_element_type=f32
    )


def sigmoid(v):
    return 0.5 * jnp.tanh(0.5 * v) + 0.5


def iotas(shape):
    return (
        lax.broadcasted_iota(jnp.int32, shape, 0),
        lax.broadcasted_iota(jnp.int32, shape, 1),
    )


def column(row, lanes=SPAN):
    return mm_tn_precise(row, jnp.ones((1, lanes), f32))


def rate_columns(decay_ref):
    half = column(-jnp.exp(decay_ref[...]) * LOG2E)
    return jnp.concatenate([half, half], axis=0)


def spread_taps(taps_s, taps_ref, offset_ref):
    shards, taps, width = taps_ref.shape
    ones = jnp.ones((1, SPAN), bf16)
    for s in range(shards):
        rows = slice(s * width, (s + 1) * width)
        for k in range(taps):
            taps_s[k, rows, :] = mm_tn(taps_ref[s, k : k + 1, :], ones)
        if offset_ref is not None:
            taps_s[taps, rows, :] = mm_tn(offset_ref[s], ones)


def join_row(row_s, ref):
    shards, _, width = ref.shape
    for s in range(shards):
        row_s[:, s * width : (s + 1) * width] = ref[s].astype(f32)


def lane_sums(value):
    return lax.dot_general(
        jnp.ones((8, value.shape[1]), f32), value, (((1,), (1,)), ((), ())),
        precision=precise, preferred_element_type=f32,
    )[:1]


def step_sums(x, rate):
    rows, cols = iotas((SPAN, SPAN))
    steps = jnp.maximum(x, 0.0) + jnp.log1p(jnp.exp(-jnp.abs(x)))
    scaled = steps * rate
    fcum = mm(scaled[:HEADS], (rows <= cols).astype(f32), precise)
    rcum = mm(scaled[HEADS:], (rows >= cols).astype(f32), precise)
    return steps, fcum, rcum


def span_tails(steps, fcum, rcum):
    tail_f = jnp.exp2(fcum[:, SPAN - 1 :] - fcum) * steps[:HEADS]
    tail_r = jnp.exp2(rcum[:, :1] - rcum) * steps[HEADS:]
    return tail_f, tail_r


def enter_kernel(
    len_ref,
    tok_ref,
    wide_ref,
    time_ref,
    pre_ref,
    taps_ref,
    offset_ref,
    bias_ref,
    decay_ref,
    gate_o,
    fin_o,
    filt_o,
    act_o,
    x_o,
    state_o,
    last_s,
    run_s,
    taps_s,
    wide_s,
    time_s,
    pre_s,
    rate_s,
    bias_s,
):
    seq = pl.program_id(0)
    block = pl.program_id(1)
    length = len_ref[seq]

    @pl.when((seq == 0) & (block == 0))
    def _():
        spread_taps(taps_s, taps_ref, offset_ref)
        join_row(pre_s, pre_ref)
        rate_s[...] = rate_columns(decay_ref)
        bias_s[...] = column(bias_ref[...], BLOCK)
        rows_d, cols_d = iotas((D, D))
        time_s[...] = mm_tn(time_ref[...], (rows_d == cols_d).astype(bf16)).astype(bf16)
        for i in range(WIDE // 256):
            wide_s[i * 256 : (i + 1) * 256, :] = wide_ref[:, i * 256 : (i + 1) * 256].T

    @pl.when(block == 0)
    def _():
        last_s[...] = jnp.zeros_like(last_s)
        run_s[...] = jnp.zeros_like(run_s)

    @pl.when(block * BLOCK < length)
    def _():
        tok = tok_ref[0].astype(f32)
        scale = lax.rsqrt(jnp.mean(tok * tok, axis=-1, keepdims=True) + EPS)
        normed = (tok * scale * pre_s[...]).astype(bf16)
        x_o[0] = mm_nt(time_s[...], normed) + bias_s[...]
        place = block * BLOCK + lax.broadcasted_iota(jnp.int32, (1, BLOCK), 1)
        mask = (place < length).astype(f32)

        def project(i):
            fin_o[0, i * 256 : (i + 1) * 256, :] = mm_nt(
                wide_s[INNER + i * 256 : INNER + (i + 1) * 256, :], normed
            ).astype(bf16)

        def filter_rows(i):
            r = slice(i * 32, (i + 1) * 32)
            now = fin_o[0, r, :]
            w = jnp.concatenate([last_s[r, :], now], axis=1)
            last_s[r, :] = now[:, SPAN:]
            twice = lambda k: jnp.concatenate([taps_s[k, r, :]] * 2, axis=1)
            acc = twice(4) + twice(3) * now.astype(f32)
            for lag in range(1, CONV):
                moved = pltpu.roll(w, lag, 1)[:, SPAN:].astype(f32)
                acc = acc + twice(3 - lag) * moved
            filt_o[0, r, :] = acc.astype(bf16)
            act = acc * sigmoid(acc)
            if i < INNER // 32:
                act = act * mask
            act_o[0, r, :] = act.astype(bf16)

        for i in range(CHANNELS // 256):
            project(i)
            if i:
                for j in range(8):
                    filter_rows((i - 1) * 8 + j)
        for i in range(INNER // 256):
            gate_o[0, i * 256 : (i + 1) * 256, :] = mm_nt(
                wide_s[i * 256 : (i + 1) * 256, :], normed
            ).astype(bf16)
            if i == 0:
                for j in range(8):
                    filter_rows((CHANNELS // 256 - 1) * 8 + j)

        lane = lax.broadcasted_iota(jnp.int32, (1, SPAN), 1)

        def span(sub, _):
            cols = pl.ds(pl.multiple_of(sub * SPAN, SPAN), SPAN)
            steps, fcum, rcum = step_sums(x_o[0, :, cols], rate_s[:, :1])
            tail_f, tail_r = span_tails(steps, fcum, rcum)
            decay = jnp.exp2(fcum[:, SPAN - 1 :])
            ins_f = act_o[0, INNER : INNER + 64, cols].astype(f32)
            ins_r = act_o[0, INNER + 128 : INNER + 192, cols].astype(f32)
            for h in range(HEADS):
                rows = slice(h * 64, (h + 1) * 64)
                weighted = jnp.concatenate(
                    [
                        (ins_f * tail_f[h : h + 1]).astype(bf16),
                        (ins_r * tail_r[h : h + 1]).astype(bf16),
                    ],
                    axis=0,
                )
                fresh = mm_nt(act_o[0, rows, cols], weighted)
                run = run_s[rows, :]
                state_o[0, sub, rows, :] = jnp.where(lane < 64, run, fresh).astype(bf16)
                run_s[rows, :] = run * decay[h : h + 1] + fresh
            return None

        lax.fori_loop(0, SUBS, span, None)


def middle_kernel(
    len_ref,
    skip_ref,
    tok_ref,
    cot_ref,
    gate_ref,
    act_ref,
    x_ref,
    state_ref,
    narrow_ref,
    post_ref,
    decay_ref,
    result_o,
    dgate_o,
    dval_o,
    dio_o,
    sums_o,
    dstate_o,
    rstate_o,
    narrow_o,
    post_o,
    skip_o,
    run_s,
    grun_s,
    ahead_s,
    behind_s,
    gated_s,
    dgn_s,
    spread_s,
    matrix_s,
    held_s,
    slope_s,
    norm_s,
    gain_s,
    rate_s,
    narrow_s,
    post_s,
):
    seq = pl.program_id(0)
    step = pl.program_id(1)
    block = pl.num_programs(1) - 1 - step
    length = len_ref[seq]

    @pl.when((seq == 0) & (step == 0))
    def _():
        narrow_s[...] = jnp.zeros_like(narrow_s)
        post_s[...] = jnp.zeros_like(post_s)
        skip_o[...] = jnp.zeros_like(skip_o)
        shards, _, width = post_ref.shape
        for s in range(shards):
            gain_s[s * width : (s + 1) * width, :] = mm_tn(post_ref[s], jnp.ones((1, SPAN), bf16))
        rate_s[...] = rate_columns(decay_ref)

    @pl.when(step == 0)
    def _():
        run_s[...] = jnp.zeros_like(run_s)
        grun_s[...] = jnp.zeros_like(grun_s)

    @pl.when(block * BLOCK >= length)
    def _():
        result_o[...] = tok_ref[...]

    @pl.when(block * BLOCK < length)
    def _():
        rows_i, cols_i = iotas((SPAN, SPAN))
        lower = rows_i < cols_i
        upper = rows_i > cols_i
        lane = lax.broadcasted_iota(jnp.int32, (1, SPAN), 1)
        place = block * BLOCK + lax.broadcasted_iota(jnp.int32, (BLOCK, 1), 0)
        inside = place < length
        slope_s[...] = jnp.where(inside, cot_ref[0].astype(f32), 0.0).astype(bf16)
        for i in range(3):
            rows = slice(i * 512, (i + 1) * 512)
            dgn_s[rows, :] = mm_nt(narrow_ref[rows, :], slope_s[...])
        zero = jnp.zeros((64, SPAN), bf16)

        def span_scores(cols):
            fi = act_ref[0, INNER : INNER + 64, cols]
            fo = act_ref[0, INNER + 64 : INNER + 128, cols]
            ri = act_ref[0, INNER + 128 : INNER + 192, cols]
            ro = act_ref[0, INNER + 192 : INNER + 256, cols]
            return fi, fo, ri, ro

        def fold(value):
            return jnp.sum(value.reshape(8, 8, SPAN), axis=0)

        def forward_span(back, _):
            sub = SUBS - 1 - back
            cols = pl.ds(pl.multiple_of(sub * SPAN, SPAN), SPAN)
            steps, fcum, rcum = step_sums(x_ref[0, :, cols], rate_s[:, :1])
            least = jnp.log2(jnp.maximum(steps, TINY))
            columns = jnp.concatenate(
                [fcum - least[:HEADS], rcum - least[HEADS:], jnp.zeros((SPAN - 48, SPAN), f32)],
                axis=0,
            ).T
            out_f = jnp.exp2(fcum)
            out_r = jnp.exp2(rcum)
            decay = jnp.exp2(rcum[:, :1])
            fi, fo, ri, ro = span_scores(cols)
            ahead_scores = jnp.where(lower, mm_tn(fi, fo), 0.0)
            behind_scores = jnp.where(upper, mm_tn(ri, ro), 0.0)
            fo = fo.astype(f32)
            ro = ro.astype(f32)
            squares = jnp.zeros((8, SPAN), f32)
            dots = jnp.zeros((8, SPAN), f32)
            for h in range(HEADS):
                rows = slice(h * 64, (h + 1) * 64)
                power = jnp.where(
                    lower,
                    fcum[h : h + 1] - columns[:, h : h + 1],
                    rcum[h : h + 1] - columns[:, HEADS + h : HEADS + h + 1],
                )
                spread = jnp.exp2(power)
                spread_s[sub, h] = spread.astype(bf16)
                low = (spread * ahead_scores).astype(bf16)
                high = (spread * behind_scores).astype(bf16)
                out_low = (fo * out_f[h : h + 1]).astype(bf16)
                out_high = (ro * out_r[h : h + 1]).astype(bf16)
                matrix_s[sub, h, :SPAN] = low
                matrix_s[sub, h, SPAN : 2 * SPAN] = high
                matrix_s[sub, h, 2 * SPAN : 2 * SPAN + 64] = out_low
                matrix_s[sub, h, 2 * SPAN + 64 :] = out_high
                matrix = jnp.concatenate(
                    [
                        jnp.concatenate([low, out_low, zero], axis=0),
                        jnp.concatenate([high, zero, out_high], axis=0),
                    ],
                    axis=1,
                )
                state = state_ref[0, sub, rows, :].astype(f32)
                run = run_s[rows, :]
                rstate_o[0, sub, rows, :] = run.astype(bf16)
                held = jnp.where(lane < 64, state, run).astype(bf16)
                held_s[sub, rows, :] = held
                run_s[rows, :] = run * decay[h : h + 1] + state
                values = act_ref[0, rows, cols]
                pair = mm(jnp.concatenate([values, held], axis=1), matrix)
                ahead = pair[:, :SPAN]
                behind = pair[:, SPAN:]
                ahead_s[rows, cols] = ahead
                behind_s[rows, cols] = behind
                mixed = ahead + behind + skip_ref[h] * values.astype(f32)
                gate = gate_ref[0, rows, cols].astype(f32)
                gated = mixed * (gate * sigmoid(gate))
                gated_s[rows, cols] = gated
                squares = squares + fold(gated * gated)
                dots = dots + fold(gated * gain_s[rows, :] * dgn_s[rows, cols])
            rs = lax.rsqrt(jnp.sum(squares, axis=0, keepdims=True) * (1.0 / INNER) + EPS)
            pull = rs * rs * rs * (jnp.sum(dots, axis=0, keepdims=True) * (1.0 / INNER))
            norm_s[:1, cols] = rs
            norm_s[1:2, cols] = pull
            return None

        lax.fori_loop(0, SUBS, forward_span, None)
        rs = norm_s[:1, :]

        def norm_rows(i, _):
            r = pl.ds(pl.multiple_of(i * 32, 32), 32)
            kept = gated_s[r, :] * rs
            gain = gain_s[r, :]
            dgate_o[0, r, :] = (kept * jnp.concatenate([gain, gain], axis=1)).astype(bf16)
            product = kept * dgn_s[r, :]
            post_s[r, :] += product[:, :SPAN] + product[:, SPAN:]
            return None

        lax.fori_loop(0, INNER // 32, norm_rows, None, unroll=8)
        gnormed = dgate_o[0]
        branch = mm_tn(gnormed, narrow_ref[...])
        result_o[0] = (tok_ref[0].astype(f32) + jnp.where(inside, branch, 0.0)).astype(bf16)
        for i in range(3):
            rows = slice(i * 512, (i + 1) * 512)
            narrow_s[rows, :] += mm(gnormed[rows], slope_s[...])

        def backward_span(back, _):
            sub = SUBS - 1 - back
            cols = pl.ds(pl.multiple_of(sub * SPAN, SPAN), SPAN)
            steps, fcum, rcum = step_sums(x_ref[0, :, cols], rate_s[:, :1])
            out_f = jnp.exp2(fcum)
            out_r = jnp.exp2(rcum)
            decay = jnp.exp2(fcum[:, SPAN - 1 :])
            fi, fo, ri, ro = span_scores(cols)
            rs = norm_s[:1, cols]
            pull = norm_s[1:2, cols]
            dscores = jnp.zeros((SPAN, SPAN), f32)
            dfo = jnp.zeros((64, SPAN), f32)
            dro = jnp.zeros((64, SPAN), f32)

            def down(value):
                return jnp.sum(value, axis=0, keepdims=True)

            for h in range(HEADS):
                rows = slice(h * 64, (h + 1) * 64)
                gate = gate_ref[0, rows, cols].astype(f32)
                sig = sigmoid(gate)
                values = act_ref[0, rows, cols]
                values32 = values.astype(f32)
                ahead = ahead_s[rows, cols]
                behind = behind_s[rows, cols]
                mixed = ahead + behind + skip_ref[h] * values32
                dgated = rs * (gain_s[rows, :] * dgn_s[rows, cols]) - gated_s[rows, cols] * pull
                dmixed = dgated * (gate * sig)
                dgate = dgated * mixed * (sig * (1.0 + gate * (1.0 - sig)))
                dgate_o[0, rows, cols] = dgate.astype(bf16)
                skip_o[h : h + 1, :] += down(dmixed * values32)
                dm = dmixed.astype(bf16)
                dm32 = dm.astype(f32)
                held = held_s[sub, rows, :]
                grad = mm_tn(jnp.concatenate([values, held], axis=1), dm)
                dscores = dscores + grad[:SPAN] * spread_s[sub, h].astype(f32)
                dfo = dfo + grad[SPAN : SPAN + 64] * out_f[h : h + 1]
                dro = dro + grad[SPAN + 64 :] * out_r[h : h + 1]
                dall = mm_nt(dm, matrix_s[sub, h])
                dlow = dall[:, :SPAN]
                dhigh = dall[:, SPAN : 2 * SPAN]
                dheld = dall[:, 2 * SPAN :]
                dval_o[0, rows, cols] = (dlow + dhigh + skip_ref[h] * dmixed).astype(bf16)
                run = grun_s[rows, :]
                dstate_o[0, sub, rows, :] = jnp.where(lane < 64, run, dheld).astype(bf16)
                grun_s[rows, :] = run * decay[h : h + 1] + dheld
                sums_o[0, h : h + 1, cols] = down(dm32 * ahead)
                sums_o[0, HEADS + h : HEADS + h + 1, cols] = down(dm32 * behind)
                sums_o[0, 2 * HEADS + h : 2 * HEADS + h + 1, cols] = down(values32 * dlow)
                sums_o[0, 3 * HEADS + h : 3 * HEADS + h + 1, cols] = down(values32 * dhigh)
                sums_o[0, 4 * HEADS + h : 4 * HEADS + h + 1, cols] = decay[h : h + 1] * down(
                    jnp.where(lane < 64, run * held.astype(f32), 0.0)
                )
            low = jnp.where(lower, dscores, 0.0).astype(bf16)
            high = jnp.where(upper, dscores, 0.0).astype(bf16)
            dio_o[0, 0:64, cols] = mm_nt(fo, low)
            dio_o[0, 64:128, cols] = dfo + mm(fi, low)
            dio_o[0, 128:192, cols] = mm_nt(ro, high)
            dio_o[0, 192:256, cols] = dro + mm(ri, high)
            return None

        lax.fori_loop(0, SUBS, backward_span, None)

    @pl.when((seq == pl.num_programs(0) - 1) & (step == pl.num_programs(1) - 1))
    def _():
        post_o[...] = lane_sums(post_s[...])
        halves, shards, rows = narrow_o.shape[0] * SPAN // D, *narrow_o.shape[1:3]
        for unit in range(narrow_o.shape[0]):
            half, tile = divmod(unit, D // SPAN)
            for s in range(shards):
                start = (s * halves + half) * rows
                narrow_o[unit, s] = narrow_s[
                    start : start + rows, tile * SPAN : (tile + 1) * SPAN
                ].astype(bf16)


def leave_kernel(
    len_ref,
    filt_ref,
    act_ref,
    fin_ref,
    x_ref,
    dval_ref,
    dio_ref,
    sums_ref,
    dstate_ref,
    rstate_ref,
    decay_ref,
    skip_ref,
    dfilt_o,
    draw_o,
    lines_o,
    heads_o,
    grun_s,
    near_s,
    dact_s,
    last_s,
    offset_s,
    taps_s,
    bias_s,
    decay_s,
    rate_s,
):
    seq = pl.program_id(0)
    block = pl.program_id(1)
    length = len_ref[seq]

    @pl.when((seq == 0) & (block == 0))
    def _():
        offset_s[...] = jnp.zeros_like(offset_s)
        taps_s[...] = jnp.zeros_like(taps_s)
        bias_s[...] = jnp.zeros_like(bias_s)
        decay_s[...] = jnp.zeros_like(decay_s)
        rate_s[...] = rate_columns(decay_ref)

    @pl.when(block == 0)
    def _():
        grun_s[...] = jnp.zeros_like(grun_s)
        last_s[...] = jnp.zeros_like(last_s)

    @pl.when(block * BLOCK < length)
    def _():
        rows_i, cols_i = iotas((SPAN, SPAN))
        lane = lax.broadcasted_iota(jnp.int32, (1, SPAN), 1)

        def span(sub, _):
            cols = pl.ds(pl.multiple_of(sub * SPAN, SPAN), SPAN)
            x = x_ref[0, :, cols]
            steps, fcum, rcum = step_sums(x, rate_s[:, :1])
            tail_f, tail_r = span_tails(steps, fcum, rcum)
            decay = jnp.exp2(rcum[:, :1])
            fi = act_ref[0, INNER : INNER + 64, cols].astype(f32)
            ri = act_ref[0, INNER + 128 : INNER + 192, cols].astype(f32)
            dfi = jnp.zeros((64, SPAN), f32)
            dri = jnp.zeros((64, SPAN), f32)
            ends_f = []
            ends_r = []
            for h in range(HEADS):
                rows = slice(h * 64, (h + 1) * 64)
                weighted = jnp.concatenate(
                    [
                        (fi * tail_f[h : h + 1]).astype(bf16),
                        (ri * tail_r[h : h + 1]).astype(bf16),
                    ],
                    axis=0,
                )
                dstate = dstate_ref[0, sub, rows, :].astype(f32)
                run = grun_s[rows, :]
                dfresh = jnp.where(lane < 64, dstate, run).astype(bf16)
                near_s[h : h + 1, :] = decay[h : h + 1] * jnp.sum(
                    jnp.where(lane < 64, 0.0, run * rstate_ref[0, sub, rows, :].astype(f32)),
                    axis=0,
                    keepdims=True,
                )
                grun_s[rows, :] = run * decay[h : h + 1] + dstate
                values = act_ref[0, rows, cols]
                dact_s[rows, cols] = dval_ref[0, rows, cols].astype(f32) + mm(dfresh, weighted)
                dweighted = mm_tn(dfresh, values)
                part_f = dweighted[:64] * tail_f[h : h + 1]
                part_r = dweighted[64:] * tail_r[h : h + 1]
                dfi = dfi + part_f
                dri = dri + part_r
                ends_f.append(jnp.sum(part_f * fi, axis=0, keepdims=True))
                ends_r.append(jnp.sum(part_r * ri, axis=0, keepdims=True))
            dact_s[INNER : INNER + 64, cols] = dio_ref[0, 0:64, cols] + dfi
            dact_s[INNER + 64 : INNER + 128, cols] = dio_ref[0, 64:128, cols]
            dact_s[INNER + 128 : INNER + 192, cols] = dio_ref[0, 128:192, cols] + dri
            dact_s[INNER + 192 : INNER + 256, cols] = dio_ref[0, 192:256, cols]
            ends_f = jnp.concatenate(ends_f, axis=0)
            ends_r = jnp.concatenate(ends_r, axis=0)
            col_f = sums_ref[0, 2 * HEADS : 3 * HEADS, cols]
            col_r = sums_ref[0, 3 * HEADS : 4 * HEADS, cols]
            far_f = jnp.sum(sums_ref[0, 4 * HEADS :, cols], axis=1, keepdims=True)
            far_r = jnp.sum(near_s[...], axis=1, keepdims=True)
            dfa = mm(sums_ref[0, :HEADS, cols] - col_f, (rows_i >= cols_i).astype(f32), precise)
            dra = mm(
                sums_ref[0, HEADS : 2 * HEADS, cols] - col_r,
                (rows_i <= cols_i).astype(f32),
                precise,
            )
            dfa = dfa + far_f + mm(ends_f, (rows_i < cols_i).astype(f32), precise)
            dra = dra + far_r + mm(ends_r, (rows_i > cols_i).astype(f32), precise)
            sig = jax.nn.sigmoid(x)
            rate = rate_s[:, :1] * (1.0 / LOG2E)
            share = sig / jnp.maximum(steps, TINY)
            span_d = jnp.concatenate([dfa, dra], axis=0)
            draw = jnp.concatenate([col_f + ends_f, col_r + ends_r], axis=0) * share + span_d * (rate * sig)
            draw_o[0, :, cols] = draw.astype(bf16)
            bias_s[...] += draw
            decay_s[...] += span_d * steps * rate
            return None

        lax.fori_loop(0, SUBS, span, None)
        place = block * BLOCK + lax.broadcasted_iota(jnp.int32, (1, BLOCK), 1)
        mask = (place < length).astype(f32)

        def filter_rows(i, masked):
            r = pl.ds(pl.multiple_of(i * 32, 32), 32)
            filt = filt_ref[0, r, :].astype(f32)
            sig = sigmoid(filt)
            dact = dact_s[r, :]
            if masked:
                dact = dact * mask
            dfilt = dact * (sig * (1.0 + filt * (1.0 - sig)))
            dfilt_o[0, r, :] = dfilt.astype(bf16)
            offset_s[r, :] += dfilt[:, :SPAN] + dfilt[:, SPAN:]
            fin = fin_ref[0, r, :]
            w = jnp.concatenate([last_s[r, :], fin], axis=1)
            last_s[r, :] = fin[:, SPAN:]
            product = dfilt * fin.astype(f32)
            taps_s[3, r, :] += product[:, :SPAN] + product[:, SPAN:]
            for lag in range(1, CONV):
                product = dfilt * pltpu.roll(w, lag, 1)[:, SPAN:].astype(f32)
                taps_s[3 - lag, r, :] += product[:, :SPAN] + product[:, SPAN:]
            return None

        lax.fori_loop(0, INNER // 32, lambda i, _: filter_rows(i, True), None, unroll=8)
        lax.fori_loop(INNER // 32, CHANNELS // 32, lambda i, _: filter_rows(i, False), None, unroll=8)

    @pl.when((seq == pl.num_programs(0) - 1) & (block == pl.num_programs(1) - 1))
    def _():
        lines_o[...] = jnp.zeros_like(lines_o)
        heads_o[...] = jnp.zeros_like(heads_o)
        for k in range(CONV):
            lines_o[k : k + 1, :] = lane_sums(taps_s[k])
        lines_o[CONV : CONV + 1, :] = lane_sums(offset_s[...])
        heads_o[:1, : 2 * HEADS] = lane_sums(bias_s[...])
        heads_o[1:2, :HEADS] = lane_sums(decay_s[:HEADS] + decay_s[HEADS:])
        heads_o[2:3, :HEADS] = lane_sums(skip_ref[...])


def widen_kernel(
    len_ref,
    tok_ref,
    cot_ref,
    dgate_ref,
    dfilt_ref,
    next_ref,
    draw_ref,
    wide_ref,
    time_ref,
    pre_ref,
    taps_ref,
    lines_ref,
    post_ref,
    slope_o,
    wide_o,
    small_o,
    dproj_s,
    taps_s,
    wide_s,
    time_s,
    total_s,
    pre_s,
    lines_s,
):
    seq = pl.program_id(0)
    block = pl.program_id(1)
    length = len_ref[seq]

    @pl.when((seq == 0) & (block == 0))
    def _():
        wide_s[...] = jnp.zeros_like(wide_s)
        time_s[...] = jnp.zeros_like(time_s)
        total_s[...] = jnp.zeros_like(total_s)
        spread_taps(taps_s, taps_ref, None)
        join_row(pre_s, pre_ref)

    @pl.when(block * BLOCK >= length)
    def _():
        slope_o[...] = cot_ref[...]

    @pl.when(block * BLOCK < length)
    def _():
        tok = tok_ref[0].astype(f32)
        scale = lax.rsqrt(jnp.mean(tok * tok, axis=-1, keepdims=True) + EPS)
        normed = (tok * scale * pre_s[...]).astype(bf16)
        normed_t = normed.T
        dproj_s[:INNER, :] = dgate_ref[0]
        beyond = (block + 1) * BLOCK < length

        def filter_rows(i, _):
            r = pl.ds(pl.multiple_of(i * 32, 32), 32)
            following = jnp.where(beyond, next_ref[0, r, :].astype(f32), 0.0).astype(bf16)
            now = dfilt_ref[0, r, :]
            w = jnp.concatenate([now, following], axis=1)
            twice = lambda k: jnp.concatenate([taps_s[k, r, :]] * 2, axis=1)
            acc = twice(3) * now.astype(f32)
            for lag in range(1, CONV):
                moved = pltpu.roll(w, BLOCK + SPAN - lag, 1)[:, :BLOCK].astype(f32)
                acc = acc + twice(3 - lag) * moved
            dproj_s[pl.ds(pl.multiple_of(INNER + i * 32, 32), 32), :] = acc.astype(bf16)
            return None

        lax.fori_loop(0, CHANNELS // 32, filter_rows, None, unroll=8)
        for i in range(WIDE // 256):
            rows = slice(i * 256, (i + 1) * 256)
            wide_s[:, rows] += mm_nt(normed_t, dproj_s[rows, :])
        draw = draw_ref[0]
        time_s[:, : 2 * HEADS] += mm_nt(normed_t, draw)
        dnormed = (mm(wide_ref[...], dproj_s[...]) + mm(time_ref[...], draw)).T
        product = dnormed * tok
        total_s[...] += jnp.sum((product * scale).reshape(BLOCK // 8, 8, D), axis=0)
        gain = pre_s[...]
        mean = jnp.mean(product * gain, axis=-1, keepdims=True)
        grad = scale * (gain * dnormed) - tok * (scale * scale * scale * mean)
        slope_o[0] = (cot_ref[0].astype(f32) + grad).astype(bf16)

    @pl.when((seq == pl.num_programs(0) - 1) & (block == pl.num_programs(1) - 1))
    def _():
        tiles, shards, rows = wide_o.shape[:3]
        for s in range(shards):
            own = slice(s * rows, (s + 1) * rows)
            for unit in range(tiles):
                wide_o[unit, s] = wide_s[own, unit * SPAN : (unit + 1) * SPAN].astype(bf16)
            small_o[0, s] = time_s[own, :].astype(bf16)
        pre_sum = jnp.sum(total_s[...], axis=0, keepdims=True)
        vectors = [(lines_ref[k : k + 1, :], CHANNELS // shards) for k in range(CONV + 1)]
        vectors += [(pre_sum, rows), (post_ref[...], INNER // shards)]
        lines_s[...] = jnp.zeros_like(lines_s)
        for s in range(shards):
            line = 0
            for vector, width in vectors:
                for start in range(0, width, SPAN):
                    size = min(SPAN, width - start)
                    begin = s * width + start
                    lines_s[line : line + 1, :size] = vector[:, begin : begin + size]
                    line += 1
            small_o[1, s] = lines_s[...].astype(bf16)


def whole(shape):
    return pl.BlockSpec(
        shape, lambda s, c, *_: (0,) * len(shape), pipeline_mode=pl.Buffered(1)
    )


def layer(
    tokens, cotangent, lengths, wide, time, narrow, taps, offset, prenorm, postnorm,
    timestep_bias, decay_log, skip_gain,
):
    count, length = tokens.shape[:2]
    shards = taps.shape[0]
    rows = D // shards
    blocks = length // BLOCK
    spans = length // SPAN
    bias = timestep_bias[None]
    decay = decay_log[None]
    grid = (count, blocks)
    sds = jax.ShapeDtypeStruct

    def ahead(rows, width=BLOCK):
        return pl.BlockSpec((1, rows, width), lambda s, c, *_: (s, 0, c))

    def back(rows, width=BLOCK):
        return pl.BlockSpec((1, rows, width), lambda s, c, *_: (s, 0, blocks - 1 - c))

    def tall(reverse):
        if reverse:
            return pl.BlockSpec((1, BLOCK, D), lambda s, c, *_: (s, blocks - 1 - c, 0))
        return pl.BlockSpec((1, BLOCK, D), lambda s, c, *_: (s, c, 0))

    def states(reverse):
        if reverse:
            return pl.BlockSpec((1, SUBS, INNER, SPAN), lambda s, c, *_: (s, blocks - 1 - c, 0, 0))
        return pl.BlockSpec((1, SUBS, INNER, SPAN), lambda s, c, *_: (s, c, 0, 0))

    params = pltpu.CompilerParams(
        dimension_semantics=("arbitrary", "arbitrary"), vmem_limit_bytes=VMEM_LIMIT
    )
    state_shape = sds((count, spans, INNER, SPAN), bf16)
    gate, fin, filt, act, x, state = pl.pallas_call(
        enter_kernel,
        grid_spec=pltpu.PrefetchScalarGridSpec(
            num_scalar_prefetch=1,
            grid=grid,
            in_specs=[
                tall(False), whole((D, WIDE)), whole((D, 48)), whole(prenorm.shape),
                whole(taps.shape), whole(offset.shape), whole((1, 48)), whole((1, HEADS)),
            ],
            out_specs=[
                ahead(INNER), ahead(CHANNELS), ahead(CHANNELS), ahead(CHANNELS), ahead(48), states(False),
            ],
            scratch_shapes=[
                pltpu.VMEM((CHANNELS, SPAN), bf16),
                pltpu.VMEM((INNER, SPAN), f32),
                pltpu.VMEM((CONV + 1, CHANNELS, SPAN), f32),
                pltpu.VMEM((WIDE, D), bf16),
                pltpu.VMEM((48, D), bf16),
                pltpu.VMEM((1, D), f32),
                pltpu.VMEM((48, SPAN), f32),
                pltpu.VMEM((48, BLOCK), f32),
            ],
        ),
        out_shape=[
            sds((count, INNER, length), bf16),
            sds((count, CHANNELS, length), bf16),
            sds((count, CHANNELS, length), bf16),
            sds((count, CHANNELS, length), bf16),
            sds((count, 48, length), f32),
            state_shape,
        ],
        compiler_params=params,
        name="enter",
    )(lengths, tokens, wide, time, prenorm, taps, offset, bias, decay)

    across = 2 * D // SPAN
    result, dgate, dval, dio, sums, dstate, rstate, narrow_grad, post_grad, skip_grad = pl.pallas_call(
        middle_kernel,
        grid_spec=pltpu.PrefetchScalarGridSpec(
            num_scalar_prefetch=1,
            grid=grid,
            in_specs=[
                pl.BlockSpec(memory_space=pltpu.SMEM),
                tall(True), tall(True), back(INNER), back(CHANNELS), back(48), states(True),
                whole((INNER, D)), whole(postnorm.shape), whole((1, HEADS)),
            ],
            out_specs=[
                tall(True), back(INNER), back(INNER), back(256), back(120), states(True), states(True),
                whole((across, shards, rows, SPAN)), whole((1, INNER)), whole((HEADS, SPAN)),
            ],
            scratch_shapes=[
                pltpu.VMEM((INNER, SPAN), f32),
                pltpu.VMEM((INNER, SPAN), f32),
                pltpu.VMEM((INNER, BLOCK), f32),
                pltpu.VMEM((INNER, BLOCK), f32),
                pltpu.VMEM((INNER, BLOCK), f32),
                pltpu.VMEM((INNER, BLOCK), f32),
                pltpu.VMEM((SUBS, HEADS, SPAN, SPAN), bf16),
                pltpu.VMEM((SUBS, HEADS, 3 * SPAN, SPAN), bf16),
                pltpu.VMEM((SUBS, INNER, SPAN), bf16),
                pltpu.VMEM((BLOCK, D), bf16),
                pltpu.VMEM((8, BLOCK), f32),
                pltpu.VMEM((INNER, SPAN), f32),
                pltpu.VMEM((48, SPAN), f32),
                pltpu.VMEM((INNER, D), f32),
                pltpu.VMEM((INNER, SPAN), f32),
            ],
        ),
        out_shape=[
            sds((count, length, D), bf16),
            sds((count, INNER, length), bf16),
            sds((count, INNER, length), bf16),
            sds((count, 256, length), f32),
            sds((count, 120, length), f32),
            state_shape,
            state_shape,
            sds((across, shards, rows, SPAN), bf16),
            sds((1, INNER), f32),
            sds((HEADS, SPAN), f32),
        ],
        compiler_params=params,
        name="middle",
    )(lengths, skip_gain, tokens, cotangent, gate, act, x, state, narrow, postnorm, decay)

    dfilt, draw, lines, heads = pl.pallas_call(
        leave_kernel,
        grid_spec=pltpu.PrefetchScalarGridSpec(
            num_scalar_prefetch=1,
            grid=grid,
            in_specs=[
                ahead(CHANNELS), ahead(CHANNELS), ahead(CHANNELS), ahead(48), ahead(INNER), ahead(256), ahead(120),
                states(False), states(False), whole((1, HEADS)), whole((HEADS, SPAN)),
            ],
            out_specs=[
                ahead(CHANNELS), ahead(48), whole((8, CHANNELS)), whole((8, SPAN)),
            ],
            scratch_shapes=[
                pltpu.VMEM((INNER, SPAN), f32),
                pltpu.VMEM((HEADS, SPAN), f32),
                pltpu.VMEM((CHANNELS, BLOCK), f32),
                pltpu.VMEM((CHANNELS, SPAN), bf16),
                pltpu.VMEM((CHANNELS, SPAN), f32),
                pltpu.VMEM((CONV, CHANNELS, SPAN), f32),
                pltpu.VMEM((48, SPAN), f32),
                pltpu.VMEM((48, SPAN), f32),
                pltpu.VMEM((48, SPAN), f32),
            ],
        ),
        out_shape=[
            sds((count, CHANNELS, length), bf16),
            sds((count, 48, length), bf16),
            sds((8, CHANNELS), f32),
            sds((8, SPAN), f32),
        ],
        compiler_params=params,
        name="leave",
    )(lengths, filt, act, fin, x, dval, dio, sums, dstate, rstate, decay, skip_grad)

    slope, wide_grad, small_grad = pl.pallas_call(
        widen_kernel,
        grid_spec=pltpu.PrefetchScalarGridSpec(
            num_scalar_prefetch=1,
            grid=grid,
            in_specs=[
                tall(False), tall(False), ahead(INNER), ahead(CHANNELS),
                pl.BlockSpec(
                    (1, CHANNELS, SPAN),
                    lambda s, c, *_: (s, 0, jnp.minimum(SUBS * (c + 1), spans - 1)),
                ),
                ahead(48),
                whole((D, WIDE)), whole((D, 48)), whole(prenorm.shape), whole(taps.shape),
                whole((8, CHANNELS)), whole((1, INNER)),
            ],
            out_specs=[
                tall(False), whole((WIDE // SPAN, shards, rows, SPAN)), whole((2, shards, rows, SPAN)),
            ],
            scratch_shapes=[
                pltpu.VMEM((WIDE, BLOCK), bf16),
                pltpu.VMEM((CONV, CHANNELS, SPAN), f32),
                pltpu.VMEM((D, WIDE), f32),
                pltpu.VMEM((D, SPAN), f32),
                pltpu.VMEM((8, D), f32),
                pltpu.VMEM((1, D), f32),
                pltpu.VMEM((rows, SPAN), f32),
            ],
        ),
        out_shape=[
            sds((count, length, D), bf16),
            sds((WIDE // SPAN, shards, rows, SPAN), bf16),
            sds((2, shards, rows, SPAN), bf16),
        ],
        compiler_params=params,
        name="widen",
    )(lengths, tokens, cotangent, dgate, dfilt, dfilt, draw, wide, time, prenorm, taps, lines, post_grad)
    return result, slope, wide_grad, narrow_grad, small_grad, heads


def peer(rep, shard):
    return {"rep": rep, "shard": shard}


def remote(src, dst, send, recv, device):
    return pltpu.make_async_remote_copy(
        src_ref=src, dst_ref=dst, send_sem=send, recv_sem=recv,
        device_id=device, device_id_type=pl.DeviceIdType.MESH,
    )


def greet(devices):
    barrier = pltpu.get_barrier_semaphore()
    for device in devices:
        pl.semaphore_signal(barrier, inc=1, device_id=device, device_id_type=pl.DeviceIdType.MESH)
    pl.semaphore_wait(barrier, len(devices))


STRIDE = 2


def reduce_kernel(
    lines, wide,
    wide_ref, narrow_ref, small_ref, heads_ref, out_ref, heads_out_ref,
    own_s, near_s, sum_s, p1_s, q1_s, t0_s, t1_s, p2_s, q2_s, r_s, z_s,
    hc_s, hx_s, hy_s, hz_s,
    send_sem, recv_sem, hsend_sem, hrecv_sem, near_sem, arrive_sem, own_sem,
):
    piece, rows = out_ref.shape[3:5]
    sources = (wide_ref, narrow_ref, small_ref)
    rep = lax.axis_index("rep")
    shard = lax.axis_index("shard")
    core, x = lax.rem(rep, 2), lax.div(rep, 2)
    y, z = lax.rem(shard, 2), lax.div(shard, 2)
    sibling = peer(rep + 1 - 2 * core, shard)
    partner = peer(rep, shard + 1 - 2 * y)
    across = [peer(lax.rem(x + k, wide) * 2 + core, shard) for k in range(1, wide)]
    along = [peer(rep, lax.rem(z + k, lines) * 2 + y) for k in range(1, lines)]
    greet([sibling, partner, *across, *along])
    started = []
    used = [0, 0]

    def launch(src, dst, device, small=False):
        i = used[small]
        used[small] += 1
        pair = (hsend_sem, hrecv_sem) if small else (send_sem, recv_sem)
        copy = remote(src, dst, pair[0].at[i], pair[1].at[i], device)
        copy.start()
        started.append(copy)
        return copy

    def add(where, extents, dst, *srcs):
        flat = 1
        for extent in extents:
            flat *= extent
        for unit in range(*where):

            def body(i, _, unit=unit):
                place = []
                rest = i
                for extent in reversed(extents):
                    place.append(lax.rem(rest, extent))
                    rest = lax.div(rest, extent)
                place = tuple(reversed(place))
                total = None
                for ref, index in srcs:
                    term = ref[index(unit, *place)].astype(f32)
                    total = term if total is None else total + term
                ref, index = dst
                ref[index(unit, *place)] = total.astype(ref.dtype)
                return None

            lax.fori_loop(0, flat, body, None)

    def source(position, order, unit):
        j = (position * 2 + order) * piece + unit
        for ref in sources:
            if j < ref.shape[1]:
                return ref, j
            j -= ref.shape[1]
        return None, None

    def chunk(*where):
        units = pl.ds(where[0], where[1] - where[0])
        near = []
        own = []
        for position in range(wide):
            for order in range(2):
                for unit in range(*where):
                    ref, j = source(position, order, unit)
                    if ref is None:
                        continue
                    place = (position, order, unit)
                    i = (position * 2 + order) * piece + unit
                    copy = remote(
                        ref.at[1 - core, j], near_s.at[place], near_sem.at[i], arrive_sem.at[i], sibling
                    )
                    copy.start()
                    started.append(copy)
                    near.append((order, place, copy))
                    copy = pltpu.make_async_copy(ref.at[core, j], own_s.at[place], own_sem.at[i])
                    copy.start()
                    own.append((order, place, copy))
        yield
        for order in range(2):
            for position in range(wide):
                for unit in range(*where):
                    if source(position, order, unit)[0] is None:
                        sum_s[position, order, unit] = jnp.zeros(sum_s.shape[3:], bf16)
            for mine, theirs in zip(own, near):
                if mine[0] != order:
                    continue
                place = mine[1]
                mine[2].wait()
                theirs[2].wait_recv()
                add(
                    (place[2], place[2] + 1), (lines, 2),
                    (sum_s, lambda u, a, b, p=place: (*p, a, b)),
                    (own_s, lambda u, a, b, p=place: (*p, a, b)),
                    (near_s, lambda u, a, b, p=place: (*p, a, b)),
                )
            if order == 0:
                p1 = [
                    launch(sum_s.at[lax.rem(x + k, wide), 0, units], p1_s.at[k - 1, units], across[k - 1])
                    for k in range(1, wide)
                ]
            else:
                q1 = launch(sum_s.at[:, 1, units, :, 1 - y], q1_s.at[:, units], partner)
        yield
        for copy in p1:
            copy.wait_recv()
        add(
            where, (lines, 2),
            (t0_s, lambda u, a, b: (u, a, b)),
            (sum_s, lambda u, a, b: (x, 0, u, a, b)),
            *[(p1_s, lambda u, a, b, k=k: (k, u, a, b)) for k in range(wide - 1)],
        )
        p2 = launch(t0_s.at[units, :, 1 - y], p2_s.at[units], partner)
        q1.wait_recv()
        add(
            where, (wide, lines),
            (t1_s, lambda u, p, a: (p, u, a)),
            (sum_s, lambda u, p, a: (p, 1, u, a, y)),
            (q1_s, lambda u, p, a: (p, u, a)),
        )
        q2 = [
            launch(t1_s.at[lax.rem(x + k, wide), units], q2_s.at[k - 1, units], across[k - 1])
            for k in range(1, wide)
        ]
        yield
        p2.wait_recv()
        add(
            where, (lines,),
            (r_s, lambda u, a: (0, u, a)), (t0_s, lambda u, a: (u, a, y)), (p2_s, lambda u, a: (u, a)),
        )
        for copy in q2:
            copy.wait_recv()
        add(
            where, (lines,),
            (r_s, lambda u, a: (1, u, a)), (t1_s, lambda u, a: (x, u, a)),
            *[(q2_s, lambda u, a, k=k: (k, u, a)) for k in range(wide - 1)],
        )
        last = [
            launch(r_s.at[:, units, lax.rem(z + k, lines)], z_s.at[k - 1, :, units], along[k - 1])
            for k in range(1, lines)
        ]
        yield
        for copy in last:
            copy.wait_recv()
        add(
            where, (2,),
            (out_ref, lambda u, o: (core, x, o, u)), (r_s, lambda u, o: (o, u, z)),
            *[(z_s, lambda u, o, k=k: (k, o, u)) for k in range(lines - 1)],
        )
        mine = out_ref.at[core, x, :, units]
        shares = [launch(mine, mine, device) for device in across]
        yield
        for copy in shares:
            copy.wait_recv()
        half = out_ref.at[core, :, :, units]
        swap = launch(half, half, sibling)
        yield
        swap.wait_recv()
        yield

    def sum_heads():
        hc_s[core] = heads_ref[...]
        head = launch(hc_s.at[core], hc_s.at[core], sibling, True)
        yield
        head.wait_recv()
        hx_s[x] = hc_s[0] + hc_s[1]
        heads = [launch(hx_s.at[x], hx_s.at[x], device, True) for device in across]
        yield
        for copy in heads:
            copy.wait_recv()
        total = hx_s[0]
        for k in range(1, wide):
            total = total + hx_s[k]
        hy_s[y] = total
        head = launch(hy_s.at[y], hy_s.at[y], partner, True)
        yield
        head.wait_recv()
        hz_s[z] = hy_s[0] + hy_s[1]
        heads = [launch(hz_s.at[z], hz_s.at[z], device, True) for device in along]
        yield
        for copy in heads:
            copy.wait_recv()
        total = hz_s[0]
        for k in range(1, lines):
            total = total + hz_s[k]
        heads_out_ref[...] = total
        yield

    works = [chunk(i, min(i + STRIDE, piece)) for i in range(0, piece, STRIDE)]
    stages = 7
    small_work = sum_heads()
    for slot in range(len(works) + stages - 1):
        for g in range(len(works)):
            if 0 <= slot - g < stages:
                next(works[g])
        if slot < 5:
            next(small_work)
    for copy in started:
        copy.wait_send()


def reduce_units(wide_units, narrow_units, small_units, heads, wide, lines):
    rows = wide_units.shape[2]
    halves = [a.reshape(2, -1, lines, 2, rows, SPAN) for a in (wide_units, narrow_units, small_units)]
    used = sum(a.shape[1] for a in halves)
    unit = -(-used // (2 * wide))
    piece = (rows, SPAN)
    chunks = -(-unit // STRIDE)
    copies = (3 * (wide - 1) + 3 + lines - 1) * chunks
    small = 1 + (wide - 1) + 1 + (lines - 1)
    others = max(wide - 1, 1)
    vmem = pl.BlockSpec(memory_space=pltpu.VMEM)
    hbm = pl.BlockSpec(memory_space=pl.ANY)
    return pl.pallas_call(
        partial(reduce_kernel, lines, wide),
        in_specs=[hbm, hbm, hbm, vmem],
        out_specs=[vmem, vmem],
        out_shape=[
            jax.ShapeDtypeStruct((2, wide, 2, unit, *piece), bf16),
            jax.ShapeDtypeStruct((8, SPAN), f32),
        ],
        scratch_shapes=[
            pltpu.VMEM((wide, 2, unit, lines, 2, *piece), bf16),
            pltpu.VMEM((wide, 2, unit, lines, 2, *piece), bf16),
            pltpu.VMEM((wide, 2, unit, lines, 2, *piece), bf16),
            pltpu.VMEM((others, unit, lines, 2, *piece), bf16),
            pltpu.VMEM((wide, unit, lines, *piece), bf16),
            pltpu.VMEM((unit, lines, 2, *piece), bf16),
            pltpu.VMEM((wide, unit, lines, *piece), bf16),
            pltpu.VMEM((unit, lines, *piece), bf16),
            pltpu.VMEM((others, unit, lines, *piece), bf16),
            pltpu.VMEM((2, unit, lines, *piece), bf16),
            pltpu.VMEM((lines - 1, 2, unit, *piece), bf16),
            pltpu.VMEM((2, 8, SPAN), f32),
            pltpu.VMEM((wide, 8, SPAN), f32),
            pltpu.VMEM((2, 8, SPAN), f32),
            pltpu.VMEM((lines, 8, SPAN), f32),
            pltpu.SemaphoreType.DMA((copies,)),
            pltpu.SemaphoreType.DMA((copies,)),
            pltpu.SemaphoreType.DMA((small,)),
            pltpu.SemaphoreType.DMA((small,)),
            pltpu.SemaphoreType.DMA((2 * wide * unit,)),
            pltpu.SemaphoreType.DMA((2 * wide * unit,)),
            pltpu.SemaphoreType.DMA((2 * wide * unit,)),
        ],
        compiler_params=pltpu.CompilerParams(
            collective_id=1, has_side_effects=True, vmem_limit_bytes=VMEM_LIMIT
        ),
        name="reduce",
    )(*halves, heads)


def finish_kernel(
    wide, summed_ref, heads_ref,
    wide_o, time_o, narrow_o, taps_o, offset_o, pre_o, post_o, bias_o, decay_o, skip_o,
):
    unit, rows = summed_ref.shape[3:5]
    tiles_wide = wide_o.shape[1] // SPAN // 2
    tiles_narrow = narrow_o.shape[1] // SPAN

    def read(core, j):
        block, i = divmod(j, unit)
        return summed_ref[core, block // 2, block % 2, i].astype(f32)

    for core in range(2):
        for j in range(tiles_wide):
            column = (core * tiles_wide + j) * SPAN
            wide_o[:, column : column + SPAN] = read(core, j)
        for j in range(tiles_narrow):
            narrow_o[core * rows : (core + 1) * rows, j * SPAN : (j + 1) * SPAN] = read(
                core, tiles_wide + j
            )
    time_o[...] = read(0, tiles_wide + tiles_narrow)[:, : 2 * HEADS]
    vectors = read(1, tiles_wide + tiles_narrow)
    line = 0
    outs = [(taps_o, k) for k in range(CONV)] + [(offset_o, 0), (pre_o, 0), (post_o, 0)]
    for out, k in outs:
        width = out.shape[1]
        for start in range(0, width, SPAN):
            size = min(SPAN, width - start)
            out[k : k + 1, start : start + size] = vectors[line : line + 1, :size]
            line += 1
    bias_o[...] = heads_ref[:1, : 2 * HEADS]
    decay_o[...] = heads_ref[1:2, :HEADS]
    skip_o[...] = heads_ref[2:3, :HEADS]


def finish(summed, heads, wide, rows, width):
    shapes = [
        (rows, WIDE), (rows, 2 * HEADS), (2 * rows, D), (CONV, width), (1, width), (1, rows), (1, 2 * rows),
        (1, 2 * HEADS), (1, HEADS), (1, HEADS),
    ]
    return pl.pallas_call(
        partial(finish_kernel, wide),
        out_shape=[jax.ShapeDtypeStruct(shape, f32) for shape in shapes],
        compiler_params=pltpu.CompilerParams(vmem_limit_bytes=VMEM_LIMIT),
        name="finish",
    )(summed, heads)


def gather_kernel(lines, cuts, kinds, *refs):
    ins, outs = refs[:kinds], refs[kinds : 2 * kinds]
    send_sem, recv_sem, own_sem = refs[2 * kinds :]
    rep = lax.axis_index("rep")
    shard = lax.axis_index("shard")
    core = lax.rem(rep, 2)
    y, z = lax.rem(shard, 2), lax.div(shard, 2)
    half = sum(cuts)
    sibling = peer(rep + 1 - 2 * core, shard)
    partner = peer(rep, shard + 1 - 2 * y)
    has_up, has_down = z < lines - 1, z > 0
    up = peer(rep, jnp.minimum(z + 1, lines - 1) * 2 + y)
    down = peer(rep, jnp.maximum(z - 1, 0) * 2 + y)
    barrier = pltpu.get_barrier_semaphore()

    def hello(device):
        pl.semaphore_signal(barrier, inc=1, device_id=device, device_id_type=pl.DeviceIdType.MESH)

    hello(sibling)
    hello(partner)
    pl.when(has_up)(lambda: hello(up))
    pl.when(has_down)(lambda: hello(down))
    pl.semaphore_wait(barrier, 2 + has_up.astype(jnp.int32) + has_down.astype(jnp.int32))

    own = [
        pltpu.make_async_copy(src, dst.at[shard], own_sem.at[i])
        for i, (src, dst) in enumerate(zip(ins, outs))
    ]
    for copy in own:
        copy.start()

    def place(order, part, ref, index, side):
        if part:
            return ref if index is None else ref.at[index]
        start = pl.multiple_of(side * half + (cuts[0] if order else 0), 128)
        columns = pl.ds(start, cuts[order])
        return ref.at[:, columns] if index is None else ref.at[index, :, columns]

    def copies(way, order, index, device, mine=False, side=None):
        side = core if side is None else side
        parts = range(kinds) if order == 0 and way != 3 else (0,)
        made = []
        for part in parts:
            made.append(
                remote(
                    place(order, part, ins[part] if mine else outs[part], None if mine else index, side),
                    place(order, part, outs[part], index, side),
                    send_sem.at[way, order, part, index],
                    recv_sem.at[way, order, part, index],
                    device,
                )
            )
        return made

    def start(*args, **kw):
        for copy in copies(*args, **kw):
            copy.start()

    def arrive(*args, **kw):
        for copy in copies(*args, **kw):
            copy.wait_recv()

    def sent(*args, **kw):
        for copy in copies(*args, **kw):
            copy.wait_send()

    other = shard + 1 - 2 * y

    def index_of(line, side):
        return line * 2 + side

    start(0, 1, shard, partner, mine=True)
    pl.when(has_up)(lambda: start(1, 0, shard, up, mine=True))
    pl.when(has_down)(lambda: start(2, 0, shard, down, mine=True))
    pl.when(has_up)(lambda: start(1, 1, shard, up, mine=True))
    pl.when(has_down)(lambda: start(2, 1, shard, down, mine=True))
    start(0, 0, shard, partner, mine=True)
    arrive(0, 1, other, partner)
    pl.when(has_up)(lambda: start(1, 1, other, up))
    pl.when(has_down)(lambda: start(2, 1, other, down))
    start(3, 1, other, sibling)

    def line_step(k, order, side):
        def from_below():
            index = index_of(z - k, side)
            arrive(1, order, index, down)
            pl.when(has_up)(lambda: start(1, order, index, up))
            start(3, order, index, sibling)
            if order == 0:
                start(0, 0, index, partner)

        def from_above():
            index = index_of(z + k, side)
            arrive(2, order, index, up)
            pl.when(has_down)(lambda: start(2, order, index, down))
            start(3, order, index, sibling)
            if order == 0:
                start(0, 0, index, partner)

        pl.when(z - k >= 0)(from_below)
        pl.when(z + k < lines)(from_above)

    for k in range(1, lines):
        line_step(k, 0, y)
        line_step(k, 1, y)
        line_step(k, 1, 1 - y)
    for k in range(lines):

        def take(index):
            arrive(0, 0, index, partner)
            start(3, 0, index, sibling)

        pl.when(z - k >= 0)(lambda k=k: take(index_of(z - k, 1 - y)))
        if k:
            pl.when(z + k < lines)(lambda k=k: take(index_of(z + k, 1 - y)))
    for index in range(2 * lines):

        @pl.when(index != shard)
        def _(index=index):
            for order in range(2):
                arrive(3, order, index, sibling, side=1 - core)
                sent(3, order, index, sibling)

    for line in range(lines):
        sent(0, 0, index_of(line, y), partner)
    sent(0, 1, shard, partner)
    for line in range(lines):
        for order, side in ((0, y), (1, y), (1, 1 - y)):
            index = index_of(line, side)

            @pl.when((line <= z) & has_up)
            def _(order=order, index=index):
                sent(1, order, index, up)

            @pl.when((line >= z) & has_down)
            def _(order=order, index=index):
                sent(2, order, index, down)

    for copy in own:
        copy.wait()


def gather_weights(arrays, lines):
    shards = 2 * lines
    half = arrays[0].shape[1] // 2
    first = half * 5 // 8 // 128 * 128
    hbm = pl.BlockSpec(memory_space=pl.ANY)
    kinds = len(arrays)
    return pl.pallas_call(
        partial(gather_kernel, lines, (first, half - first), kinds),
        in_specs=[hbm] * kinds,
        out_specs=[hbm] * kinds,
        out_shape=[jax.ShapeDtypeStruct((shards, *a.shape), a.dtype) for a in arrays],
        scratch_shapes=[
            pltpu.SemaphoreType.DMA((4, 2, kinds, shards)),
            pltpu.SemaphoreType.DMA((4, 2, kinds, shards)),
            pltpu.SemaphoreType.DMA((kinds,)),
        ],
        compiler_params=pltpu.CompilerParams(collective_id=0, has_side_effects=True),
        name="gather",
    )(*arrays)


def local(
    tokens,
    cotangent,
    lengths,
    widen_weight,
    timestep_weight,
    narrow_weight,
    filter_weight,
    filter_offset,
    prenorm_gain,
    postnorm_gain,
    timestep_bias,
    decay_log,
    skip_gain,
):
    lines = lax.axis_size("shard") // 2
    wide = lax.axis_size("rep") // 2
    rows = widen_weight.shape[0]
    width = filter_weight.shape[1]
    widen, timestep, taps, offset, prenorm, postnorm = gather_weights(
        [
            widen_weight, timestep_weight, filter_weight,
            filter_offset[None], prenorm_gain[None], postnorm_gain[None],
        ],
        lines,
    )
    narrow_weight, taps = lax.optimization_barrier((narrow_weight, taps))
    narrow = lax.all_gather(narrow_weight, "shard", axis=0, tiled=True)
    result, slope, wide_grad, narrow_grad, small_grad, heads = layer(
        tokens, cotangent, lengths, widen.reshape(D, WIDE), timestep.reshape(D, 2 * HEADS), narrow,
        taps, offset, prenorm, postnorm, timestep_bias, decay_log, skip_gain,
    )
    summed, heads = reduce_units(wide_grad, narrow_grad, small_grad, heads, wide, lines)
    (
        widen_out, timestep_out, narrow_out, filter_out, offset_out, prenorm_out, postnorm_out,
        bias_out, decay_out, skip_out,
    ) = finish(summed, heads, wide, rows, width)
    return (
        result, slope, widen_out, timestep_out, narrow_out, filter_out,
        *[row.reshape(-1) for row in (offset_out, prenorm_out, postnorm_out, bias_out, decay_out, skip_out)],
    )


def solution(mesh):
    placed = (
        P(("rep", "shard"), None, None),
        P(("rep", "shard"), None, None),
        P(("rep", "shard")),
        P("shard", None),
        P("shard", None),
        P("shard", None),
        P(None, "shard"),
        P("shard"),
        P("shard"),
        P("shard"),
        P(),
        P(),
        P(),
    )
    return jax.shard_map(
        local,
        mesh=mesh,
        in_specs=placed,
        out_specs=(
            P(("rep", "shard"), None, None),
            P(("rep", "shard"), None, None),
            P("shard", None),
            P("shard", None),
            P("shard", None),
            P(None, "shard"),
            P("shard"),
            P("shard"),
            P("shard"),
            P(),
            P(),
            P(),
        ),
        check_vma=False,
    )
```

```python
from functools import partial

import jax
import jax.numpy as jnp
from jax import lax
from jax.experimental import pallas as pl
from jax.experimental.pallas import tpu as pltpu
from jax.sharding import PartitionSpec as P

HEADS = 24
HEADDIM = 64
STATE = 64
CONV = 4
INNER = 1536
CHANNELS = 1792
D = 768
WIDE = INNER + CHANNELS
SPAN = 128
BLOCK = 256
SUBS = BLOCK // SPAN
EPS = 1e-05
LOG2E = 1.4426950408889634
TINY = 1.2e-38
f32 = jnp.float32
bf16 = jnp.bfloat16
precise = lax.Precision.HIGHEST
VMEM_LIMIT = 60 * 1024 * 1024


def mm(a, b, precision=None):
    return lax.dot_general(
        a, b, (((1,), (0,)), ((), ())), precision=precision, preferred_element_type=f32
    )


def mm_nt(a, b):
    return lax.dot_general(a, b, (((1,), (1,)), ((), ())), preferred_element_type=f32)


def mm_tn(a, b):
    return lax.dot_general(a, b, (((0,), (0,)), ((), ())), preferred_element_type=f32)


def mm_tn_precise(a, b):
    return lax.dot_general(
        a, b, (((0,), (0,)), ((), ())), precision=precise, preferred_element_type=f32
    )


def sigmoid(v):
    return 0.5 * jnp.tanh(0.5 * v) + 0.5


def iotas(shape):
    return (
        lax.broadcasted_iota(jnp.int32, shape, 0),
        lax.broadcasted_iota(jnp.int32, shape, 1),
    )


def column(row, lanes=SPAN):
    return mm_tn_precise(row, jnp.ones((1, lanes), f32))


def rate_columns(decay_ref):
    half = column(-jnp.exp(decay_ref[...]) * LOG2E)
    return jnp.concatenate([half, half], axis=0)


def vector_parts(vectors_ref):
    shards = vectors_ref.shape[0]
    sizes = [CHANNELS // shards] * (CONV + 1) + [D // shards, INNER // shards]
    starts = [sum(sizes[:i]) for i in range(len(sizes))]
    return [slice(start, start + size) for start, size in zip(starts, sizes)]


def spread_vectors(out_s, vectors_ref, which):
    part = vector_parts(vectors_ref)[which]
    width = part.stop - part.start
    for s in range(vectors_ref.shape[0]):
        out_s[s * width : (s + 1) * width, :] = mm_tn(
            vectors_ref[s, :, part], jnp.ones((1, SPAN), bf16)
        )


def join_row(row_s, vectors_ref, which):
    part = vector_parts(vectors_ref)[which]
    width = part.stop - part.start
    for s in range(vectors_ref.shape[0]):
        row_s[:, s * width : (s + 1) * width] = vectors_ref[s, :, part].astype(f32)


def lane_sums(value):
    return lax.dot_general(
        jnp.ones((8, value.shape[1]), f32), value, (((1,), (1,)), ((), ())),
        precision=precise, preferred_element_type=f32,
    )[:1]


def split_rows(value):
    high = value.astype(bf16)
    rest = value - high.astype(f32)
    middle = rest.astype(bf16)
    low = (rest - middle.astype(f32)).astype(bf16)
    return jnp.concatenate([high, middle, low], axis=0)


def exact_mm(value, ones):
    m = value.shape[0]
    parts = mm(split_rows(value), ones)
    return (parts[2 * m :] + parts[m : 2 * m]) + parts[:m]


def span_matrix(compare):
    rows, cols = iotas((BLOCK, BLOCK))
    return (compare(rows, cols) & (rows // SPAN == cols // SPAN)).astype(bf16)


def enter_kernel(
    len_ref,
    tok_ref,
    wide_ref,
    time_ref,
    vectors_ref,
    bias_ref,
    decay_ref,
    gate_o,
    fin_o,
    filt_o,
    act_o,
    rows_o,
    cols_o,
    state_o,
    last_s,
    run_s,
    taps_s,
    wide_s,
    time_s,
    pre_s,
    rate_s,
    bias_s,
    until_s,
    from_s,
):
    seq = pl.program_id(0)
    block = pl.program_id(1)
    length = len_ref[seq]

    @pl.when((seq == 0) & (block == 0))
    def _():
        for k in range(CONV + 1):
            spread_vectors(taps_s.at[k], vectors_ref, k)
        join_row(pre_s, vectors_ref, CONV + 1)
        rate_s[...] = rate_columns(decay_ref)
        until_s[...] = span_matrix(lambda r, c: r <= c)
        from_s[...] = span_matrix(lambda r, c: r >= c)
        bias_s[...] = column(bias_ref[...], BLOCK)
        shards, _, width = time_ref.shape
        for s in range(shards):
            time_s[:, s * width : (s + 1) * width] = time_ref[s].astype(f32)
        for i in range(WIDE // 256):
            wide_s[i * 256 : (i + 1) * 256, :] = wide_ref[:, i * 256 : (i + 1) * 256].T

    @pl.when(block == 0)
    def _():
        last_s[...] = jnp.zeros_like(last_s)
        run_s[...] = jnp.zeros_like(run_s)

    @pl.when(block * BLOCK < length)
    def _():
        tok = tok_ref[0].astype(f32)
        scale = lax.rsqrt(jnp.mean(tok * tok, axis=-1, keepdims=True) + EPS)
        normed = (tok * scale * pre_s[...]).astype(bf16)
        x = mm_nt(time_s[...].astype(bf16), normed) + bias_s[...]
        steps = jnp.maximum(x, 0.0) + jnp.log1p(jnp.exp(-jnp.abs(x)))
        scaled = steps * rate_s[:, :1]
        fcum = exact_mm(scaled[:HEADS], until_s[...])
        rcum = exact_mm(scaled[HEADS:], from_s[...])
        least = jnp.log2(jnp.maximum(steps, TINY))
        cums = jnp.concatenate([fcum, rcum], axis=0)
        blank = jnp.zeros((SPAN - 48, BLOCK), f32)
        cols_o[0] = jnp.concatenate([cums - least, blank], axis=0).T
        rows_o[0, :48, :] = x
        rows_o[0, 48:96, :] = steps
        rows_o[0, 96:144, :] = cums
        rows_o[0, 144:192, :] = jnp.exp2(cums)
        for sub in range(SUBS):
            part = slice(sub * SPAN, (sub + 1) * SPAN)
            last = (sub + 1) * SPAN - 1
            rows_o[0, 192:216, part] = jnp.exp2(fcum[:, last : last + 1] - fcum[:, part]) * steps[:HEADS, part]
            first = sub * SPAN
            rows_o[0, 216:240, part] = jnp.exp2(rcum[:, first : first + 1] - rcum[:, part]) * steps[HEADS:, part]
        place = block * BLOCK + lax.broadcasted_iota(jnp.int32, (1, BLOCK), 1)
        mask = (place < length).astype(f32)

        def project(i):
            fin_o[0, i * 256 : (i + 1) * 256, :] = mm_nt(
                wide_s[INNER + i * 256 : INNER + (i + 1) * 256, :], normed
            ).astype(bf16)

        def filter_rows(i):
            r = slice(i * 32, (i + 1) * 32)
            now = fin_o[0, r, :]
            w = jnp.concatenate([last_s[r, :], now], axis=1)
            last_s[r, :] = now[:, SPAN:]
            twice = lambda k: jnp.concatenate([taps_s[k, r, :]] * 2, axis=1)
            acc = twice(4) + twice(3) * now.astype(f32)
            for lag in range(1, CONV):
                moved = pltpu.roll(w, lag, 1)[:, SPAN:].astype(f32)
                acc = acc + twice(3 - lag) * moved
            filt_o[0, r, :] = acc.astype(bf16)
            act = acc * sigmoid(acc)
            if i < INNER // 32:
                act = act * mask
            act_o[0, r, :] = act.astype(bf16)

        for i in range(CHANNELS // 256):
            project(i)
            if i:
                for j in range(8):
                    filter_rows((i - 1) * 8 + j)
        for i in range(INNER // 256):
            gate_o[0, i * 256 : (i + 1) * 256, :] = mm_nt(
                wide_s[i * 256 : (i + 1) * 256, :], normed
            ).astype(bf16)
            if i == 0:
                for j in range(8):
                    filter_rows((CHANNELS // 256 - 1) * 8 + j)

        lane = lax.broadcasted_iota(jnp.int32, (1, SPAN), 1)

        for sub in range(SUBS):
            cols = slice(sub * SPAN, (sub + 1) * SPAN)
            tail_f = rows_o[0, 192:216, cols]
            tail_r = rows_o[0, 216:240, cols]
            decay = rows_o[0, 144:168, (sub + 1) * SPAN - 1 : (sub + 1) * SPAN]
            ins_f = act_o[0, INNER : INNER + 64, cols].astype(f32)
            ins_r = act_o[0, INNER + 128 : INNER + 192, cols].astype(f32)
            for h in range(HEADS):
                rows = slice(h * 64, (h + 1) * 64)
                weighted = jnp.concatenate(
                    [
                        (ins_f * tail_f[h : h + 1]).astype(bf16),
                        (ins_r * tail_r[h : h + 1]).astype(bf16),
                    ],
                    axis=0,
                )
                fresh = mm_nt(act_o[0, rows, cols], weighted)
                run = run_s[rows, :]
                state_o[0, sub, rows, :] = jnp.where(lane < 64, run, fresh).astype(bf16)
                run_s[rows, :] = run * decay[h : h + 1] + fresh


def middle_kernel(
    len_ref,
    skip_ref,
    tok_ref,
    cot_ref,
    gate_ref,
    act_ref,
    rows_ref,
    cols_ref,
    state_ref,
    narrow_ref,
    post_ref,
    result_o,
    dgate_o,
    dval_o,
    dio_o,
    sums_o,
    dstate_o,
    rstate_o,
    narrow_o,
    post_o,
    skip_o,
    run_s,
    grun_s,
    ahead_s,
    behind_s,
    gated_s,
    dgn_s,
    spread_s,
    matrix_s,
    held_s,
    slope_s,
    norm_s,
    gain_s,
    narrow_s,
    post_s,
):
    seq = pl.program_id(0)
    step = pl.program_id(1)
    block = pl.num_programs(1) - 1 - step
    length = len_ref[seq]

    @pl.when((seq == 0) & (step == 0))
    def _():
        narrow_s[...] = jnp.zeros_like(narrow_s)
        post_s[...] = jnp.zeros_like(post_s)
        skip_o[...] = jnp.zeros_like(skip_o)
        spread_vectors(gain_s, post_ref, CONV + 2)

    @pl.when(step == 0)
    def _():
        run_s[...] = jnp.zeros_like(run_s)
        grun_s[...] = jnp.zeros_like(grun_s)

    @pl.when(block * BLOCK >= length)
    def _():
        result_o[...] = tok_ref[...]

    @pl.when(block * BLOCK < length)
    def _():
        rows_i, cols_i = iotas((SPAN, SPAN))
        lower = rows_i < cols_i
        upper = rows_i > cols_i
        lane = lax.broadcasted_iota(jnp.int32, (1, SPAN), 1)
        place = block * BLOCK + lax.broadcasted_iota(jnp.int32, (BLOCK, 1), 0)
        inside = place < length
        slope_s[...] = jnp.where(inside, cot_ref[0].astype(f32), 0.0).astype(bf16)
        for i in range(3):
            rows = slice(i * 512, (i + 1) * 512)
            dgn_s[rows, :] = mm_nt(narrow_ref[rows, :], slope_s[...])
        zero = jnp.zeros((64, SPAN), bf16)

        def span_scores(cols):
            fi = act_ref[0, INNER : INNER + 64, cols]
            fo = act_ref[0, INNER + 64 : INNER + 128, cols]
            ri = act_ref[0, INNER + 128 : INNER + 192, cols]
            ro = act_ref[0, INNER + 192 : INNER + 256, cols]
            return fi, fo, ri, ro

        def fold(value):
            return jnp.sum(value.reshape(8, 8, SPAN), axis=0)

        def forward_span(sub):
            cols = slice(sub * SPAN, (sub + 1) * SPAN)
            fcum = rows_ref[0, 96:120, cols]
            rcum = rows_ref[0, 120:144, cols]
            columns = cols_ref[0, cols, :]
            out_f = rows_ref[0, 144:168, cols]
            out_r = rows_ref[0, 168:192, cols]
            decay = rows_ref[0, 168:192, sub * SPAN : sub * SPAN + 1]
            fi, fo, ri, ro = span_scores(cols)
            ahead_scores = jnp.where(lower, mm_tn(fi, fo), 0.0)
            behind_scores = jnp.where(upper, mm_tn(ri, ro), 0.0)
            fo = fo.astype(f32)
            ro = ro.astype(f32)
            squares = jnp.zeros((8, SPAN), f32)
            dots = jnp.zeros((8, SPAN), f32)
            for h in range(HEADS):
                rows = slice(h * 64, (h + 1) * 64)
                power = jnp.where(
                    lower,
                    fcum[h : h + 1] - columns[:, h : h + 1],
                    rcum[h : h + 1] - columns[:, HEADS + h : HEADS + h + 1],
                )
                spread = jnp.exp2(power)
                spread_s[sub, h] = spread.astype(bf16)
                low = (spread * ahead_scores).astype(bf16)
                high = (spread * behind_scores).astype(bf16)
                out_low = (fo * out_f[h : h + 1]).astype(bf16)
                out_high = (ro * out_r[h : h + 1]).astype(bf16)
                matrix_s[sub, h, :SPAN] = low
                matrix_s[sub, h, SPAN : 2 * SPAN] = high
                matrix_s[sub, h, 2 * SPAN : 2 * SPAN + 64] = out_low
                matrix_s[sub, h, 2 * SPAN + 64 :] = out_high
                matrix = jnp.concatenate(
                    [
                        jnp.concatenate([low, out_low, zero], axis=0),
                        jnp.concatenate([high, zero, out_high], axis=0),
                    ],
                    axis=1,
                )
                state = state_ref[0, sub, rows, :].astype(f32)
                run = run_s[rows, :]
                rstate_o[0, sub, rows, :] = run.astype(bf16)
                held = jnp.where(lane < 64, state, run).astype(bf16)
                held_s[sub, rows, :] = held
                run_s[rows, :] = run * decay[h : h + 1] + state
                values = act_ref[0, rows, cols]
                pair = mm(jnp.concatenate([values, held], axis=1), matrix)
                ahead = pair[:, :SPAN]
                behind = pair[:, SPAN:]
                ahead_s[rows, cols] = ahead
                behind_s[rows, cols] = behind
                mixed = ahead + behind + skip_ref[h] * values.astype(f32)
                gate = gate_ref[0, rows, cols].astype(f32)
                gated = mixed * (gate * sigmoid(gate))
                gated_s[rows, cols] = gated
                squares = squares + fold(gated * gated)
                dots = dots + fold(gated * gain_s[rows, :] * dgn_s[rows, cols])
            rs = lax.rsqrt(jnp.sum(squares, axis=0, keepdims=True) * (1.0 / INNER) + EPS)
            pull = rs * rs * rs * (jnp.sum(dots, axis=0, keepdims=True) * (1.0 / INNER))
            norm_s[:1, cols] = rs
            norm_s[1:2, cols] = pull

        for sub in reversed(range(SUBS)):
            forward_span(sub)
        rs = norm_s[:1, :]

        def norm_rows(i, _):
            r = pl.ds(pl.multiple_of(i * 32, 32), 32)
            kept = gated_s[r, :] * rs
            gain = gain_s[r, :]
            dgate_o[0, r, :] = (kept * jnp.concatenate([gain, gain], axis=1)).astype(bf16)
            product = kept * dgn_s[r, :]
            post_s[r, :] += product[:, :SPAN] + product[:, SPAN:]
            return None

        lax.fori_loop(0, INNER // 32, norm_rows, None, unroll=8)
        gnormed = dgate_o[0]
        branch = mm_tn(gnormed, narrow_ref[...])
        result_o[0] = (tok_ref[0].astype(f32) + jnp.where(inside, branch, 0.0)).astype(bf16)
        for i in range(3):
            rows = slice(i * 512, (i + 1) * 512)
            narrow_s[rows, :] += mm(gnormed[rows], slope_s[...])

        def backward_span(sub):
            cols = slice(sub * SPAN, (sub + 1) * SPAN)
            out_f = rows_ref[0, 144:168, cols]
            out_r = rows_ref[0, 168:192, cols]
            decay = rows_ref[0, 144:168, (sub + 1) * SPAN - 1 : (sub + 1) * SPAN]
            fi, fo, ri, ro = span_scores(cols)
            rs = norm_s[:1, cols]
            pull = norm_s[1:2, cols]
            dscores = jnp.zeros((SPAN, SPAN), f32)
            dfo = jnp.zeros((64, SPAN), f32)
            dro = jnp.zeros((64, SPAN), f32)

            def down(value):
                return jnp.sum(value, axis=0, keepdims=True)

            for h in range(HEADS):
                rows = slice(h * 64, (h + 1) * 64)
                gate = gate_ref[0, rows, cols].astype(f32)
                sig = sigmoid(gate)
                values = act_ref[0, rows, cols]
                values32 = values.astype(f32)
                ahead = ahead_s[rows, cols]
                behind = behind_s[rows, cols]
                mixed = ahead + behind + skip_ref[h] * values32
                dgated = rs * (gain_s[rows, :] * dgn_s[rows, cols]) - gated_s[rows, cols] * pull
                dmixed = dgated * (gate * sig)
                dgate = dgated * mixed * (sig * (1.0 + gate * (1.0 - sig)))
                dgate_o[0, rows, cols] = dgate.astype(bf16)
                skip_o[h : h + 1, :] += down(dmixed * values32)
                dm = dmixed.astype(bf16)
                dm32 = dm.astype(f32)
                held = held_s[sub, rows, :]
                grad = mm_tn(jnp.concatenate([values, held], axis=1), dm)
                dscores = dscores + grad[:SPAN] * spread_s[sub, h].astype(f32)
                dfo = dfo + grad[SPAN : SPAN + 64] * out_f[h : h + 1]
                dro = dro + grad[SPAN + 64 :] * out_r[h : h + 1]
                dall = mm_nt(dm, matrix_s[sub, h])
                dlow = dall[:, :SPAN]
                dhigh = dall[:, SPAN : 2 * SPAN]
                dheld = dall[:, 2 * SPAN :]
                dval_o[0, rows, cols] = (dlow + dhigh + skip_ref[h] * dmixed).astype(bf16)
                run = grun_s[rows, :]
                dstate_o[0, sub, rows, :] = jnp.where(lane < 64, run, dheld).astype(bf16)
                grun_s[rows, :] = run * decay[h : h + 1] + dheld
                sums_o[0, h : h + 1, cols] = down(dm32 * ahead)
                sums_o[0, HEADS + h : HEADS + h + 1, cols] = down(dm32 * behind)
                sums_o[0, 2 * HEADS + h : 2 * HEADS + h + 1, cols] = down(values32 * dlow)
                sums_o[0, 3 * HEADS + h : 3 * HEADS + h + 1, cols] = down(values32 * dhigh)
                sums_o[0, 4 * HEADS + h : 4 * HEADS + h + 1, cols] = decay[h : h + 1] * down(
                    jnp.where(lane < 64, run * held.astype(f32), 0.0)
                )
            low = jnp.where(lower, dscores, 0.0).astype(bf16)
            high = jnp.where(upper, dscores, 0.0).astype(bf16)
            dio_o[0, 0:64, cols] = mm_nt(fo, low)
            dio_o[0, 64:128, cols] = dfo + mm(fi, low)
            dio_o[0, 128:192, cols] = mm_nt(ro, high)
            dio_o[0, 192:256, cols] = dro + mm(ri, high)

        for sub in reversed(range(SUBS)):
            backward_span(sub)

    @pl.when((seq == pl.num_programs(0) - 1) & (step == pl.num_programs(1) - 1))
    def _():
        post_o[...] = lane_sums(post_s[...])
        halves, shards, rows = narrow_o.shape[0] * SPAN // D, *narrow_o.shape[1:3]
        for unit in range(narrow_o.shape[0]):
            half, tile = divmod(unit, D // SPAN)
            for s in range(shards):
                start = (s * halves + half) * rows
                narrow_o[unit, s] = narrow_s[
                    start : start + rows, tile * SPAN : (tile + 1) * SPAN
                ].astype(bf16)


def leave_kernel(
    len_ref,
    filt_ref,
    act_ref,
    fin_ref,
    rows_ref,
    dval_ref,
    dio_ref,
    sums_ref,
    dstate_ref,
    rstate_ref,
    decay_ref,
    skip_ref,
    dfilt_o,
    draw_o,
    lines_o,
    heads_o,
    grun_s,
    near_s,
    dact_s,
    last_s,
    offset_s,
    taps_s,
    bias_s,
    decay_s,
    rate_s,
    ends_s,
    ahead_s,
    behind_s,
):
    seq = pl.program_id(0)
    block = pl.program_id(1)
    length = len_ref[seq]

    @pl.when((seq == 0) & (block == 0))
    def _():
        offset_s[...] = jnp.zeros_like(offset_s)
        taps_s[...] = jnp.zeros_like(taps_s)
        bias_s[...] = jnp.zeros_like(bias_s)
        decay_s[...] = jnp.zeros_like(decay_s)
        rate_s[...] = rate_columns(decay_ref) * (1.0 / LOG2E)
        same = span_matrix(lambda r, c: r == r)
        ahead_s[:BLOCK] = span_matrix(lambda r, c: r >= c)
        ahead_s[BLOCK : 2 * BLOCK] = span_matrix(lambda r, c: r < c)
        ahead_s[2 * BLOCK :] = same
        behind_s[:BLOCK] = span_matrix(lambda r, c: r <= c)
        behind_s[BLOCK : 2 * BLOCK] = span_matrix(lambda r, c: r > c)
        behind_s[2 * BLOCK :] = same

    @pl.when(block == 0)
    def _():
        grun_s[...] = jnp.zeros_like(grun_s)
        last_s[...] = jnp.zeros_like(last_s)

    @pl.when(block * BLOCK < length)
    def _():
        lane = lax.broadcasted_iota(jnp.int32, (1, SPAN), 1)

        place = block * BLOCK + lax.broadcasted_iota(jnp.int32, (1, BLOCK), 1)
        mask = (place < length).astype(f32)

        def filter_rows(i):
            r = slice(i * 32, (i + 1) * 32)
            filt = filt_ref[0, r, :].astype(f32)
            sig = sigmoid(filt)
            dact = dact_s[r, :]
            if i < INNER // 32:
                dact = dact * mask
            dfilt = dact * (sig * (1.0 + filt * (1.0 - sig)))
            dfilt_o[0, r, :] = dfilt.astype(bf16)
            offset_s[r, :] += dfilt[:, :SPAN] + dfilt[:, SPAN:]
            fin = fin_ref[0, r, :]
            w = jnp.concatenate([last_s[r, :], fin], axis=1)
            last_s[r, :] = fin[:, SPAN:]
            product = dfilt * fin.astype(f32)
            taps_s[3, r, :] += product[:, :SPAN] + product[:, SPAN:]
            for lag in range(1, CONV):
                product = dfilt * pltpu.roll(w, lag, 1)[:, SPAN:].astype(f32)
                taps_s[3 - lag, r, :] += product[:, :SPAN] + product[:, SPAN:]

        def span(sub):
            cols = slice(sub * SPAN, (sub + 1) * SPAN)
            tail_f = rows_ref[0, 192:216, cols]
            tail_r = rows_ref[0, 216:240, cols]
            decay = rows_ref[0, 168:192, sub * SPAN : sub * SPAN + 1]
            fi = act_ref[0, INNER : INNER + 64, cols].astype(f32)
            ri = act_ref[0, INNER + 128 : INNER + 192, cols].astype(f32)
            dfi = jnp.zeros((64, SPAN), f32)
            dri = jnp.zeros((64, SPAN), f32)
            for h in range(HEADS):
                rows = slice(h * 64, (h + 1) * 64)
                weighted = jnp.concatenate(
                    [
                        (fi * tail_f[h : h + 1]).astype(bf16),
                        (ri * tail_r[h : h + 1]).astype(bf16),
                    ],
                    axis=0,
                )
                dstate = dstate_ref[0, sub, rows, :].astype(f32)
                run = grun_s[rows, :]
                dfresh = jnp.where(lane < 64, dstate, run).astype(bf16)
                near_s[h : h + 1, cols] = decay[h : h + 1] * jnp.sum(
                    jnp.where(lane < 64, 0.0, run * rstate_ref[0, sub, rows, :].astype(f32)),
                    axis=0,
                    keepdims=True,
                )
                grun_s[rows, :] = run * decay[h : h + 1] + dstate
                values = act_ref[0, rows, cols]
                dact_s[rows, cols] = dval_ref[0, rows, cols].astype(f32) + mm(dfresh, weighted)
                dweighted = mm_tn(dfresh, values)
                part_f = dweighted[:64] * tail_f[h : h + 1]
                part_r = dweighted[64:] * tail_r[h : h + 1]
                dfi = dfi + part_f
                dri = dri + part_r
                ends_s[h : h + 1, cols] = jnp.sum(part_f * fi, axis=0, keepdims=True)
                ends_s[HEADS + h : HEADS + h + 1, cols] = jnp.sum(
                    part_r * ri, axis=0, keepdims=True
                )
                if sub == SUBS - 1:
                    filter_rows(2 * h)
                    filter_rows(2 * h + 1)
            dact_s[INNER : INNER + 64, cols] = dio_ref[0, 0:64, cols] + dfi
            dact_s[INNER + 64 : INNER + 128, cols] = dio_ref[0, 64:128, cols]
            dact_s[INNER + 128 : INNER + 192, cols] = dio_ref[0, 128:192, cols] + dri
            dact_s[INNER + 192 : INNER + 256, cols] = dio_ref[0, 192:256, cols]

        for sub in range(SUBS):
            span(sub)
        for i in range(INNER // 32, CHANNELS // 32):
            filter_rows(i)
        col_f = sums_ref[0, 2 * HEADS : 3 * HEADS, :]
        col_r = sums_ref[0, 3 * HEADS : 4 * HEADS, :]
        ends_f = ends_s[:HEADS, :]
        ends_r = ends_s[HEADS:, :]
        dfa = exact_mm(
            jnp.concatenate(
                [sums_ref[0, :HEADS, :] - col_f, ends_f, sums_ref[0, 4 * HEADS :, :]], axis=1
            ),
            ahead_s[...],
        )
        dra = exact_mm(
            jnp.concatenate(
                [sums_ref[0, HEADS : 2 * HEADS, :] - col_r, ends_r, near_s[...]], axis=1
            ),
            behind_s[...],
        )
        sig = jax.nn.sigmoid(rows_ref[0, :48, :])
        steps = rows_ref[0, 48:96, :]
        rate = rate_s[:, :1]
        share = sig / jnp.maximum(steps, TINY)
        passed = jnp.concatenate([dfa, dra], axis=0) * rate
        draw = jnp.concatenate([col_f + ends_f, col_r + ends_r], axis=0) * share + passed * sig
        draw_o[0] = draw.astype(bf16)
        bias_s[...] += draw[:, :SPAN] + draw[:, SPAN:]
        product = passed * steps
        decay_s[...] += product[:, :SPAN] + product[:, SPAN:]
    @pl.when((seq == pl.num_programs(0) - 1) & (block == pl.num_programs(1) - 1))
    def _():
        lines_o[...] = jnp.zeros_like(lines_o)
        heads_o[...] = jnp.zeros_like(heads_o)
        for k in range(CONV):
            lines_o[k : k + 1, :] = lane_sums(taps_s[k])
        lines_o[CONV : CONV + 1, :] = lane_sums(offset_s[...])
        heads_o[:1, : 2 * HEADS] = lane_sums(bias_s[...])
        heads_o[1:2, :HEADS] = lane_sums(decay_s[:HEADS] + decay_s[HEADS:])
        heads_o[2:3, :HEADS] = lane_sums(skip_ref[...])


def widen_kernel(
    len_ref,
    tok_ref,
    cot_ref,
    dgate_ref,
    dfilt_ref,
    next_ref,
    draw_ref,
    wide_ref,
    time_ref,
    vectors_ref,
    lines_ref,
    post_ref,
    slope_o,
    wide_o,
    small_o,
    dproj_s,
    taps_s,
    wide_s,
    time_s,
    total_s,
    pre_s,
    lines_s,
    turned_s,
):
    seq = pl.program_id(0)
    block = pl.program_id(1)
    length = len_ref[seq]

    @pl.when((seq == 0) & (block == 0))
    def _():
        wide_s[...] = jnp.zeros_like(wide_s)
        time_s[...] = jnp.zeros_like(time_s)
        total_s[...] = jnp.zeros_like(total_s)
        for k in range(CONV):
            spread_vectors(taps_s.at[k], vectors_ref, k)
        join_row(pre_s, vectors_ref, CONV + 1)
        shards, _, width = time_ref.shape
        for s in range(shards):
            turned_s[:, s * width : (s + 1) * width] = time_ref[s].astype(f32)

    @pl.when(block * BLOCK >= length)
    def _():
        slope_o[...] = cot_ref[...]

    @pl.when(block * BLOCK < length)
    def _():
        tok = tok_ref[0].astype(f32)
        scale = lax.rsqrt(jnp.mean(tok * tok, axis=-1, keepdims=True) + EPS)
        normed = (tok * scale * pre_s[...]).astype(bf16)
        normed_t = normed.T
        beyond = (block + 1) * BLOCK < length

        def filter_rows(i):
            r = slice(i * 32, (i + 1) * 32)
            following = jnp.where(beyond, next_ref[0, r, :].astype(f32), 0.0).astype(bf16)
            now = dfilt_ref[0, r, :]
            w = jnp.concatenate([now, following], axis=1)
            twice = lambda k: jnp.concatenate([taps_s[k, r, :]] * 2, axis=1)
            acc = twice(3) * now.astype(f32)
            for lag in range(1, CONV):
                moved = pltpu.roll(w, BLOCK + SPAN - lag, 1)[:, :BLOCK].astype(f32)
                acc = acc + twice(3 - lag) * moved
            dproj_s[i * 32 : (i + 1) * 32, :] = acc.astype(bf16)

        groups = CHANNELS // 32
        done = 0
        for i in range(WIDE // 256):
            rows = slice(i * 256, (i + 1) * 256)
            if i < INNER // 256:
                right = dgate_ref[0, rows, :]
            else:
                right = dproj_s[i * 256 - INNER : (i + 1) * 256 - INNER, :]
            wide_s[:, rows] += mm_nt(normed_t, right)
            upto = min(groups, -(-groups * (i + 1) // (INNER // 256)))
            for j in range(done, upto):
                filter_rows(j)
            done = upto
        draw = draw_ref[0]
        time_s[...] += mm(draw, normed)
        dnormed = (
            mm(wide_ref[:, :INNER], dgate_ref[0])
            + mm(wide_ref[:, INNER:], dproj_s[...])
            + mm_tn(turned_s[...].astype(bf16), draw)
        ).T
        product = dnormed * tok
        total_s[...] += jnp.sum((product * scale).reshape(BLOCK // 8, 8, D), axis=0)
        gain = pre_s[...]
        mean = jnp.mean(product * gain, axis=-1, keepdims=True)
        grad = scale * (gain * dnormed) - tok * (scale * scale * scale * mean)
        slope_o[0] = (cot_ref[0].astype(f32) + grad).astype(bf16)

    @pl.when((seq == pl.num_programs(0) - 1) & (block == pl.num_programs(1) - 1))
    def _():
        tiles, shards, rows = wide_o.shape[:3]
        for s in range(shards):
            own = slice(s * rows, (s + 1) * rows)
            for unit in range(tiles):
                wide_o[unit, s] = wide_s[own, unit * SPAN : (unit + 1) * SPAN].astype(bf16)
            lines_s[...] = jnp.zeros_like(lines_s)
            time_rows = time_s[...]
            for start in range(0, 2 * HEADS, rows):
                size = min(rows, 2 * HEADS - start)
                lines_s[:size, start : start + rows] = time_rows[start : start + size, own]
            small_o[0, s] = lines_s[...].astype(bf16)
        pre_sum = jnp.sum(total_s[...], axis=0, keepdims=True)
        vectors = [(lines_ref[k : k + 1, :], CHANNELS // shards) for k in range(CONV + 1)]
        vectors += [(pre_sum, rows), (post_ref[...], INNER // shards)]
        lines_s[...] = jnp.zeros_like(lines_s)
        for s in range(shards):
            line = 0
            for vector, width in vectors:
                for start in range(0, width, SPAN):
                    size = min(SPAN, width - start)
                    begin = s * width + start
                    lines_s[line : line + 1, :size] = vector[:, begin : begin + size]
                    line += 1
            small_o[1, s] = lines_s[...].astype(bf16)


def whole(shape):
    return pl.BlockSpec(
        shape, lambda s, c, *_: (0,) * len(shape), pipeline_mode=pl.Buffered(1)
    )


def layer(
    tokens, cotangent, lengths, wide, time, narrow, vectors, timestep_bias, decay_log, skip_gain
):
    count, length = tokens.shape[:2]
    shards = vectors.shape[0]
    rows = D // shards
    blocks = length // BLOCK
    spans = length // SPAN
    bias = timestep_bias[None]
    decay = decay_log[None]
    grid = (count, blocks)
    sds = jax.ShapeDtypeStruct

    def ahead(rows, width=BLOCK):
        return pl.BlockSpec((1, rows, width), lambda s, c, *_: (s, 0, c))

    def back(rows, width=BLOCK):
        return pl.BlockSpec((1, rows, width), lambda s, c, *_: (s, 0, blocks - 1 - c))

    def tall(reverse):
        if reverse:
            return pl.BlockSpec((1, BLOCK, D), lambda s, c, *_: (s, blocks - 1 - c, 0))
        return pl.BlockSpec((1, BLOCK, D), lambda s, c, *_: (s, c, 0))

    def states(reverse):
        if reverse:
            return pl.BlockSpec((1, SUBS, INNER, SPAN), lambda s, c, *_: (s, blocks - 1 - c, 0, 0))
        return pl.BlockSpec((1, SUBS, INNER, SPAN), lambda s, c, *_: (s, c, 0, 0))

    def turned(reverse):
        if reverse:
            return pl.BlockSpec((1, BLOCK, SPAN), lambda s, c, *_: (s, blocks - 1 - c, 0))
        return pl.BlockSpec((1, BLOCK, SPAN), lambda s, c, *_: (s, c, 0))

    params = pltpu.CompilerParams(
        dimension_semantics=("arbitrary", "arbitrary"), vmem_limit_bytes=VMEM_LIMIT
    )
    state_shape = sds((count, spans, INNER, SPAN), bf16)
    gate, fin, filt, act, step_rows, step_cols, state = pl.pallas_call(
        enter_kernel,
        grid_spec=pltpu.PrefetchScalarGridSpec(
            num_scalar_prefetch=1,
            grid=grid,
            in_specs=[
                tall(False), whole((D, WIDE)), whole(time.shape), whole(vectors.shape),
                whole((1, 48)), whole((1, HEADS)),
            ],
            out_specs=[
                ahead(INNER), ahead(CHANNELS), ahead(CHANNELS), ahead(CHANNELS), ahead(240), turned(False), states(False),
            ],
            scratch_shapes=[
                pltpu.VMEM((CHANNELS, SPAN), bf16),
                pltpu.VMEM((INNER, SPAN), f32),
                pltpu.VMEM((CONV + 1, CHANNELS, SPAN), f32),
                pltpu.VMEM((WIDE, D), bf16),
                pltpu.VMEM((48, D), f32),
                pltpu.VMEM((1, D), f32),
                pltpu.VMEM((48, SPAN), f32),
                pltpu.VMEM((48, BLOCK), f32),
                pltpu.VMEM((BLOCK, BLOCK), bf16),
                pltpu.VMEM((BLOCK, BLOCK), bf16),
            ],
        ),
        out_shape=[
            sds((count, INNER, length), bf16),
            sds((count, CHANNELS, length), bf16),
            sds((count, CHANNELS, length), bf16),
            sds((count, CHANNELS, length), bf16),
            sds((count, 240, length), f32),
            sds((count, length, SPAN), f32),
            state_shape,
        ],
        compiler_params=params,
        name="enter",
    )(lengths, tokens, wide, time, vectors, bias, decay)

    across = 2 * D // SPAN
    result, dgate, dval, dio, sums, dstate, rstate, narrow_grad, post_grad, skip_grad = pl.pallas_call(
        middle_kernel,
        grid_spec=pltpu.PrefetchScalarGridSpec(
            num_scalar_prefetch=1,
            grid=grid,
            in_specs=[
                pl.BlockSpec(memory_space=pltpu.SMEM),
                tall(True), tall(True), back(INNER), back(CHANNELS), back(240), turned(True), states(True),
                whole((INNER, D)), whole(vectors.shape),
            ],
            out_specs=[
                tall(True), back(INNER), back(INNER), back(256), back(120), states(True), states(True),
                whole((across, shards, rows, SPAN)), whole((1, INNER)), whole((HEADS, SPAN)),
            ],
            scratch_shapes=[
                pltpu.VMEM((INNER, SPAN), f32),
                pltpu.VMEM((INNER, SPAN), f32),
                pltpu.VMEM((INNER, BLOCK), f32),
                pltpu.VMEM((INNER, BLOCK), f32),
                pltpu.VMEM((INNER, BLOCK), f32),
                pltpu.VMEM((INNER, BLOCK), f32),
                pltpu.VMEM((SUBS, HEADS, SPAN, SPAN), bf16),
                pltpu.VMEM((SUBS, HEADS, 3 * SPAN, SPAN), bf16),
                pltpu.VMEM((SUBS, INNER, SPAN), bf16),
                pltpu.VMEM((BLOCK, D), bf16),
                pltpu.VMEM((8, BLOCK), f32),
                pltpu.VMEM((INNER, SPAN), f32),
                pltpu.VMEM((INNER, D), f32),
                pltpu.VMEM((INNER, SPAN), f32),
            ],
        ),
        out_shape=[
            sds((count, length, D), bf16),
            sds((count, INNER, length), bf16),
            sds((count, INNER, length), bf16),
            sds((count, 256, length), f32),
            sds((count, 120, length), f32),
            state_shape,
            state_shape,
            sds((across, shards, rows, SPAN), bf16),
            sds((1, INNER), f32),
            sds((HEADS, SPAN), f32),
        ],
        compiler_params=params,
        name="middle",
    )(lengths, skip_gain, tokens, cotangent, gate, act, step_rows, step_cols, state, narrow, vectors)

    dfilt, draw, lines, heads = pl.pallas_call(
        leave_kernel,
        grid_spec=pltpu.PrefetchScalarGridSpec(
            num_scalar_prefetch=1,
            grid=grid,
            in_specs=[
                ahead(CHANNELS), ahead(CHANNELS), ahead(CHANNELS), ahead(240), ahead(INNER), ahead(256), ahead(120),
                states(False), states(False), whole((1, HEADS)), whole((HEADS, SPAN)),
            ],
            out_specs=[
                ahead(CHANNELS), ahead(48), whole((8, CHANNELS)), whole((8, SPAN)),
            ],
            scratch_shapes=[
                pltpu.VMEM((INNER, SPAN), f32),
                pltpu.VMEM((HEADS, BLOCK), f32),
                pltpu.VMEM((CHANNELS, BLOCK), f32),
                pltpu.VMEM((CHANNELS, SPAN), bf16),
                pltpu.VMEM((CHANNELS, SPAN), f32),
                pltpu.VMEM((CONV, CHANNELS, SPAN), f32),
                pltpu.VMEM((48, SPAN), f32),
                pltpu.VMEM((48, SPAN), f32),
                pltpu.VMEM((48, SPAN), f32),
                pltpu.VMEM((48, BLOCK), f32),
                pltpu.VMEM((3 * BLOCK, BLOCK), bf16),
                pltpu.VMEM((3 * BLOCK, BLOCK), bf16),
            ],
        ),
        out_shape=[
            sds((count, CHANNELS, length), bf16),
            sds((count, 48, length), bf16),
            sds((8, CHANNELS), f32),
            sds((8, SPAN), f32),
        ],
        compiler_params=params,
        name="leave",
    )(lengths, filt, act, fin, step_rows, dval, dio, sums, dstate, rstate, decay, skip_grad)

    slope, wide_grad, small_grad = pl.pallas_call(
        widen_kernel,
        grid_spec=pltpu.PrefetchScalarGridSpec(
            num_scalar_prefetch=1,
            grid=grid,
            in_specs=[
                tall(False), tall(False), ahead(INNER), ahead(CHANNELS),
                pl.BlockSpec(
                    (1, CHANNELS, SPAN),
                    lambda s, c, *_: (s, 0, jnp.minimum(SUBS * (c + 1), spans - 1)),
                ),
                ahead(48),
                whole((D, WIDE)), whole(time.shape), whole(vectors.shape),
                whole((8, CHANNELS)), whole((1, INNER)),
            ],
            out_specs=[
                tall(False), whole((WIDE // SPAN, shards, rows, SPAN)), whole((2, shards, rows, SPAN)),
            ],
            scratch_shapes=[
                pltpu.VMEM((CHANNELS, BLOCK), bf16),
                pltpu.VMEM((CONV, CHANNELS, SPAN), f32),
                pltpu.VMEM((D, WIDE), f32),
                pltpu.VMEM((48, D), f32),
                pltpu.VMEM((8, D), f32),
                pltpu.VMEM((1, D), f32),
                pltpu.VMEM((rows, SPAN), f32),
                pltpu.VMEM((48, D), f32),
            ],
        ),
        out_shape=[
            sds((count, length, D), bf16),
            sds((WIDE // SPAN, shards, rows, SPAN), bf16),
            sds((2, shards, rows, SPAN), bf16),
        ],
        compiler_params=params,
        name="widen",
    )(lengths, tokens, cotangent, dgate, dfilt, dfilt, draw, wide, time, vectors, lines, post_grad)
    return result, slope, wide_grad, narrow_grad, small_grad, heads


def peer(rep, shard):
    return {"rep": rep, "shard": shard}


def remote(src, dst, send, recv, device):
    return pltpu.make_async_remote_copy(
        src_ref=src, dst_ref=dst, send_sem=send, recv_sem=recv,
        device_id=device, device_id_type=pl.DeviceIdType.MESH,
    )


def greet(devices):
    barrier = pltpu.get_barrier_semaphore()
    for device in devices:
        pl.semaphore_signal(barrier, inc=1, device_id=device, device_id_type=pl.DeviceIdType.MESH)
    pl.semaphore_wait(barrier, len(devices))


STRIDE = 2


def reduce_kernel(
    lines, wide,
    wide_ref, narrow_ref, small_ref, heads_ref, out_ref, heads_out_ref,
    own_s, near_s, sum_s, p1_s, q1_s, t0_s, t1_s, p2_s, q2_s, r_s, z_s,
    hc_s, hx_s, hy_s, hz_s,
    send_sem, recv_sem, hsend_sem, hrecv_sem, near_sem, arrive_sem, own_sem,
):
    piece, rows = out_ref.shape[3:5]
    sources = (wide_ref, narrow_ref, small_ref)
    rep = lax.axis_index("rep")
    shard = lax.axis_index("shard")
    core, x = lax.rem(rep, 2), lax.div(rep, 2)
    y, z = lax.rem(shard, 2), lax.div(shard, 2)
    sibling = peer(rep + 1 - 2 * core, shard)
    partner = peer(rep, shard + 1 - 2 * y)
    across = [peer(lax.rem(x + k, wide) * 2 + core, shard) for k in range(1, wide)]
    along = [peer(rep, lax.rem(z + k, lines) * 2 + y) for k in range(1, lines)]
    greet([sibling, partner, *across, *along])
    started = []
    used = [0, 0]

    def launch(src, dst, device, small=False):
        i = used[small]
        used[small] += 1
        pair = (hsend_sem, hrecv_sem) if small else (send_sem, recv_sem)
        copy = remote(src, dst, pair[0].at[i], pair[1].at[i], device)
        copy.start()
        started.append(copy)
        return copy

    def add(where, extents, dst, *srcs):
        flat = 1
        for extent in extents:
            flat *= extent
        for unit in range(*where):

            def body(i, _, unit=unit):
                place = []
                rest = i
                for extent in reversed(extents):
                    place.append(lax.rem(rest, extent))
                    rest = lax.div(rest, extent)
                place = tuple(reversed(place))
                total = None
                for ref, index in srcs:
                    term = ref[index(unit, *place)].astype(f32)
                    total = term if total is None else total + term
                ref, index = dst
                ref[index(unit, *place)] = total.astype(ref.dtype)
                return None

            lax.fori_loop(0, flat, body, None)

    def source(position, order, unit):
        j = (position * 2 + order) * piece + unit
        for ref in sources:
            if j < ref.shape[1]:
                return ref, j
            j -= ref.shape[1]
        return None, None

    def chunk(*where):
        units = pl.ds(where[0], where[1] - where[0])
        near = []
        own = []
        for position in range(wide):
            for order in range(2):
                for unit in range(*where):
                    ref, j = source(position, order, unit)
                    if ref is None:
                        continue
                    place = (position, order, unit)
                    i = (position * 2 + order) * piece + unit
                    copy = remote(
                        ref.at[1 - core, j], near_s.at[place], near_sem.at[i], arrive_sem.at[i], sibling
                    )
                    copy.start()
                    started.append(copy)
                    near.append((order, place, copy))
                    copy = pltpu.make_async_copy(ref.at[core, j], own_s.at[place], own_sem.at[i])
                    copy.start()
                    own.append((order, place, copy))
        yield
        for order in range(2):
            for position in range(wide):
                for unit in range(*where):
                    if source(position, order, unit)[0] is None:
                        sum_s[position, order, unit] = jnp.zeros(sum_s.shape[3:], bf16)
            for mine, theirs in zip(own, near):
                if mine[0] != order:
                    continue
                place = mine[1]
                mine[2].wait()
                theirs[2].wait_recv()
                add(
                    (place[2], place[2] + 1), (lines, 2),
                    (sum_s, lambda u, a, b, p=place: (*p, a, b)),
                    (own_s, lambda u, a, b, p=place: (*p, a, b)),
                    (near_s, lambda u, a, b, p=place: (*p, a, b)),
                )
            if order == 0:
                p1 = [
                    launch(sum_s.at[lax.rem(x + k, wide), 0, units], p1_s.at[k - 1, units], across[k - 1])
                    for k in range(1, wide)
                ]
            else:
                q1 = launch(sum_s.at[:, 1, units, :, 1 - y], q1_s.at[:, units], partner)
        yield
        for copy in p1:
            copy.wait_recv()
        add(
            where, (lines, 2),
            (t0_s, lambda u, a, b: (u, a, b)),
            (sum_s, lambda u, a, b: (x, 0, u, a, b)),
            *[(p1_s, lambda u, a, b, k=k: (k, u, a, b)) for k in range(wide - 1)],
        )
        p2 = launch(t0_s.at[units, :, 1 - y], p2_s.at[units], partner)
        q1.wait_recv()
        add(
            where, (wide, lines),
            (t1_s, lambda u, p, a: (p, u, a)),
            (sum_s, lambda u, p, a: (p, 1, u, a, y)),
            (q1_s, lambda u, p, a: (p, u, a)),
        )
        q2 = [
            launch(t1_s.at[lax.rem(x + k, wide), units], q2_s.at[k - 1, units], across[k - 1])
            for k in range(1, wide)
        ]
        yield
        p2.wait_recv()
        add(
            where, (lines,),
            (r_s, lambda u, a: (0, u, a)), (t0_s, lambda u, a: (u, a, y)), (p2_s, lambda u, a: (u, a)),
        )
        for copy in q2:
            copy.wait_recv()
        add(
            where, (lines,),
            (r_s, lambda u, a: (1, u, a)), (t1_s, lambda u, a: (x, u, a)),
            *[(q2_s, lambda u, a, k=k: (k, u, a)) for k in range(wide - 1)],
        )
        last = [
            launch(r_s.at[:, units, lax.rem(z + k, lines)], z_s.at[k - 1, :, units], along[k - 1])
            for k in range(1, lines)
        ]
        yield
        for copy in last:
            copy.wait_recv()
        add(
            where, (2,),
            (out_ref, lambda u, o: (core, x, o, u)), (r_s, lambda u, o: (o, u, z)),
            *[(z_s, lambda u, o, k=k: (k, o, u)) for k in range(lines - 1)],
        )
        mine = out_ref.at[core, x, :, units]
        shares = [launch(mine, mine, device) for device in across]
        yield
        for copy in shares:
            copy.wait_recv()
        half = out_ref.at[core, :, :, units]
        swap = launch(half, half, sibling)
        yield
        swap.wait_recv()
        yield

    def sum_heads():
        hc_s[core] = heads_ref[...]
        head = launch(hc_s.at[core], hc_s.at[core], sibling, True)
        yield
        head.wait_recv()
        hx_s[x] = hc_s[0] + hc_s[1]
        heads = [launch(hx_s.at[x], hx_s.at[x], device, True) for device in across]
        yield
        for copy in heads:
            copy.wait_recv()
        total = hx_s[0]
        for k in range(1, wide):
            total = total + hx_s[k]
        hy_s[y] = total
        head = launch(hy_s.at[y], hy_s.at[y], partner, True)
        yield
        head.wait_recv()
        hz_s[z] = hy_s[0] + hy_s[1]
        heads = [launch(hz_s.at[z], hz_s.at[z], device, True) for device in along]
        yield
        for copy in heads:
            copy.wait_recv()
        total = hz_s[0]
        for k in range(1, lines):
            total = total + hz_s[k]
        heads_out_ref[...] = total
        yield

    works = [chunk(i, min(i + STRIDE, piece)) for i in range(0, piece, STRIDE)]
    stages = 7
    small_work = sum_heads()
    for slot in range(len(works) + stages - 1):
        for g in range(len(works)):
            if 0 <= slot - g < stages:
                next(works[g])
        if slot < 5:
            next(small_work)
    for copy in started:
        copy.wait_send()


def reduce_units(wide_units, narrow_units, small_units, heads, wide, lines):
    rows = wide_units.shape[2]
    halves = [a.reshape(2, -1, lines, 2, rows, SPAN) for a in (wide_units, narrow_units, small_units)]
    used = sum(a.shape[1] for a in halves)
    unit = -(-used // (2 * wide))
    piece = (rows, SPAN)
    chunks = -(-unit // STRIDE)
    copies = (3 * (wide - 1) + 3 + lines - 1) * chunks
    small = 1 + (wide - 1) + 1 + (lines - 1)
    others = max(wide - 1, 1)
    vmem = pl.BlockSpec(memory_space=pltpu.VMEM)
    hbm = pl.BlockSpec(memory_space=pl.ANY)
    return pl.pallas_call(
        partial(reduce_kernel, lines, wide),
        in_specs=[hbm, hbm, hbm, vmem],
        out_specs=[vmem, vmem],
        out_shape=[
            jax.ShapeDtypeStruct((2, wide, 2, unit, *piece), bf16),
            jax.ShapeDtypeStruct((8, SPAN), f32),
        ],
        scratch_shapes=[
            pltpu.VMEM((wide, 2, unit, lines, 2, *piece), bf16),
            pltpu.VMEM((wide, 2, unit, lines, 2, *piece), bf16),
            pltpu.VMEM((wide, 2, unit, lines, 2, *piece), bf16),
            pltpu.VMEM((others, unit, lines, 2, *piece), bf16),
            pltpu.VMEM((wide, unit, lines, *piece), bf16),
            pltpu.VMEM((unit, lines, 2, *piece), bf16),
            pltpu.VMEM((wide, unit, lines, *piece), bf16),
            pltpu.VMEM((unit, lines, *piece), bf16),
            pltpu.VMEM((others, unit, lines, *piece), bf16),
            pltpu.VMEM((2, unit, lines, *piece), bf16),
            pltpu.VMEM((lines - 1, 2, unit, *piece), bf16),
            pltpu.VMEM((2, 8, SPAN), f32),
            pltpu.VMEM((wide, 8, SPAN), f32),
            pltpu.VMEM((2, 8, SPAN), f32),
            pltpu.VMEM((lines, 8, SPAN), f32),
            pltpu.SemaphoreType.DMA((copies,)),
            pltpu.SemaphoreType.DMA((copies,)),
            pltpu.SemaphoreType.DMA((small,)),
            pltpu.SemaphoreType.DMA((small,)),
            pltpu.SemaphoreType.DMA((2 * wide * unit,)),
            pltpu.SemaphoreType.DMA((2 * wide * unit,)),
            pltpu.SemaphoreType.DMA((2 * wide * unit,)),
        ],
        compiler_params=pltpu.CompilerParams(
            collective_id=1, has_side_effects=True, vmem_limit_bytes=VMEM_LIMIT
        ),
        name="reduce",
    )(*halves, heads)


def finish_kernel(
    wide, summed_ref, heads_ref,
    wide_o, time_o, narrow_o, taps_o, offset_o, pre_o, post_o, bias_o, decay_o, skip_o,
):
    unit, rows = summed_ref.shape[3:5]
    tiles_wide = wide_o.shape[1] // SPAN // 2
    tiles_narrow = narrow_o.shape[1] // SPAN

    def read(core, j):
        block, i = divmod(j, unit)
        return summed_ref[core, block // 2, block % 2, i].astype(f32)

    for core in range(2):
        for j in range(tiles_wide):
            column = (core * tiles_wide + j) * SPAN
            wide_o[:, column : column + SPAN] = read(core, j)
        for j in range(tiles_narrow):
            narrow_o[core * rows : (core + 1) * rows, j * SPAN : (j + 1) * SPAN] = read(
                core, tiles_wide + j
            )
    times = read(0, tiles_wide + tiles_narrow)
    for start in range(0, 2 * HEADS, rows):
        size = min(rows, 2 * HEADS - start)
        time_o[start : start + size, :] = times[:size, start : start + rows]
    vectors = read(1, tiles_wide + tiles_narrow)
    line = 0
    outs = [(taps_o, k) for k in range(CONV)] + [(offset_o, 0), (pre_o, 0), (post_o, 0)]
    for out, k in outs:
        width = out.shape[1]
        for start in range(0, width, SPAN):
            size = min(SPAN, width - start)
            out[k : k + 1, start : start + size] = vectors[line : line + 1, :size]
            line += 1
    bias_o[...] = heads_ref[:1, : 2 * HEADS]
    decay_o[...] = heads_ref[1:2, :HEADS]
    skip_o[...] = heads_ref[2:3, :HEADS]


def finish(summed, heads, wide, rows, width):
    shapes = [
        (rows, WIDE), (2 * HEADS, rows), (2 * rows, D), (CONV, width), (1, width), (1, rows), (1, 2 * rows),
        (1, 2 * HEADS), (1, HEADS), (1, HEADS),
    ]
    return pl.pallas_call(
        partial(finish_kernel, wide),
        out_shape=[jax.ShapeDtypeStruct(shape, f32) for shape in shapes],
        compiler_params=pltpu.CompilerParams(vmem_limit_bytes=VMEM_LIMIT),
        name="finish",
    )(summed, heads)


def gather_kernel(lines, large, kinds, *refs):
    ins, outs = refs[:kinds], refs[kinds : 2 * kinds]
    send_sem, recv_sem, own_sem, small_send, small_recv = refs[2 * kinds :]
    rep = lax.axis_index("rep")
    shard = lax.axis_index("shard")
    shards = 2 * lines
    core, x = lax.rem(rep, 2), lax.div(rep, 2)
    odd = lax.rem(x, 2)
    y, z = lax.rem(shard, 2), lax.div(shard, 2)
    sibling = peer(rep + 1 - 2 * core, shard)
    across = peer((x + 1 - 2 * odd) * 2 + core, shard)
    partner = peer(rep, shard + 1 - 2 * y)
    has_up, has_down = z < lines - 1, z > 0
    up = peer(rep, jnp.minimum(z + 1, lines - 1) * 2 + y)
    down = peer(rep, jnp.maximum(z - 1, 0) * 2 + y)
    away = [lax.rem(shard + k, shards) for k in range(1, shards)]
    greet([sibling, across, *[peer(rep, other) for other in away]])

    own = [
        pltpu.make_async_copy(src, dst.at[shard], own_sem.at[i])
        for i, (src, dst) in enumerate(zip(ins, outs))
    ]

    def place(group, part, ref, index, side):
        half = ref.shape[-1] // SPAN // 2
        thin = max(1, half * 5 // 13)
        thick = half - 2 * thin
        start = side * half
        if group:
            swap = odd if group == 1 else 1 - odd
            start = start + thick + swap * thin
        columns = pl.ds(pl.multiple_of(start * SPAN, SPAN), (thin if group else thick) * SPAN)
        return ref.at[:, columns] if index is None else ref.at[index, :, columns]

    def copies(way, group, index, device, mine=False, side=None):
        side = core if side is None else side
        return [
            remote(
                place(group, part, ins[part] if mine else outs[part], None if mine else index, side),
                place(group, part, outs[part], index, side),
                send_sem.at[way, group, part, index],
                recv_sem.at[way, 1 if way == 4 else group, part, index],
                device,
            )
            for part in range(large)
        ]

    def start(*args, **kw):
        for copy in copies(*args, **kw):
            copy.start()

    def arrive(*args, **kw):
        for copy in copies(*args, **kw):
            copy.wait_recv()

    def sent(*args, **kw):
        for copy in copies(*args, **kw):
            copy.wait_send()

    other = shard + 1 - 2 * y

    def index_of(line, side):
        return line * 2 + side

    for group in (1, 0):
        pl.when(has_up)(lambda group=group: start(1, group, shard, up, mine=True))
        pl.when(has_down)(lambda group=group: start(2, group, shard, down, mine=True))
        start(0, group, shard, partner, mine=True)
    for copy in own:
        copy.start()
    small = []
    for k, index in enumerate(away):
        for part in range(large, kinds):
            copy = remote(
                ins[part], outs[part].at[shard], small_send.at[part - large, k], small_recv.at[part - large, k],
                peer(rep, index),
            )
            copy.start()
            small.append(copy)

    def line_step(k, group):
        def spread(index):
            start(0, group, index, partner)
            if group == 1:
                start(4, 1, index, across)
            start(3, group, index, sibling)

        def from_below():
            index = index_of(z - k, y)
            arrive(1, group, index, down)
            pl.when(has_up)(lambda: start(1, group, index, up))
            spread(index)

        def from_above():
            index = index_of(z + k, y)
            arrive(2, group, index, up)
            pl.when(has_down)(lambda: start(2, group, index, down))
            spread(index)

        pl.when(z - k >= 0)(from_below)
        pl.when(z + k < lines)(from_above)

    def take(group, index):
        arrive(0, group, index, partner)
        if group == 1:
            start(4, 1, index, across)
        start(3, group, index, sibling)

    def cross(index):
        arrive(4, 2, index, across)
        start(3, 2, index, sibling)

    def either(k, action, side):
        pl.when(z - k >= 0)(lambda: action(index_of(z - k, side)))
        if k:
            pl.when(z + k < lines)(lambda: action(index_of(z + k, side)))

    take(1, other)
    take(0, other)
    for k in range(1, lines):
        line_step(k, 1)
        line_step(k, 0)
        if k > 1:
            either(k - 1, partial(take, 1), 1 - y)
            either(k - 1, partial(take, 0), 1 - y)
    either(lines - 1, partial(take, 1), 1 - y)
    either(lines - 1, partial(take, 0), 1 - y)
    either(0, cross, 1 - y)
    for k in range(1, lines):
        either(k, cross, y)
        either(k, cross, 1 - y)
    for index in range(shards):

        @pl.when(index != shard)
        def _(index=index):
            for group in range(3):
                arrive(3, group, index, sibling, side=1 - core)
                sent(3, group, index, sibling)
            sent(4, 1, index, across)

    for line in range(lines):
        for group in range(2):
            index = index_of(line, y)
            sent(0, group, index, partner)

            @pl.when((line <= z) & has_up)
            def _(group=group, index=index):
                sent(1, group, index, up)

            @pl.when((line >= z) & has_down)
            def _(group=group, index=index):
                sent(2, group, index, down)

    for copy in own:
        copy.wait()
    for copy in small:
        copy.wait_send()
    for k in range(1, shards):
        index = lax.rem(shard + shards - k, shards)
        for part in range(large, kinds):
            remote(
                ins[part], outs[part].at[index], small_send.at[part - large, k - 1],
                small_recv.at[part - large, k - 1], peer(rep, index),
            ).wait_recv()


def gather_weights(arrays, large, lines):
    shards = 2 * lines
    hbm = pl.BlockSpec(memory_space=pl.ANY)
    kinds = len(arrays)
    return pl.pallas_call(
        partial(gather_kernel, lines, large, kinds),
        in_specs=[hbm] * kinds,
        out_specs=[hbm] * kinds,
        out_shape=[jax.ShapeDtypeStruct((shards, *a.shape), a.dtype) for a in arrays],
        scratch_shapes=[
            pltpu.SemaphoreType.DMA((5, 3, large, shards)),
            pltpu.SemaphoreType.DMA((5, 3, large, shards)),
            pltpu.SemaphoreType.DMA((kinds,)),
            pltpu.SemaphoreType.DMA((kinds - large, shards - 1)),
            pltpu.SemaphoreType.DMA((kinds - large, shards - 1)),
        ],
        compiler_params=pltpu.CompilerParams(collective_id=0, has_side_effects=True),
        name="gather",
    )(*arrays)


def local(
    tokens,
    cotangent,
    lengths,
    widen_weight,
    timestep_weight,
    narrow_weight,
    filter_weight,
    filter_offset,
    prenorm_gain,
    postnorm_gain,
    timestep_bias,
    decay_log,
    skip_gain,
):
    lines = lax.axis_size("shard") // 2
    wide = lax.axis_size("rep") // 2
    rows = widen_weight.shape[0]
    width = filter_weight.shape[1]
    own = jnp.concatenate(
        [filter_weight.reshape(-1), filter_offset, prenorm_gain, postnorm_gain]
    )
    widen, narrow, timestep, vectors = gather_weights(
        [widen_weight, narrow_weight, timestep_weight.T, own[None]], 2, lines
    )
    result, slope, wide_grad, narrow_grad, small_grad, heads = layer(
        tokens, cotangent, lengths, widen.reshape(D, WIDE), timestep, narrow.reshape(INNER, D),
        vectors, timestep_bias, decay_log, skip_gain,
    )
    summed, heads = reduce_units(wide_grad, narrow_grad, small_grad, heads, wide, lines)
    (
        widen_out, timestep_out, narrow_out, filter_out, offset_out, prenorm_out, postnorm_out,
        bias_out, decay_out, skip_out,
    ) = finish(summed, heads, wide, rows, width)
    return (
        result, slope, widen_out, timestep_out.T, narrow_out, filter_out,
        *[row.reshape(-1) for row in (offset_out, prenorm_out, postnorm_out, bias_out, decay_out, skip_out)],
    )


def solution(mesh):
    placed = (
        P(("rep", "shard"), None, None),
        P(("rep", "shard"), None, None),
        P(("rep", "shard")),
        P("shard", None),
        P("shard", None),
        P("shard", None),
        P(None, "shard"),
        P("shard"),
        P("shard"),
        P("shard"),
        P(),
        P(),
        P(),
    )
    return jax.shard_map(
        local,
        mesh=mesh,
        in_specs=placed,
        out_specs=(
            P(("rep", "shard"), None, None),
            P(("rep", "shard"), None, None),
            P("shard", None),
            P("shard", None),
            P("shard", None),
            P(None, "shard"),
            P("shard"),
            P("shard"),
            P("shard"),
            P(),
            P(),
            P(),
        ),
        check_vma=False,
    )
```

```python
from functools import partial

import jax
import jax.numpy as jnp
from jax import lax
from jax.experimental import pallas as pl
from jax.experimental.pallas import tpu as pltpu
from jax.sharding import PartitionSpec as P

HEADS = 24
HEADDIM = 64
STATE = 64
CONV = 4
INNER = 1536
CHANNELS = 1792
D = 768
WIDE = INNER + CHANNELS
SPAN = 128
BLOCK = 256
SUBS = BLOCK // SPAN
EPS = 1e-05
LOG2E = 1.4426950408889634
TINY = 1.2e-38
f32 = jnp.float32
bf16 = jnp.bfloat16
precise = lax.Precision.HIGHEST
VMEM_LIMIT = 60 * 1024 * 1024


def mm(a, b, precision=None):
    return lax.dot_general(
        a, b, (((1,), (0,)), ((), ())), precision=precision, preferred_element_type=f32
    )


def mm_nt(a, b):
    return lax.dot_general(a, b, (((1,), (1,)), ((), ())), preferred_element_type=f32)


def mm_tn(a, b):
    return lax.dot_general(a, b, (((0,), (0,)), ((), ())), preferred_element_type=f32)


def mm_tn_precise(a, b):
    return lax.dot_general(
        a, b, (((0,), (0,)), ((), ())), precision=precise, preferred_element_type=f32
    )


def sigmoid(v):
    return 0.5 * jnp.tanh(0.5 * v) + 0.5


def iotas(shape):
    return (
        lax.broadcasted_iota(jnp.int32, shape, 0),
        lax.broadcasted_iota(jnp.int32, shape, 1),
    )


def column(row, lanes=SPAN):
    return mm_tn_precise(row, jnp.ones((1, lanes), f32))


def rate_columns(decay_ref):
    half = column(-jnp.exp(decay_ref[...]) * LOG2E)
    return jnp.concatenate([half, half], axis=0)


def vector_parts(vectors_ref):
    shards = vectors_ref.shape[0]
    sizes = [CHANNELS // shards] * (CONV + 1) + [D // shards, INNER // shards]
    starts = [sum(sizes[:i]) for i in range(len(sizes))]
    return [slice(start, start + size) for start, size in zip(starts, sizes)]


def spread_vectors(out_s, vectors_ref, which):
    part = vector_parts(vectors_ref)[which]
    width = part.stop - part.start
    for s in range(vectors_ref.shape[0]):
        out_s[s * width : (s + 1) * width, :] = mm_tn(
            vectors_ref[s, :, part], jnp.ones((1, SPAN), bf16)
        )


def join_row(row_s, vectors_ref, which):
    part = vector_parts(vectors_ref)[which]
    width = part.stop - part.start
    for s in range(vectors_ref.shape[0]):
        row_s[:, s * width : (s + 1) * width] = vectors_ref[s, :, part].astype(f32)


def split_rows(value):
    high = value.astype(bf16)
    rest = value - high.astype(f32)
    middle = rest.astype(bf16)
    low = (rest - middle.astype(f32)).astype(bf16)
    return jnp.concatenate([high, middle, low], axis=0)


def exact_mm(value, ones):
    m = value.shape[0]
    parts = mm(split_rows(value), ones)
    return (parts[2 * m :] + parts[m : 2 * m]) + parts[:m]


def span_matrix(compare):
    rows, cols = iotas((BLOCK, BLOCK))
    return (compare(rows, cols) & (rows // SPAN == cols // SPAN)).astype(bf16)


def lane_sums(value):
    m = value.shape[0]
    parts = mm_nt(jnp.ones((8, value.shape[1]), bf16), split_rows(value))[:1]
    return (parts[:, 2 * m :] + parts[:, m : 2 * m]) + parts[:, :m]


def enter_kernel(
    len_ref,
    tok_ref,
    wide_ref,
    time_ref,
    vectors_ref,
    bias_ref,
    decay_ref,
    gate_o,
    fin_o,
    filt_o,
    act_o,
    rows_o,
    cols_o,
    state_o,
    last_s,
    run_s,
    taps_s,
    wide_s,
    time_s,
    pre_s,
    rate_s,
    bias_s,
    until_s,
    from_s,
):
    seq = pl.program_id(0)
    block = pl.program_id(1)
    length = len_ref[seq]

    @pl.when((seq == 0) & (block == 0))
    def _():
        for k in range(CONV + 1):
            spread_vectors(taps_s.at[k], vectors_ref, k)
        join_row(pre_s, vectors_ref, CONV + 1)
        rate_s[...] = rate_columns(decay_ref)
        until_s[...] = span_matrix(lambda r, c: r <= c)
        from_s[...] = span_matrix(lambda r, c: r >= c)
        bias_s[...] = column(bias_ref[...], BLOCK)
        shards, _, width = time_ref.shape
        for s in range(shards):
            time_s[:, s * width : (s + 1) * width] = time_ref[s].astype(f32)
        for i in range(WIDE // 256):
            wide_s[i * 256 : (i + 1) * 256, :] = wide_ref[:, i * 256 : (i + 1) * 256].T

    @pl.when(block == 0)
    def _():
        last_s[...] = jnp.zeros_like(last_s)
        run_s[...] = jnp.zeros_like(run_s)

    @pl.when(block * BLOCK < length)
    def _():
        tok = tok_ref[0].astype(f32)
        scale = lax.rsqrt(jnp.mean(tok * tok, axis=-1, keepdims=True) + EPS)
        normed = (tok * scale * pre_s[...]).astype(bf16)
        x = mm_nt(time_s[...].astype(bf16), normed) + bias_s[...]
        steps = jnp.maximum(x, 0.0) + jnp.log1p(jnp.exp(-jnp.abs(x)))
        scaled = steps * rate_s[:, :1]
        fcum = exact_mm(scaled[:HEADS], until_s[...])
        rcum = exact_mm(scaled[HEADS:], from_s[...])
        least = jnp.log2(jnp.maximum(steps, TINY))
        cums = jnp.concatenate([fcum, rcum], axis=0)
        blank = jnp.zeros((SPAN - 48, BLOCK), f32)
        cols_o[0] = jnp.concatenate([cums - least, blank], axis=0).T
        rows_o[0, :48, :] = x
        rows_o[0, 48:96, :] = steps
        rows_o[0, 96:144, :] = cums
        rows_o[0, 144:192, :] = jnp.exp2(cums)
        for sub in range(SUBS):
            part = slice(sub * SPAN, (sub + 1) * SPAN)
            last = (sub + 1) * SPAN - 1
            rows_o[0, 192:216, part] = jnp.exp2(fcum[:, last : last + 1] - fcum[:, part]) * steps[:HEADS, part]
            first = sub * SPAN
            rows_o[0, 216:240, part] = jnp.exp2(rcum[:, first : first + 1] - rcum[:, part]) * steps[HEADS:, part]
        place = block * BLOCK + lax.broadcasted_iota(jnp.int32, (1, BLOCK), 1)
        mask = (place < length).astype(f32)

        def project(i):
            fin_o[0, i * 256 : (i + 1) * 256, :] = mm_nt(
                wide_s[INNER + i * 256 : INNER + (i + 1) * 256, :], normed
            ).astype(bf16)

        def filter_rows(i):
            r = slice(i * 32, (i + 1) * 32)
            now = fin_o[0, r, :]
            w = jnp.concatenate([last_s[r, :], now], axis=1)
            last_s[r, :] = now[:, SPAN:]
            twice = lambda k: jnp.concatenate([taps_s[k, r, :]] * 2, axis=1)
            acc = twice(4) + twice(3) * now.astype(f32)
            for lag in range(1, CONV):
                moved = pltpu.roll(w, lag, 1)[:, SPAN:].astype(f32)
                acc = acc + twice(3 - lag) * moved
            filt_o[0, r, :] = acc.astype(bf16)
            act = acc * sigmoid(acc)
            if i < INNER // 32:
                act = act * mask
            act_o[0, r, :] = act.astype(bf16)

        for i in range(CHANNELS // 256):
            project(i)
            if i:
                for j in range(8):
                    filter_rows((i - 1) * 8 + j)
        for i in range(INNER // 256):
            gate_o[0, i * 256 : (i + 1) * 256, :] = mm_nt(
                wide_s[i * 256 : (i + 1) * 256, :], normed
            ).astype(bf16)
            if i == 0:
                for j in range(8):
                    filter_rows((CHANNELS // 256 - 1) * 8 + j)

        lane = lax.broadcasted_iota(jnp.int32, (1, SPAN), 1)

        for sub in range(SUBS):
            cols = slice(sub * SPAN, (sub + 1) * SPAN)
            tail_f = rows_o[0, 192:216, cols]
            tail_r = rows_o[0, 216:240, cols]
            decay = rows_o[0, 144:168, (sub + 1) * SPAN - 1 : (sub + 1) * SPAN]
            ins_f = act_o[0, INNER : INNER + 64, cols].astype(f32)
            ins_r = act_o[0, INNER + 128 : INNER + 192, cols].astype(f32)
            for h in range(HEADS):
                rows = slice(h * 64, (h + 1) * 64)
                weighted = jnp.concatenate(
                    [
                        (ins_f * tail_f[h : h + 1]).astype(bf16),
                        (ins_r * tail_r[h : h + 1]).astype(bf16),
                    ],
                    axis=0,
                )
                fresh = mm_nt(act_o[0, rows, cols], weighted)
                run = run_s[rows, :]
                state_o[0, sub, rows, :] = jnp.where(lane < 64, run, fresh).astype(bf16)
                run_s[rows, :] = run * decay[h : h + 1] + fresh


def middle_kernel(
    len_ref,
    skip_ref,
    tok_ref,
    cot_ref,
    gate_ref,
    act_ref,
    rows_ref,
    cols_ref,
    state_ref,
    narrow_ref,
    post_ref,
    result_o,
    dgate_o,
    dval_o,
    dio_o,
    sums_o,
    dstate_o,
    rstate_o,
    narrow_o,
    post_o,
    skip_o,
    run_s,
    grun_s,
    ahead_s,
    behind_s,
    gated_s,
    dgn_s,
    spread_s,
    matrix_s,
    held_s,
    slope_s,
    norm_s,
    gain_s,
    narrow_s,
    post_s,
):
    seq = pl.program_id(0)
    step = pl.program_id(1)
    block = pl.num_programs(1) - 1 - step
    length = len_ref[seq]

    @pl.when((seq == 0) & (step == 0))
    def _():
        narrow_s[...] = jnp.zeros_like(narrow_s)
        post_s[...] = jnp.zeros_like(post_s)
        skip_o[...] = jnp.zeros_like(skip_o)
        spread_vectors(gain_s, post_ref, CONV + 2)

    @pl.when(step == 0)
    def _():
        run_s[...] = jnp.zeros_like(run_s)
        grun_s[...] = jnp.zeros_like(grun_s)

    @pl.when(block * BLOCK >= length)
    def _():
        result_o[...] = tok_ref[...]
        dgate_o[...] = jnp.zeros_like(dgate_o)

    @pl.when(block * BLOCK < length)
    def _():
        rows_i, cols_i = iotas((SPAN, SPAN))
        lower = rows_i < cols_i
        upper = rows_i > cols_i
        lane = lax.broadcasted_iota(jnp.int32, (1, SPAN), 1)
        place = block * BLOCK + lax.broadcasted_iota(jnp.int32, (BLOCK, 1), 0)
        inside = place < length
        slope_s[...] = jnp.where(inside, cot_ref[0].astype(f32), 0.0).astype(bf16)
        dgn_s[...] = mm_nt(narrow_ref[...], slope_s[...])
        zero = jnp.zeros((64, SPAN), bf16)

        def span_scores(cols):
            fi = act_ref[0, INNER : INNER + 64, cols]
            fo = act_ref[0, INNER + 64 : INNER + 128, cols]
            ri = act_ref[0, INNER + 128 : INNER + 192, cols]
            ro = act_ref[0, INNER + 192 : INNER + 256, cols]
            return fi, fo, ri, ro

        def fold(value):
            return jnp.sum(value.reshape(8, 8, SPAN), axis=0)

        def forward_span(sub):
            cols = slice(sub * SPAN, (sub + 1) * SPAN)
            fcum = rows_ref[0, 96:120, cols]
            rcum = rows_ref[0, 120:144, cols]
            columns = cols_ref[0, cols, :]
            out_f = rows_ref[0, 144:168, cols]
            out_r = rows_ref[0, 168:192, cols]
            decay = rows_ref[0, 168:192, sub * SPAN : sub * SPAN + 1]
            fi, fo, ri, ro = span_scores(cols)
            ahead_scores = jnp.where(lower, mm_tn(fi, fo), 0.0)
            behind_scores = jnp.where(upper, mm_tn(ri, ro), 0.0)
            fo = fo.astype(f32)
            ro = ro.astype(f32)
            squares = jnp.zeros((8, SPAN), f32)
            dots = jnp.zeros((8, SPAN), f32)
            for h in range(HEADS):
                rows = slice(h * 64, (h + 1) * 64)
                power = jnp.where(
                    lower,
                    fcum[h : h + 1] - columns[:, h : h + 1],
                    rcum[h : h + 1] - columns[:, HEADS + h : HEADS + h + 1],
                )
                spread = jnp.exp2(power)
                spread_s[sub, h] = spread.astype(bf16)
                low = (spread * ahead_scores).astype(bf16)
                high = (spread * behind_scores).astype(bf16)
                out_low = (fo * out_f[h : h + 1]).astype(bf16)
                out_high = (ro * out_r[h : h + 1]).astype(bf16)
                matrix_s[sub, h, :SPAN] = low
                matrix_s[sub, h, SPAN : 2 * SPAN] = high
                matrix_s[sub, h, 2 * SPAN : 2 * SPAN + 64] = out_low
                matrix_s[sub, h, 2 * SPAN + 64 :] = out_high
                matrix = jnp.concatenate(
                    [
                        jnp.concatenate([low, out_low, zero], axis=0),
                        jnp.concatenate([high, zero, out_high], axis=0),
                    ],
                    axis=1,
                )
                state = state_ref[0, sub, rows, :].astype(f32)
                run = run_s[rows, :]
                rstate_o[0, sub, rows, :] = run.astype(bf16)
                held = jnp.where(lane < 64, state, run).astype(bf16)
                held_s[sub, rows, :] = held
                run_s[rows, :] = run * decay[h : h + 1] + state
                values = act_ref[0, rows, cols]
                pair = mm(jnp.concatenate([values, held], axis=1), matrix)
                ahead = pair[:, :SPAN]
                behind = pair[:, SPAN:]
                ahead_s[rows, cols] = ahead
                behind_s[rows, cols] = behind
                mixed = ahead + behind + skip_ref[h] * values.astype(f32)
                gate = gate_ref[0, rows, cols].astype(f32)
                gated = mixed * (gate * sigmoid(gate))
                gated_s[rows, cols] = gated
                squares = squares + fold(gated * gated)
                dots = dots + fold(gated * gain_s[rows, :] * dgn_s[rows, cols])
            rs = lax.rsqrt(jnp.sum(squares, axis=0, keepdims=True) * (1.0 / INNER) + EPS)
            pull = rs * rs * rs * (jnp.sum(dots, axis=0, keepdims=True) * (1.0 / INNER))
            norm_s[:1, cols] = rs
            norm_s[1:2, cols] = pull

        for sub in reversed(range(SUBS)):
            forward_span(sub)
        rs = norm_s[:1, :]

        def norm_rows(i, _):
            r = pl.ds(pl.multiple_of(i * 32, 32), 32)
            kept = gated_s[r, :] * rs
            gain = gain_s[r, :]
            dgate_o[0, r, :] = (kept * jnp.concatenate([gain, gain], axis=1)).astype(bf16)
            product = kept * dgn_s[r, :]
            post_s[r, :] += product[:, :SPAN] + product[:, SPAN:]
            return None

        lax.fori_loop(0, INNER // 32, norm_rows, None, unroll=8)
        gnormed = dgate_o[0]
        branch = mm_tn(narrow_ref[...], gnormed).T
        result_o[0] = (tok_ref[0].astype(f32) + jnp.where(inside, branch, 0.0)).astype(bf16)
        narrow_s[...] += mm(gnormed, slope_s[...])

        def backward_span(sub):
            cols = slice(sub * SPAN, (sub + 1) * SPAN)
            out_f = rows_ref[0, 144:168, cols]
            out_r = rows_ref[0, 168:192, cols]
            decay = rows_ref[0, 144:168, (sub + 1) * SPAN - 1 : (sub + 1) * SPAN]
            fi, fo, ri, ro = span_scores(cols)
            rs = norm_s[:1, cols]
            pull = norm_s[1:2, cols]
            dscores = jnp.zeros((SPAN, SPAN), f32)
            dfo = jnp.zeros((64, SPAN), f32)
            dro = jnp.zeros((64, SPAN), f32)

            def down(value):
                return jnp.sum(value, axis=0, keepdims=True)

            for h in range(HEADS):
                rows = slice(h * 64, (h + 1) * 64)
                gate = gate_ref[0, rows, cols].astype(f32)
                sig = sigmoid(gate)
                values = act_ref[0, rows, cols]
                values32 = values.astype(f32)
                ahead = ahead_s[rows, cols]
                behind = behind_s[rows, cols]
                mixed = ahead + behind + skip_ref[h] * values32
                dgated = rs * (gain_s[rows, :] * dgn_s[rows, cols]) - gated_s[rows, cols] * pull
                dmixed = dgated * (gate * sig)
                dgate = dgated * mixed * (sig * (1.0 + gate * (1.0 - sig)))
                dgate_o[0, rows, cols] = dgate.astype(bf16)
                skip_o[h : h + 1, :] += down(dmixed * values32)
                dm = dmixed.astype(bf16)
                dm32 = dm.astype(f32)
                held = held_s[sub, rows, :]
                grad = mm_tn(jnp.concatenate([values, held], axis=1), dm)
                dscores = dscores + grad[:SPAN] * spread_s[sub, h].astype(f32)
                dfo = dfo + grad[SPAN : SPAN + 64] * out_f[h : h + 1]
                dro = dro + grad[SPAN + 64 :] * out_r[h : h + 1]
                dall = mm_nt(dm, matrix_s[sub, h])
                dlow = dall[:, :SPAN]
                dhigh = dall[:, SPAN : 2 * SPAN]
                dheld = dall[:, 2 * SPAN :]
                dval_o[0, rows, cols] = (dlow + dhigh + skip_ref[h] * dmixed).astype(bf16)
                run = grun_s[rows, :]
                dstate_o[0, sub, rows, :] = jnp.where(lane < 64, run, dheld).astype(bf16)
                grun_s[rows, :] = run * decay[h : h + 1] + dheld
                sums_o[0, h : h + 1, cols] = down(dm32 * ahead)
                sums_o[0, HEADS + h : HEADS + h + 1, cols] = down(dm32 * behind)
                sums_o[0, 2 * HEADS + h : 2 * HEADS + h + 1, cols] = down(values32 * dlow)
                sums_o[0, 3 * HEADS + h : 3 * HEADS + h + 1, cols] = down(values32 * dhigh)
                sums_o[0, 4 * HEADS + h : 4 * HEADS + h + 1, cols] = decay[h : h + 1] * down(
                    jnp.where(lane < 64, run * held.astype(f32), 0.0)
                )
            low = jnp.where(lower, dscores, 0.0).astype(bf16)
            high = jnp.where(upper, dscores, 0.0).astype(bf16)
            dio_o[0, 0:64, cols] = mm_nt(fo, low)
            dio_o[0, 64:128, cols] = dfo + mm(fi, low)
            dio_o[0, 128:192, cols] = mm_nt(ro, high)
            dio_o[0, 192:256, cols] = dro + mm(ri, high)

        for sub in reversed(range(SUBS)):
            backward_span(sub)

    @pl.when((seq == pl.num_programs(0) - 1) & (step == pl.num_programs(1) - 1))
    def _():
        post_o[...] = lane_sums(post_s[...])
        halves, shards, rows = narrow_o.shape[0] * SPAN // D, *narrow_o.shape[1:3]
        for unit in range(narrow_o.shape[0]):
            half, tile = divmod(unit, D // SPAN)
            for s in range(shards):
                start = (s * halves + half) * rows
                narrow_o[unit, s] = narrow_s[
                    start : start + rows, tile * SPAN : (tile + 1) * SPAN
                ].astype(bf16)


def leave_kernel(
    len_ref,
    filt_ref,
    act_ref,
    fin_ref,
    rows_ref,
    dval_ref,
    dio_ref,
    sums_ref,
    dstate_ref,
    rstate_ref,
    decay_ref,
    skip_ref,
    dfilt_o,
    draw_o,
    lines_o,
    heads_o,
    grun_s,
    near_s,
    dact_s,
    last_s,
    offset_s,
    taps_s,
    bias_s,
    decay_s,
    rate_s,
    ends_s,
    ahead_s,
    behind_s,
):
    seq = pl.program_id(0)
    block = pl.program_id(1)
    length = len_ref[seq]

    @pl.when((seq == 0) & (block == 0))
    def _():
        offset_s[...] = jnp.zeros_like(offset_s)
        taps_s[...] = jnp.zeros_like(taps_s)
        bias_s[...] = jnp.zeros_like(bias_s)
        decay_s[...] = jnp.zeros_like(decay_s)
        rate_s[...] = rate_columns(decay_ref) * (1.0 / LOG2E)
        same = span_matrix(lambda r, c: r == r)
        ahead_s[:BLOCK] = span_matrix(lambda r, c: r >= c)
        ahead_s[BLOCK : 2 * BLOCK] = span_matrix(lambda r, c: r < c)
        ahead_s[2 * BLOCK :] = same
        behind_s[:BLOCK] = span_matrix(lambda r, c: r <= c)
        behind_s[BLOCK : 2 * BLOCK] = span_matrix(lambda r, c: r > c)
        behind_s[2 * BLOCK :] = same

    @pl.when(block == 0)
    def _():
        grun_s[...] = jnp.zeros_like(grun_s)
        last_s[...] = jnp.zeros_like(last_s)

    @pl.when(block * BLOCK >= length)
    def _():
        draw_o[...] = jnp.zeros_like(draw_o)

    @pl.when(block * BLOCK < length)
    def _():
        lane = lax.broadcasted_iota(jnp.int32, (1, SPAN), 1)

        place = block * BLOCK + lax.broadcasted_iota(jnp.int32, (1, BLOCK), 1)
        mask = (place < length).astype(f32)

        def filter_rows(i):
            r = slice(i * 32, (i + 1) * 32)
            filt = filt_ref[0, r, :].astype(f32)
            sig = sigmoid(filt)
            dact = dact_s[r, :]
            if i < INNER // 32:
                dact = dact * mask
            dfilt = dact * (sig * (1.0 + filt * (1.0 - sig)))
            dfilt_o[0, r, :] = dfilt.astype(bf16)
            offset_s[r, :] += dfilt[:, :SPAN] + dfilt[:, SPAN:]
            fin = fin_ref[0, r, :]
            w = jnp.concatenate([last_s[r, :], fin], axis=1)
            last_s[r, :] = fin[:, SPAN:]
            product = dfilt * fin.astype(f32)
            taps_s[3, r, :] += product[:, :SPAN] + product[:, SPAN:]
            for lag in range(1, CONV):
                product = dfilt * pltpu.roll(w, lag, 1)[:, SPAN:].astype(f32)
                taps_s[3 - lag, r, :] += product[:, :SPAN] + product[:, SPAN:]

        def span(sub):
            cols = slice(sub * SPAN, (sub + 1) * SPAN)
            tail_f = rows_ref[0, 192:216, cols]
            tail_r = rows_ref[0, 216:240, cols]
            decay = rows_ref[0, 168:192, sub * SPAN : sub * SPAN + 1]
            fi = act_ref[0, INNER : INNER + 64, cols].astype(f32)
            ri = act_ref[0, INNER + 128 : INNER + 192, cols].astype(f32)
            dfi = jnp.zeros((64, SPAN), f32)
            dri = jnp.zeros((64, SPAN), f32)
            for h in range(HEADS):
                rows = slice(h * 64, (h + 1) * 64)
                weighted = jnp.concatenate(
                    [
                        (fi * tail_f[h : h + 1]).astype(bf16),
                        (ri * tail_r[h : h + 1]).astype(bf16),
                    ],
                    axis=0,
                )
                dstate = dstate_ref[0, sub, rows, :].astype(f32)
                run = grun_s[rows, :]
                dfresh = jnp.where(lane < 64, dstate, run).astype(bf16)
                near_s[h : h + 1, cols] = decay[h : h + 1] * jnp.sum(
                    jnp.where(lane < 64, 0.0, run * rstate_ref[0, sub, rows, :].astype(f32)),
                    axis=0,
                    keepdims=True,
                )
                grun_s[rows, :] = run * decay[h : h + 1] + dstate
                values = act_ref[0, rows, cols]
                dact_s[rows, cols] = dval_ref[0, rows, cols].astype(f32) + mm(dfresh, weighted)
                dweighted = mm_tn(dfresh, values)
                part_f = dweighted[:64] * tail_f[h : h + 1]
                part_r = dweighted[64:] * tail_r[h : h + 1]
                dfi = dfi + part_f
                dri = dri + part_r
                ends_s[h : h + 1, cols] = jnp.sum(part_f * fi, axis=0, keepdims=True)
                ends_s[HEADS + h : HEADS + h + 1, cols] = jnp.sum(
                    part_r * ri, axis=0, keepdims=True
                )
                if sub == SUBS - 1:
                    filter_rows(2 * h)
                    filter_rows(2 * h + 1)
            dact_s[INNER : INNER + 64, cols] = dio_ref[0, 0:64, cols] + dfi
            dact_s[INNER + 64 : INNER + 128, cols] = dio_ref[0, 64:128, cols]
            dact_s[INNER + 128 : INNER + 192, cols] = dio_ref[0, 128:192, cols] + dri
            dact_s[INNER + 192 : INNER + 256, cols] = dio_ref[0, 192:256, cols]

        for sub in range(SUBS):
            span(sub)
        for i in range(INNER // 32, CHANNELS // 32):
            filter_rows(i)
        col_f = sums_ref[0, 2 * HEADS : 3 * HEADS, :]
        col_r = sums_ref[0, 3 * HEADS : 4 * HEADS, :]
        ends_f = ends_s[:HEADS, :]
        ends_r = ends_s[HEADS:, :]
        dfa = exact_mm(
            jnp.concatenate(
                [sums_ref[0, :HEADS, :] - col_f, ends_f, sums_ref[0, 4 * HEADS :, :]], axis=1
            ),
            ahead_s[...],
        )
        dra = exact_mm(
            jnp.concatenate(
                [sums_ref[0, HEADS : 2 * HEADS, :] - col_r, ends_r, near_s[...]], axis=1
            ),
            behind_s[...],
        )
        sig = jax.nn.sigmoid(rows_ref[0, :48, :])
        steps = rows_ref[0, 48:96, :]
        rate = rate_s[:, :1]
        share = sig / jnp.maximum(steps, TINY)
        passed = jnp.concatenate([dfa, dra], axis=0) * rate
        draw = jnp.concatenate([col_f + ends_f, col_r + ends_r], axis=0) * share + passed * sig
        draw_o[0] = draw.astype(bf16)
        bias_s[...] += draw[:, :SPAN] + draw[:, SPAN:]
        product = passed * steps
        decay_s[...] += product[:, :SPAN] + product[:, SPAN:]
    @pl.when((seq == pl.num_programs(0) - 1) & (block == pl.num_programs(1) - 1))
    def _():
        lines_o[...] = jnp.zeros_like(lines_o)
        heads_o[...] = jnp.zeros_like(heads_o)
        for k in range(CONV):
            lines_o[k : k + 1, :] = lane_sums(taps_s[k])
        lines_o[CONV : CONV + 1, :] = lane_sums(offset_s[...])
        heads_o[:1, : 2 * HEADS] = lane_sums(bias_s[...])
        heads_o[1:2, :HEADS] = lane_sums(decay_s[:HEADS] + decay_s[HEADS:])
        heads_o[2:3, :HEADS] = lane_sums(skip_ref[...])


def widen_kernel(
    len_ref,
    tok_ref,
    dgate_ref,
    dfilt_ref,
    next_ref,
    draw_ref,
    vectors_ref,
    lines_ref,
    post_ref,
    dfin_o,
    wide_o,
    small_o,
    taps_s,
    wide_s,
    time_s,
    pre_s,
    lines_s,
):
    seq = pl.program_id(0)
    block = pl.program_id(1)
    length = len_ref[seq]

    @pl.when((seq == 0) & (block == 0))
    def _():
        wide_s[...] = jnp.zeros_like(wide_s)
        time_s[...] = jnp.zeros_like(time_s)
        for k in range(CONV):
            spread_vectors(taps_s.at[k], vectors_ref, k)
        join_row(pre_s, vectors_ref, CONV + 1)

    @pl.when(block * BLOCK >= length)
    def _():
        dfin_o[...] = jnp.zeros_like(dfin_o)

    @pl.when(block * BLOCK < length)
    def _():
        tok = tok_ref[0].astype(f32)
        scale = lax.rsqrt(jnp.mean(tok * tok, axis=-1, keepdims=True) + EPS)
        normed = (tok * scale * pre_s[...]).astype(bf16)
        normed_t = normed.T
        beyond = (block + 1) * BLOCK < length

        def filter_rows(i):
            r = slice(i * 32, (i + 1) * 32)
            following = jnp.where(beyond, next_ref[0, r, :].astype(f32), 0.0).astype(bf16)
            now = dfilt_ref[0, r, :]
            w = jnp.concatenate([now, following], axis=1)
            twice = lambda k: jnp.concatenate([taps_s[k, r, :]] * 2, axis=1)
            acc = twice(3) * now.astype(f32)
            for lag in range(1, CONV):
                moved = pltpu.roll(w, BLOCK + SPAN - lag, 1)[:, :BLOCK].astype(f32)
                acc = acc + twice(3 - lag) * moved
            dfin_o[0, r, :] = acc.astype(bf16)

        groups = CHANNELS // 32
        done = 0
        for i in range(WIDE // 256):
            rows = slice(i * 256, (i + 1) * 256)
            if i < INNER // 256:
                right = dgate_ref[0, rows, :]
            else:
                right = dfin_o[0, i * 256 - INNER : (i + 1) * 256 - INNER, :]
            wide_s[:, rows] += mm_nt(normed_t, right)
            upto = min(groups, -(-groups * (i + 1) // (INNER // 256)))
            for j in range(done, upto):
                filter_rows(j)
            done = upto
        draw = draw_ref[0]
        time_s[...] += mm(draw, normed)

    @pl.when((seq == pl.num_programs(0) - 1) & (block == pl.num_programs(1) - 1))
    def _():
        tiles, shards, rows = wide_o.shape[:3]
        for s in range(shards):
            own = slice(s * rows, (s + 1) * rows)
            for unit in range(tiles):
                wide_o[unit, s] = wide_s[own, unit * SPAN : (unit + 1) * SPAN].astype(bf16)
            lines_s[...] = jnp.zeros_like(lines_s)
            time_rows = time_s[...]
            for start in range(0, 2 * HEADS, rows):
                size = min(rows, 2 * HEADS - start)
                lines_s[:size, start : start + rows] = time_rows[start : start + size, own]
            small_o[0, s] = lines_s[...].astype(bf16)
        vectors = [(lines_ref[k : k + 1, :], CHANNELS // shards) for k in range(CONV + 1)]
        vectors += [(post_ref[...], INNER // shards)]
        lines_s[...] = jnp.zeros_like(lines_s)
        for s in range(shards):
            line = 0
            for vector, width in vectors:
                for start in range(0, width, SPAN):
                    size = min(SPAN, width - start)
                    begin = s * width + start
                    lines_s[line : line + 1, :size] = vector[:, begin : begin + size]
                    line += 1
            small_o[1, s] = lines_s[...].astype(bf16)


def whole(shape):
    return pl.BlockSpec(
        shape, lambda s, c, *_: (0,) * len(shape), pipeline_mode=pl.Buffered(1)
    )


def layer(
    tokens, cotangent, lengths, wide, time, narrow, vectors, timestep_bias, decay_log, skip_gain
):
    count, length = tokens.shape[:2]
    shards = vectors.shape[0]
    rows = D // shards
    blocks = length // BLOCK
    spans = length // SPAN
    bias = timestep_bias[None]
    decay = decay_log[None]
    grid = (count, blocks)
    sds = jax.ShapeDtypeStruct

    def ahead(rows, width=BLOCK):
        return pl.BlockSpec((1, rows, width), lambda s, c, *_: (s, 0, c))

    def back(rows, width=BLOCK):
        return pl.BlockSpec((1, rows, width), lambda s, c, *_: (s, 0, blocks - 1 - c))

    def tall(reverse):
        if reverse:
            return pl.BlockSpec((1, BLOCK, D), lambda s, c, *_: (s, blocks - 1 - c, 0))
        return pl.BlockSpec((1, BLOCK, D), lambda s, c, *_: (s, c, 0))

    def states(reverse):
        if reverse:
            return pl.BlockSpec((1, SUBS, INNER, SPAN), lambda s, c, *_: (s, blocks - 1 - c, 0, 0))
        return pl.BlockSpec((1, SUBS, INNER, SPAN), lambda s, c, *_: (s, c, 0, 0))

    def turned(reverse):
        if reverse:
            return pl.BlockSpec((1, BLOCK, SPAN), lambda s, c, *_: (s, blocks - 1 - c, 0))
        return pl.BlockSpec((1, BLOCK, SPAN), lambda s, c, *_: (s, c, 0))

    params = pltpu.CompilerParams(
        dimension_semantics=("arbitrary", "arbitrary"), vmem_limit_bytes=VMEM_LIMIT
    )
    state_shape = sds((count, spans, INNER, SPAN), bf16)
    gate, fin, filt, act, step_rows, step_cols, state = pl.pallas_call(
        enter_kernel,
        grid_spec=pltpu.PrefetchScalarGridSpec(
            num_scalar_prefetch=1,
            grid=grid,
            in_specs=[
                tall(False), whole((D, WIDE)), whole(time.shape), whole(vectors.shape),
                whole((1, 48)), whole((1, HEADS)),
            ],
            out_specs=[
                ahead(INNER), ahead(CHANNELS), ahead(CHANNELS), ahead(CHANNELS), ahead(240), turned(False), states(False),
            ],
            scratch_shapes=[
                pltpu.VMEM((CHANNELS, SPAN), bf16),
                pltpu.VMEM((INNER, SPAN), f32),
                pltpu.VMEM((CONV + 1, CHANNELS, SPAN), f32),
                pltpu.VMEM((WIDE, D), bf16),
                pltpu.VMEM((48, D), f32),
                pltpu.VMEM((1, D), f32),
                pltpu.VMEM((48, SPAN), f32),
                pltpu.VMEM((48, BLOCK), f32),
                pltpu.VMEM((BLOCK, BLOCK), bf16),
                pltpu.VMEM((BLOCK, BLOCK), bf16),
            ],
        ),
        out_shape=[
            sds((count, INNER, length), bf16),
            sds((count, CHANNELS, length), bf16),
            sds((count, CHANNELS, length), bf16),
            sds((count, CHANNELS, length), bf16),
            sds((count, 240, length), f32),
            sds((count, length, SPAN), f32),
            state_shape,
        ],
        compiler_params=params,
        name="enter",
    )(lengths, tokens, wide, time, vectors, bias, decay)

    across = 2 * D // SPAN
    result, dgate, dval, dio, sums, dstate, rstate, narrow_grad, post_grad, skip_grad = pl.pallas_call(
        middle_kernel,
        grid_spec=pltpu.PrefetchScalarGridSpec(
            num_scalar_prefetch=1,
            grid=grid,
            in_specs=[
                pl.BlockSpec(memory_space=pltpu.SMEM),
                tall(True), tall(True), back(INNER), back(CHANNELS), back(240), turned(True), states(True),
                whole((INNER, D)), whole(vectors.shape),
            ],
            out_specs=[
                tall(True), back(INNER), back(INNER), back(256), back(120), states(True), states(True),
                whole((across, shards, rows, SPAN)), whole((1, INNER)), whole((HEADS, SPAN)),
            ],
            scratch_shapes=[
                pltpu.VMEM((INNER, SPAN), f32),
                pltpu.VMEM((INNER, SPAN), f32),
                pltpu.VMEM((INNER, BLOCK), f32),
                pltpu.VMEM((INNER, BLOCK), f32),
                pltpu.VMEM((INNER, BLOCK), f32),
                pltpu.VMEM((INNER, BLOCK), f32),
                pltpu.VMEM((SUBS, HEADS, SPAN, SPAN), bf16),
                pltpu.VMEM((SUBS, HEADS, 3 * SPAN, SPAN), bf16),
                pltpu.VMEM((SUBS, INNER, SPAN), bf16),
                pltpu.VMEM((BLOCK, D), bf16),
                pltpu.VMEM((8, BLOCK), f32),
                pltpu.VMEM((INNER, SPAN), f32),
                pltpu.VMEM((INNER, D), f32),
                pltpu.VMEM((INNER, SPAN), f32),
            ],
        ),
        out_shape=[
            sds((count, length, D), bf16),
            sds((count, INNER, length), bf16),
            sds((count, INNER, length), bf16),
            sds((count, 256, length), f32),
            sds((count, 120, length), f32),
            state_shape,
            state_shape,
            sds((across, shards, rows, SPAN), bf16),
            sds((1, INNER), f32),
            sds((HEADS, SPAN), f32),
        ],
        compiler_params=params,
        name="middle",
    )(lengths, skip_gain, tokens, cotangent, gate, act, step_rows, step_cols, state, narrow, vectors)

    dfilt, draw, lines, heads = pl.pallas_call(
        leave_kernel,
        grid_spec=pltpu.PrefetchScalarGridSpec(
            num_scalar_prefetch=1,
            grid=grid,
            in_specs=[
                ahead(CHANNELS), ahead(CHANNELS), ahead(CHANNELS), ahead(240), ahead(INNER), ahead(256), ahead(120),
                states(False), states(False), whole((1, HEADS)), whole((HEADS, SPAN)),
            ],
            out_specs=[
                ahead(CHANNELS), ahead(48), whole((8, CHANNELS)), whole((8, SPAN)),
            ],
            scratch_shapes=[
                pltpu.VMEM((INNER, SPAN), f32),
                pltpu.VMEM((HEADS, BLOCK), f32),
                pltpu.VMEM((CHANNELS, BLOCK), f32),
                pltpu.VMEM((CHANNELS, SPAN), bf16),
                pltpu.VMEM((CHANNELS, SPAN), f32),
                pltpu.VMEM((CONV, CHANNELS, SPAN), f32),
                pltpu.VMEM((48, SPAN), f32),
                pltpu.VMEM((48, SPAN), f32),
                pltpu.VMEM((48, SPAN), f32),
                pltpu.VMEM((48, BLOCK), f32),
                pltpu.VMEM((3 * BLOCK, BLOCK), bf16),
                pltpu.VMEM((3 * BLOCK, BLOCK), bf16),
            ],
        ),
        out_shape=[
            sds((count, CHANNELS, length), bf16),
            sds((count, 48, length), bf16),
            sds((8, CHANNELS), f32),
            sds((8, SPAN), f32),
        ],
        compiler_params=params,
        name="leave",
    )(lengths, filt, act, fin, step_rows, dval, dio, sums, dstate, rstate, decay, skip_grad)

    dfin, wide_grad, small_grad = pl.pallas_call(
        widen_kernel,
        grid_spec=pltpu.PrefetchScalarGridSpec(
            num_scalar_prefetch=1,
            grid=grid,
            in_specs=[
                tall(False), ahead(INNER), ahead(CHANNELS),
                pl.BlockSpec(
                    (1, CHANNELS, SPAN),
                    lambda s, c, *_: (s, 0, jnp.minimum(SUBS * (c + 1), spans - 1)),
                ),
                ahead(48),
                whole(vectors.shape),
                whole((8, CHANNELS)), whole((1, INNER)),
            ],
            out_specs=[
                ahead(CHANNELS), whole((WIDE // SPAN, shards, rows, SPAN)), whole((2, shards, rows, SPAN)),
            ],
            scratch_shapes=[
                pltpu.VMEM((CONV, CHANNELS, SPAN), f32),
                pltpu.VMEM((D, WIDE), f32),
                pltpu.VMEM((48, D), f32),
                pltpu.VMEM((1, D), f32),
                pltpu.VMEM((rows, SPAN), f32),
            ],
        ),
        out_shape=[
            sds((count, CHANNELS, length), bf16),
            sds((WIDE // SPAN, shards, rows, SPAN), bf16),
            sds((2, shards, rows, SPAN), bf16),
        ],
        compiler_params=params,
        name="widen",
    )(lengths, tokens, dgate, dfilt, dfilt, draw, vectors, lines, post_grad)
    return result, (dgate, dfin, draw), wide_grad, narrow_grad, small_grad, heads


def peer(rep, shard):
    return {"rep": rep, "shard": shard}


def remote(src, dst, send, recv, device):
    return pltpu.make_async_remote_copy(
        src_ref=src, dst_ref=dst, send_sem=send, recv_sem=recv,
        device_id=device, device_id_type=pl.DeviceIdType.MESH,
    )


def greet(devices):
    barrier = pltpu.get_barrier_semaphore()
    for device in devices:
        pl.semaphore_signal(barrier, inc=1, device_id=device, device_id_type=pl.DeviceIdType.MESH)
    pl.semaphore_wait(barrier, len(devices))


STRIDE = 2


def reduce_kernel(
    lines, wide,
    wide_ref, narrow_ref, small_ref, heads_ref,
    tok_ref, cot_ref, dgate_ref, dfin_ref, draw_ref, weight_ref, time_ref, vectors_ref,
    out_ref, heads_out_ref, slope_ref,
    own_s, near_s, sum_s, p1_s, q1_s, t0_s, t1_s, p2_s, q2_s, r_s, z_s,
    hc_s, hx_s, hy_s, hz_s,
    send_sem, recv_sem, hsend_sem, hrecv_sem, near_sem, arrive_sem, own_sem,
    heads_s, weight_s, turned_s, gain_s, total_s, tok_s, cot_s, dgate_s, dfin_s, draw_s, slope_s,
    in_sem, put_sem, weight_sem,
):
    piece, rows = out_ref.shape[3:5]
    sources = (wide_ref, narrow_ref, small_ref)
    rep = lax.axis_index("rep")
    shard = lax.axis_index("shard")
    core, x = lax.rem(rep, 2), lax.div(rep, 2)
    y, z = lax.rem(shard, 2), lax.div(shard, 2)
    sibling = peer(rep + 1 - 2 * core, shard)
    partner = peer(rep, shard + 1 - 2 * y)
    across = [peer(lax.rem(x + k, wide) * 2 + core, shard) for k in range(1, wide)]
    along = [peer(rep, lax.rem(z + k, lines) * 2 + y) for k in range(1, lines)]
    greet([sibling, partner, *across, *along])
    started = []
    used = [0, 0]

    def launch(src, dst, device, small=False):
        i = used[small]
        used[small] += 1
        pair = (hsend_sem, hrecv_sem) if small else (send_sem, recv_sem)
        copy = remote(src, dst, pair[0].at[i], pair[1].at[i], device)
        copy.start()
        started.append(copy)
        return copy

    def add(where, extents, dst, *srcs):
        flat = 1
        for extent in extents:
            flat *= extent
        for unit in range(*where):

            def body(i, _, unit=unit):
                place = []
                rest = i
                for extent in reversed(extents):
                    place.append(lax.rem(rest, extent))
                    rest = lax.div(rest, extent)
                place = tuple(reversed(place))
                total = None
                for ref, index in srcs:
                    term = ref[index(unit, *place)].astype(f32)
                    total = term if total is None else total + term
                ref, index = dst
                ref[index(unit, *place)] = total.astype(ref.dtype)
                return None

            lax.fori_loop(0, flat, body, None)

    def source(position, order, unit):
        j = (position * 2 + order) * piece + unit
        for ref in sources:
            if j < ref.shape[1]:
                return ref, j
            j -= ref.shape[1]
        return None, None

    def chunk(*where):
        units = pl.ds(where[0], where[1] - where[0])
        near = []
        own = []
        for position in range(wide):
            for order in range(2):
                for unit in range(*where):
                    ref, j = source(position, order, unit)
                    if ref is None:
                        continue
                    place = (position, order, unit)
                    i = (position * 2 + order) * piece + unit
                    copy = remote(
                        ref.at[1 - core, j], near_s.at[place], near_sem.at[i], arrive_sem.at[i], sibling
                    )
                    copy.start()
                    started.append(copy)
                    near.append((order, place, copy))
                    copy = pltpu.make_async_copy(ref.at[core, j], own_s.at[place], own_sem.at[i])
                    copy.start()
                    own.append((order, place, copy))
        yield
        for order in range(2):
            for position in range(wide):
                for unit in range(*where):
                    if source(position, order, unit)[0] is None:
                        sum_s[position, order, unit] = jnp.zeros(sum_s.shape[3:], bf16)
            for mine, theirs in zip(own, near):
                if mine[0] != order:
                    continue
                place = mine[1]
                mine[2].wait()
                theirs[2].wait_recv()
                add(
                    (place[2], place[2] + 1), (lines, 2),
                    (sum_s, lambda u, a, b, p=place: (*p, a, b)),
                    (own_s, lambda u, a, b, p=place: (*p, a, b)),
                    (near_s, lambda u, a, b, p=place: (*p, a, b)),
                )
            if order == 0:
                p1 = [
                    launch(sum_s.at[lax.rem(x + k, wide), 0, units], p1_s.at[k - 1, units], across[k - 1])
                    for k in range(1, wide)
                ]
            else:
                q1 = launch(sum_s.at[:, 1, units, :, 1 - y], q1_s.at[:, units], partner)
        yield
        for copy in p1:
            copy.wait_recv()
        add(
            where, (lines, 2),
            (t0_s, lambda u, a, b: (u, a, b)),
            (sum_s, lambda u, a, b: (x, 0, u, a, b)),
            *[(p1_s, lambda u, a, b, k=k: (k, u, a, b)) for k in range(wide - 1)],
        )
        p2 = launch(t0_s.at[units, :, 1 - y], p2_s.at[units], partner)
        q1.wait_recv()
        add(
            where, (wide, lines),
            (t1_s, lambda u, p, a: (p, u, a)),
            (sum_s, lambda u, p, a: (p, 1, u, a, y)),
            (q1_s, lambda u, p, a: (p, u, a)),
        )
        q2 = [
            launch(t1_s.at[lax.rem(x + k, wide), units], q2_s.at[k - 1, units], across[k - 1])
            for k in range(1, wide)
        ]
        yield
        p2.wait_recv()
        add(
            where, (lines,),
            (r_s, lambda u, a: (0, u, a)), (t0_s, lambda u, a: (u, a, y)), (p2_s, lambda u, a: (u, a)),
        )
        for copy in q2:
            copy.wait_recv()
        add(
            where, (lines,),
            (r_s, lambda u, a: (1, u, a)), (t1_s, lambda u, a: (x, u, a)),
            *[(q2_s, lambda u, a, k=k: (k, u, a)) for k in range(wide - 1)],
        )
        last = [
            launch(r_s.at[:, units, lax.rem(z + k, lines)], z_s.at[k - 1, :, units], along[k - 1])
            for k in range(1, lines)
        ]
        yield
        for copy in last:
            copy.wait_recv()
        add(
            where, (2,),
            (out_ref, lambda u, o: (core, x, o, u)), (r_s, lambda u, o: (o, u, z)),
            *[(z_s, lambda u, o, k=k: (k, o, u)) for k in range(lines - 1)],
        )
        mine = out_ref.at[core, x, :, units]
        shares = [launch(mine, mine, device) for device in across]
        yield
        for copy in shares:
            copy.wait_recv()
        half = out_ref.at[core, :, :, units]
        swap = launch(half, half, sibling)
        yield
        swap.wait_recv()
        yield

    blocks = tok_ref.shape[1] // BLOCK
    total_blocks = tok_ref.shape[0] * blocks

    def fetch(b):
        seq, block = divmod(b, blocks)
        slot = b % 2
        part = slice(block * BLOCK, (block + 1) * BLOCK)
        pairs = [
            (tok_ref.at[seq, part, :], tok_s.at[slot]),
            (cot_ref.at[seq, part, :], cot_s.at[slot]),
            (dgate_ref.at[seq, :, part], dgate_s.at[slot]),
            (dfin_ref.at[seq, :, part], dfin_s.at[slot]),
            (draw_ref.at[seq, :, part], draw_s.at[slot]),
        ]
        made = [pltpu.make_async_copy(src, dst, in_sem.at[slot, i]) for i, (src, dst) in enumerate(pairs)]
        for copy in made:
            copy.start()
        return made

    def token_gradient():
        weights = pltpu.make_async_copy(weight_ref, weight_s, weight_sem.at[0])
        weights.start()
        coming = fetch(0)
        join_row(gain_s, vectors_ref, CONV + 1)
        for s in range(time_ref.shape[0]):
            width = time_ref.shape[2]
            turned_s[:, s * width : (s + 1) * width] = time_ref[s].astype(f32)
        total_s[...] = jnp.zeros_like(total_s)
        put = []
        yield
        for b in range(total_blocks):
            slot = b % 2
            now = coming
            if b + 1 < total_blocks:
                coming = fetch(b + 1)
            for copy in now:
                copy.wait()
            if b == 0:
                weights.wait()
            if b >= 2:
                put[b - 2].wait()
            dnormed = (
                mm(weight_s[:, :INNER], dgate_s[slot])
                + mm(weight_s[:, INNER:], dfin_s[slot])
                + mm_tn(turned_s[...].astype(bf16), draw_s[slot])
            ).T
            tok = tok_s[slot].astype(f32)
            scale = lax.rsqrt(jnp.mean(tok * tok, axis=-1, keepdims=True) + EPS)
            product = dnormed * tok
            total_s[...] += jnp.sum((product * scale).reshape(BLOCK // 8, 8, D), axis=0)
            gain = gain_s[...]
            mean = jnp.mean(product * gain, axis=-1, keepdims=True)
            grad = scale * (gain * dnormed) - tok * (scale * scale * scale * mean)
            slope_s[slot] = (cot_s[slot].astype(f32) + grad).astype(bf16)
            seq, block = divmod(b, blocks)
            copy = pltpu.make_async_copy(
                slope_s.at[slot],
                slope_ref.at[seq, slice(block * BLOCK, (block + 1) * BLOCK), :],
                put_sem.at[slot],
            )
            copy.start()
            put.append(copy)
            yield
        for copy in put[-2:]:
            copy.wait()
        heads_s[:8, :] = heads_ref[...]
        heads_s[8:, :] = jnp.zeros((8, SPAN), f32)
        pre_sum = jnp.sum(total_s[...], axis=0, keepdims=True)
        for k in range(D // SPAN):
            heads_s[8 + k : 9 + k, :] = pre_sum[:, k * SPAN : (k + 1) * SPAN]
        yield

    def sum_heads():
        hc_s[core] = heads_s[...]
        head = launch(hc_s.at[core], hc_s.at[core], sibling, True)
        yield
        head.wait_recv()
        hx_s[x] = hc_s[0] + hc_s[1]
        heads = [launch(hx_s.at[x], hx_s.at[x], device, True) for device in across]
        yield
        for copy in heads:
            copy.wait_recv()
        total = hx_s[0]
        for k in range(1, wide):
            total = total + hx_s[k]
        hy_s[y] = total
        head = launch(hy_s.at[y], hy_s.at[y], partner, True)
        yield
        head.wait_recv()
        hz_s[z] = hy_s[0] + hy_s[1]
        heads = [launch(hz_s.at[z], hz_s.at[z], device, True) for device in along]
        yield
        for copy in heads:
            copy.wait_recv()
        total = hz_s[0]
        for k in range(1, lines):
            total = total + hz_s[k]
        heads_out_ref[...] = total
        yield

    works = [chunk(i, min(i + STRIDE, piece)) for i in range(0, piece, STRIDE)]
    stages = 7
    small_work = sum_heads()
    token_work = token_gradient()
    steps = total_blocks + 2
    early = 4
    for slot in range(max(len(works) + stages - 1, early + 5)):
        left = steps * (slot + 1) // early - steps * slot // early if slot < early else 0
        for g in range(len(works)):
            if 0 <= slot - g < stages:
                next(works[g])
                if left:
                    next(token_work)
                    left -= 1
        for _ in range(left):
            next(token_work)
        if early <= slot < early + 5:
            next(small_work)
    for copy in started:
        copy.wait_send()


def reduce_units(
    wide_units, narrow_units, small_units, heads, tokens, cotangent, parts, weight, time, vectors, wide, lines
):
    rows = wide_units.shape[2]
    halves = [a.reshape(2, -1, lines, 2, rows, SPAN) for a in (wide_units, narrow_units, small_units)]
    used = sum(a.shape[1] for a in halves)
    unit = -(-used // (2 * wide))
    piece = (rows, SPAN)
    chunks = -(-unit // STRIDE)
    copies = (3 * (wide - 1) + 3 + lines - 1) * chunks
    small = 1 + (wide - 1) + 1 + (lines - 1)
    others = max(wide - 1, 1)
    vmem = pl.BlockSpec(memory_space=pltpu.VMEM)
    hbm = pl.BlockSpec(memory_space=pl.ANY)
    return pl.pallas_call(
        partial(reduce_kernel, lines, wide),
        in_specs=[hbm, hbm, hbm, vmem] + [hbm] * 6 + [vmem, vmem],
        out_specs=[vmem, vmem, hbm],
        out_shape=[
            jax.ShapeDtypeStruct((2, wide, 2, unit, *piece), bf16),
            jax.ShapeDtypeStruct((16, SPAN), f32),
            jax.ShapeDtypeStruct(tokens.shape, bf16),
        ],
        scratch_shapes=[
            pltpu.VMEM((wide, 2, unit, lines, 2, *piece), bf16),
            pltpu.VMEM((wide, 2, unit, lines, 2, *piece), bf16),
            pltpu.VMEM((wide, 2, unit, lines, 2, *piece), bf16),
            pltpu.VMEM((others, unit, lines, 2, *piece), bf16),
            pltpu.VMEM((wide, unit, lines, *piece), bf16),
            pltpu.VMEM((unit, lines, 2, *piece), bf16),
            pltpu.VMEM((wide, unit, lines, *piece), bf16),
            pltpu.VMEM((unit, lines, *piece), bf16),
            pltpu.VMEM((others, unit, lines, *piece), bf16),
            pltpu.VMEM((2, unit, lines, *piece), bf16),
            pltpu.VMEM((lines - 1, 2, unit, *piece), bf16),
            pltpu.VMEM((2, 16, SPAN), f32),
            pltpu.VMEM((wide, 16, SPAN), f32),
            pltpu.VMEM((2, 16, SPAN), f32),
            pltpu.VMEM((lines, 16, SPAN), f32),
            pltpu.SemaphoreType.DMA((copies,)),
            pltpu.SemaphoreType.DMA((copies,)),
            pltpu.SemaphoreType.DMA((small,)),
            pltpu.SemaphoreType.DMA((small,)),
            pltpu.SemaphoreType.DMA((2 * wide * unit,)),
            pltpu.SemaphoreType.DMA((2 * wide * unit,)),
            pltpu.SemaphoreType.DMA((2 * wide * unit,)),
            pltpu.VMEM((16, SPAN), f32),
            pltpu.VMEM((D, WIDE), bf16),
            pltpu.VMEM((48, D), f32),
            pltpu.VMEM((1, D), f32),
            pltpu.VMEM((8, D), f32),
            pltpu.VMEM((2, BLOCK, D), bf16),
            pltpu.VMEM((2, BLOCK, D), bf16),
            pltpu.VMEM((2, INNER, BLOCK), bf16),
            pltpu.VMEM((2, CHANNELS, BLOCK), bf16),
            pltpu.VMEM((2, 48, BLOCK), bf16),
            pltpu.VMEM((2, BLOCK, D), bf16),
            pltpu.SemaphoreType.DMA((2, 5)),
            pltpu.SemaphoreType.DMA((2,)),
            pltpu.SemaphoreType.DMA((1,)),
        ],
        compiler_params=pltpu.CompilerParams(
            collective_id=1, has_side_effects=True, vmem_limit_bytes=VMEM_LIMIT
        ),
        name="reduce",
    )(*halves, heads, tokens, cotangent, *parts, weight, time, vectors)


def finish_kernel(
    wide, summed_ref, heads_ref,
    wide_o, time_o, narrow_o, taps_o, offset_o, pre_o, post_o, bias_o, decay_o, skip_o, joined_s,
):
    unit, rows = summed_ref.shape[3:5]
    tiles_wide = wide_o.shape[1] // SPAN // 2
    tiles_narrow = narrow_o.shape[1] // SPAN

    def read(core, j):
        block, i = divmod(j, unit)
        return summed_ref[core, block // 2, block % 2, i].astype(f32)

    for core in range(2):
        for j in range(tiles_wide):
            column = (core * tiles_wide + j) * SPAN
            wide_o[:, column : column + SPAN] = read(core, j)
        for j in range(tiles_narrow):
            narrow_o[core * rows : (core + 1) * rows, j * SPAN : (j + 1) * SPAN] = read(
                core, tiles_wide + j
            )
    times = read(0, tiles_wide + tiles_narrow)
    for start in range(0, 2 * HEADS, rows):
        size = min(rows, 2 * HEADS - start)
        time_o[start : start + size, :] = times[:size, start : start + rows]
    vectors = read(1, tiles_wide + tiles_narrow)
    line = 0
    outs = [(taps_o, k) for k in range(CONV)] + [(offset_o, 0), (post_o, 0)]
    for out, k in outs:
        width = out.shape[1]
        for start in range(0, width, SPAN):
            size = min(SPAN, width - start)
            out[k : k + 1, start : start + size] = vectors[line : line + 1, :size]
            line += 1
    for k in range(D // SPAN):
        joined_s[:, k * SPAN : (k + 1) * SPAN] = heads_ref[8 + k : 9 + k, :]
    shard = lax.axis_index("shard")
    for s in range(D // rows):

        @pl.when(shard == s)
        def _(s=s):
            pre_o[...] = joined_s[:, s * rows : (s + 1) * rows]

    bias_o[...] = heads_ref[:1, : 2 * HEADS]
    decay_o[...] = heads_ref[1:2, :HEADS]
    skip_o[...] = heads_ref[2:3, :HEADS]


def finish(summed, heads, wide, rows, width):
    shapes = [
        (rows, WIDE), (2 * HEADS, rows), (2 * rows, D), (CONV, width), (1, width), (1, rows), (1, 2 * rows),
        (1, 2 * HEADS), (1, HEADS), (1, HEADS),
    ]
    return pl.pallas_call(
        partial(finish_kernel, wide),
        out_shape=[jax.ShapeDtypeStruct(shape, f32) for shape in shapes],
        scratch_shapes=[pltpu.VMEM((1, D), f32)],
        compiler_params=pltpu.CompilerParams(vmem_limit_bytes=VMEM_LIMIT),
        name="finish",
    )(summed, heads)


def gather_kernel(lines, large, kinds, *refs):
    ins, outs = refs[:kinds], refs[kinds : 2 * kinds]
    send_sem, recv_sem, own_sem, small_send, small_recv = refs[2 * kinds :]
    rep = lax.axis_index("rep")
    shard = lax.axis_index("shard")
    shards = 2 * lines
    core, x = lax.rem(rep, 2), lax.div(rep, 2)
    odd = lax.rem(x, 2)
    y, z = lax.rem(shard, 2), lax.div(shard, 2)
    sibling = peer(rep + 1 - 2 * core, shard)
    across = peer((x + 1 - 2 * odd) * 2 + core, shard)
    partner = peer(rep, shard + 1 - 2 * y)
    has_up, has_down = z < lines - 1, z > 0
    up = peer(rep, jnp.minimum(z + 1, lines - 1) * 2 + y)
    down = peer(rep, jnp.maximum(z - 1, 0) * 2 + y)
    away = [lax.rem(shard + k, shards) for k in range(1, shards)]
    greet([sibling, across, *[peer(rep, other) for other in away]])

    own = [
        pltpu.make_async_copy(src, dst.at[shard], own_sem.at[i])
        for i, (src, dst) in enumerate(zip(ins, outs))
    ]

    def place(group, part, ref, index, side):
        half = ref.shape[-1] // SPAN // 2
        thin = max(1, half * 5 // 13)
        thick = half - 2 * thin
        start = side * half
        if group:
            swap = odd if group == 1 else 1 - odd
            start = start + thick + swap * thin
        columns = pl.ds(pl.multiple_of(start * SPAN, SPAN), (thin if group else thick) * SPAN)
        return ref.at[:, columns] if index is None else ref.at[index, :, columns]

    def copies(way, group, index, device, mine=False, side=None, part=None):
        side = core if side is None else side
        return [
            remote(
                place(group, part, ins[part] if mine else outs[part], None if mine else index, side),
                place(group, part, outs[part], index, side),
                send_sem.at[way, group, part, index],
                recv_sem.at[way, 1 if way == 4 else group, part, index],
                device,
            )
            for part in (range(large) if part is None else (part,))
        ]

    def start(*args, **kw):
        for copy in copies(*args, **kw):
            copy.start()

    def arrive(*args, **kw):
        for copy in copies(*args, **kw):
            copy.wait_recv()

    def sent(*args, **kw):
        for copy in copies(*args, **kw):
            copy.wait_send()

    other = shard + 1 - 2 * y

    def index_of(line, side):
        return line * 2 + side

    for group in (1, 0):
        pl.when(has_up)(lambda group=group: start(1, group, shard, up, mine=True))
        pl.when(has_down)(lambda group=group: start(2, group, shard, down, mine=True))
        start(0, group, shard, partner, mine=True)
    for copy in own:
        copy.start()
    small = []
    for k, index in enumerate(away):
        for part in range(large, kinds):
            copy = remote(
                ins[part], outs[part].at[shard], small_send.at[part - large, k], small_recv.at[part - large, k],
                peer(rep, index),
            )
            copy.start()
            small.append(copy)

    def line_step(k, group, part):
        def spread(index):
            start(0, group, index, partner, part=part)
            if group == 1:
                start(4, 1, index, across, part=part)
            start(3, group, index, sibling, part=part)

        def from_below():
            index = index_of(z - k, y)
            arrive(1, group, index, down, part=part)
            pl.when(has_up)(lambda: start(1, group, index, up, part=part))
            spread(index)

        def from_above():
            index = index_of(z + k, y)
            arrive(2, group, index, up, part=part)
            pl.when(has_down)(lambda: start(2, group, index, down, part=part))
            spread(index)

        pl.when(z - k >= 0)(from_below)
        pl.when(z + k < lines)(from_above)

    def take(group, part, index):
        arrive(0, group, index, partner, part=part)
        if group == 1:
            start(4, 1, index, across, part=part)
        start(3, group, index, sibling, part=part)

    def cross(part, index):
        arrive(4, 2, index, across, part=part)
        start(3, 2, index, sibling, part=part)

    def either(k, action, side):
        pl.when(z - k >= 0)(lambda: action(index_of(z - k, side)))
        if k:
            pl.when(z + k < lines)(lambda: action(index_of(z + k, side)))

    pieces = [(group, part) for group in (1, 0) for part in range(large)]
    for group, part in pieces:
        take(group, part, other)
    for k in range(1, lines):
        for group, part in pieces:
            line_step(k, group, part)
        if k > 1:
            for group, part in pieces:
                either(k - 1, partial(take, group, part), 1 - y)
    for group, part in pieces:
        either(lines - 1, partial(take, group, part), 1 - y)
    for part in range(large):
        either(0, partial(cross, part), 1 - y)
    for k in range(1, lines):
        for part in range(large):
            either(k, partial(cross, part), y)
            either(k, partial(cross, part), 1 - y)
    for index in range(shards):

        @pl.when(index != shard)
        def _(index=index):
            for group in range(3):
                arrive(3, group, index, sibling, side=1 - core)
                sent(3, group, index, sibling)
            sent(4, 1, index, across)

    for line in range(lines):
        for group in range(2):
            index = index_of(line, y)
            sent(0, group, index, partner)

            @pl.when((line <= z) & has_up)
            def _(group=group, index=index):
                sent(1, group, index, up)

            @pl.when((line >= z) & has_down)
            def _(group=group, index=index):
                sent(2, group, index, down)

    for copy in own:
        copy.wait()
    for copy in small:
        copy.wait_send()
    for k in range(1, shards):
        index = lax.rem(shard + shards - k, shards)
        for part in range(large, kinds):
            remote(
                ins[part], outs[part].at[index], small_send.at[part - large, k - 1],
                small_recv.at[part - large, k - 1], peer(rep, index),
            ).wait_recv()


def gather_weights(arrays, large, lines):
    shards = 2 * lines
    hbm = pl.BlockSpec(memory_space=pl.ANY)
    kinds = len(arrays)
    return pl.pallas_call(
        partial(gather_kernel, lines, large, kinds),
        in_specs=[hbm] * kinds,
        out_specs=[hbm] * kinds,
        out_shape=[jax.ShapeDtypeStruct((shards, *a.shape), a.dtype) for a in arrays],
        scratch_shapes=[
            pltpu.SemaphoreType.DMA((5, 3, large, shards)),
            pltpu.SemaphoreType.DMA((5, 3, large, shards)),
            pltpu.SemaphoreType.DMA((kinds,)),
            pltpu.SemaphoreType.DMA((kinds - large, shards - 1)),
            pltpu.SemaphoreType.DMA((kinds - large, shards - 1)),
        ],
        compiler_params=pltpu.CompilerParams(collective_id=0, has_side_effects=True),
        name="gather",
    )(*arrays)


def local(
    tokens,
    cotangent,
    lengths,
    widen_weight,
    timestep_weight,
    narrow_weight,
    filter_weight,
    filter_offset,
    prenorm_gain,
    postnorm_gain,
    timestep_bias,
    decay_log,
    skip_gain,
):
    lines = lax.axis_size("shard") // 2
    wide = lax.axis_size("rep") // 2
    rows = widen_weight.shape[0]
    width = filter_weight.shape[1]
    own = jnp.concatenate(
        [filter_weight.reshape(-1), filter_offset, prenorm_gain, postnorm_gain]
    )
    widen, narrow, timestep, vectors = gather_weights(
        [widen_weight, narrow_weight, timestep_weight.T, own[None]], 2, lines
    )
    widen = widen.reshape(D, WIDE)
    result, parts, wide_grad, narrow_grad, small_grad, heads = layer(
        tokens, cotangent, lengths, widen, timestep, narrow.reshape(INNER, D),
        vectors, timestep_bias, decay_log, skip_gain,
    )
    summed, heads, slope = reduce_units(
        wide_grad, narrow_grad, small_grad, heads, tokens, cotangent, parts, widen, timestep, vectors, wide, lines
    )
    (
        widen_out, timestep_out, narrow_out, filter_out, offset_out, prenorm_out, postnorm_out,
        bias_out, decay_out, skip_out,
    ) = finish(summed, heads, wide, rows, width)
    return (
        result, slope, widen_out, timestep_out.T, narrow_out, filter_out,
        *[row.reshape(-1) for row in (offset_out, prenorm_out, postnorm_out, bias_out, decay_out, skip_out)],
    )


def solution(mesh):
    placed = (
        P(("rep", "shard"), None, None),
        P(("rep", "shard"), None, None),
        P(("rep", "shard")),
        P("shard", None),
        P("shard", None),
        P("shard", None),
        P(None, "shard"),
        P("shard"),
        P("shard"),
        P("shard"),
        P(),
        P(),
        P(),
    )
    return jax.shard_map(
        local,
        mesh=mesh,
        in_specs=placed,
        out_specs=(
            P(("rep", "shard"), None, None),
            P(("rep", "shard"), None, None),
            P("shard", None),
            P("shard", None),
            P("shard", None),
            P(None, "shard"),
            P("shard"),
            P("shard"),
            P("shard"),
            P(),
            P(),
            P(),
        ),
        check_vma=False,
    )
```

```python
from functools import partial

import jax
import jax.numpy as jnp
from jax import lax
from jax.experimental import pallas as pl
from jax.experimental.pallas import tpu as pltpu
from jax.sharding import PartitionSpec as P

HEADS = 24
HEADDIM = 64
STATE = 64
CONV = 4
INNER = 1536
CHANNELS = 1792
D = 768
WIDE = INNER + CHANNELS
SPAN = 128
BLOCK = 256
SUBS = BLOCK // SPAN
EPS = 1e-05
LOG2E = 1.4426950408889634
TINY = 1.2e-38
f32 = jnp.float32
bf16 = jnp.bfloat16
precise = lax.Precision.HIGHEST
VMEM_LIMIT = 60 * 1024 * 1024


def mm(a, b, precision=None):
    return lax.dot_general(
        a, b, (((1,), (0,)), ((), ())), precision=precision, preferred_element_type=f32
    )


def mm_nt(a, b):
    return lax.dot_general(a, b, (((1,), (1,)), ((), ())), preferred_element_type=f32)


def mm_tn(a, b):
    return lax.dot_general(a, b, (((0,), (0,)), ((), ())), preferred_element_type=f32)


def mm_tn_precise(a, b):
    return lax.dot_general(
        a, b, (((0,), (0,)), ((), ())), precision=precise, preferred_element_type=f32
    )


def sigmoid(v):
    return 0.5 * jnp.tanh(0.5 * v) + 0.5


def iotas(shape):
    return (
        lax.broadcasted_iota(jnp.int32, shape, 0),
        lax.broadcasted_iota(jnp.int32, shape, 1),
    )


def column(row, lanes=SPAN):
    return mm_tn_precise(row, jnp.ones((1, lanes), f32))


def rate_columns(decay_ref):
    half = column(-jnp.exp(decay_ref[...]) * LOG2E)
    return jnp.concatenate([half, half], axis=0)


def vector_parts(vectors_ref):
    shards = vectors_ref.shape[0]
    sizes = [CHANNELS // shards] * (CONV + 1) + [D // shards, INNER // shards]
    starts = [sum(sizes[:i]) for i in range(len(sizes))]
    return [slice(start, start + size) for start, size in zip(starts, sizes)]


def spread_vectors(out_s, vectors_ref, which):
    part = vector_parts(vectors_ref)[which]
    width = part.stop - part.start
    for s in range(vectors_ref.shape[0]):
        out_s[s * width : (s + 1) * width, :] = mm_tn(
            vectors_ref[s, :, part], jnp.ones((1, SPAN), bf16)
        )


def join_row(row_s, vectors_ref, which):
    part = vector_parts(vectors_ref)[which]
    width = part.stop - part.start
    for s in range(vectors_ref.shape[0]):
        row_s[:, s * width : (s + 1) * width] = vectors_ref[s, :, part].astype(f32)


def split_rows(value):
    high = value.astype(bf16)
    rest = value - high.astype(f32)
    middle = rest.astype(bf16)
    low = (rest - middle.astype(f32)).astype(bf16)
    return jnp.concatenate([high, middle, low], axis=0)


def exact_mm(value, ones):
    m = value.shape[0]
    parts = mm(split_rows(value), ones)
    return (parts[2 * m :] + parts[m : 2 * m]) + parts[:m]


def span_matrix(compare):
    rows, cols = iotas((BLOCK, BLOCK))
    return (compare(rows, cols) & (rows // SPAN == cols // SPAN)).astype(bf16)


def lane_sums(value):
    m = value.shape[0]
    parts = mm_nt(jnp.ones((8, value.shape[1]), bf16), split_rows(value))[:1]
    return (parts[:, 2 * m :] + parts[:, m : 2 * m]) + parts[:, :m]


def enter_kernel(
    len_ref,
    tok_ref,
    wide_ref,
    time_ref,
    vectors_ref,
    bias_ref,
    decay_ref,
    gate_o,
    fin_o,
    filt_o,
    act_o,
    rows_o,
    cols_o,
    state_o,
    last_s,
    run_s,
    taps_s,
    wide_s,
    time_s,
    pre_s,
    rate_s,
    bias_s,
    until_s,
    from_s,
):
    seq = pl.program_id(0)
    block = pl.program_id(1)
    length = len_ref[seq]

    @pl.when((seq == 0) & (block == 0))
    def _():
        for k in range(CONV + 1):
            spread_vectors(taps_s.at[k], vectors_ref, k)
        join_row(pre_s, vectors_ref, CONV + 1)
        rate_s[...] = rate_columns(decay_ref)
        until_s[...] = span_matrix(lambda r, c: r <= c)
        from_s[...] = span_matrix(lambda r, c: r >= c)
        bias_s[...] = column(bias_ref[...], BLOCK)
        shards, _, width = time_ref.shape
        for s in range(shards):
            time_s[:, s * width : (s + 1) * width] = time_ref[s].astype(f32)
        for i in range(WIDE // 256):
            wide_s[i * 256 : (i + 1) * 256, :] = wide_ref[:, i * 256 : (i + 1) * 256].T

    @pl.when(block == 0)
    def _():
        last_s[...] = jnp.zeros_like(last_s)
        run_s[...] = jnp.zeros_like(run_s)

    @pl.when(block * BLOCK < length)
    def _():
        tok = tok_ref[0].astype(f32)
        scale = lax.rsqrt(jnp.mean(tok * tok, axis=-1, keepdims=True) + EPS)
        normed = (tok * scale * pre_s[...]).astype(bf16)
        x = mm_nt(time_s[...].astype(bf16), normed) + bias_s[...]
        steps = jnp.maximum(x, 0.0) + jnp.log1p(jnp.exp(-jnp.abs(x)))
        scaled = steps * rate_s[:, :1]
        fcum = exact_mm(scaled[:HEADS], until_s[...])
        rcum = exact_mm(scaled[HEADS:], from_s[...])
        least = jnp.log2(jnp.maximum(steps, TINY))
        cums = jnp.concatenate([fcum, rcum], axis=0)
        blank = jnp.zeros((SPAN - 48, BLOCK), f32)
        cols_o[0] = jnp.concatenate([cums - least, blank], axis=0).T
        rows_o[0, :48, :] = x
        rows_o[0, 48:96, :] = steps
        rows_o[0, 96:144, :] = cums
        rows_o[0, 144:192, :] = jnp.exp2(cums)
        for sub in range(SUBS):
            part = slice(sub * SPAN, (sub + 1) * SPAN)
            last = (sub + 1) * SPAN - 1
            rows_o[0, 192:216, part] = jnp.exp2(fcum[:, last : last + 1] - fcum[:, part]) * steps[:HEADS, part]
            first = sub * SPAN
            rows_o[0, 216:240, part] = jnp.exp2(rcum[:, first : first + 1] - rcum[:, part]) * steps[HEADS:, part]
        place = block * BLOCK + lax.broadcasted_iota(jnp.int32, (1, BLOCK), 1)
        mask = (place < length).astype(f32)

        def project(i):
            fin_o[0, i * 256 : (i + 1) * 256, :] = mm_nt(
                wide_s[INNER + i * 256 : INNER + (i + 1) * 256, :], normed
            ).astype(bf16)

        def filter_rows(i):
            r = slice(i * 32, (i + 1) * 32)
            now = fin_o[0, r, :]
            w = jnp.concatenate([last_s[r, :], now], axis=1)
            last_s[r, :] = now[:, SPAN:]
            twice = lambda k: jnp.concatenate([taps_s[k, r, :]] * 2, axis=1)
            acc = twice(4) + twice(3) * now.astype(f32)
            for lag in range(1, CONV):
                moved = pltpu.roll(w, lag, 1)[:, SPAN:].astype(f32)
                acc = acc + twice(3 - lag) * moved
            filt_o[0, r, :] = acc.astype(bf16)
            act = acc * sigmoid(acc)
            if i < INNER // 32:
                act = act * mask
            act_o[0, r, :] = act.astype(bf16)

        for i in range(CHANNELS // 256):
            project(i)
            if i:
                for j in range(8):
                    filter_rows((i - 1) * 8 + j)
        for i in range(INNER // 256):
            gate_o[0, i * 256 : (i + 1) * 256, :] = mm_nt(
                wide_s[i * 256 : (i + 1) * 256, :], normed
            ).astype(bf16)
            if i == 0:
                for j in range(8):
                    filter_rows((CHANNELS // 256 - 1) * 8 + j)

        lane = lax.broadcasted_iota(jnp.int32, (1, SPAN), 1)

        for sub in range(SUBS):
            cols = slice(sub * SPAN, (sub + 1) * SPAN)
            tail_f = rows_o[0, 192:216, cols]
            tail_r = rows_o[0, 216:240, cols]
            decay = rows_o[0, 144:168, (sub + 1) * SPAN - 1 : (sub + 1) * SPAN]
            ins_f = act_o[0, INNER : INNER + 64, cols].astype(f32)
            ins_r = act_o[0, INNER + 128 : INNER + 192, cols].astype(f32)
            for h in range(HEADS):
                rows = slice(h * 64, (h + 1) * 64)
                weighted = jnp.concatenate(
                    [
                        (ins_f * tail_f[h : h + 1]).astype(bf16),
                        (ins_r * tail_r[h : h + 1]).astype(bf16),
                    ],
                    axis=0,
                )
                fresh = mm_nt(act_o[0, rows, cols], weighted)
                run = run_s[rows, :]
                state_o[0, sub, rows, :] = jnp.where(lane < 64, run, fresh).astype(bf16)
                run_s[rows, :] = run * decay[h : h + 1] + fresh


def middle_kernel(
    len_ref,
    skip_ref,
    tok_ref,
    cot_ref,
    gate_ref,
    act_ref,
    rows_ref,
    cols_ref,
    state_ref,
    narrow_ref,
    post_ref,
    result_o,
    dgate_o,
    dval_o,
    dio_o,
    sums_o,
    dstate_o,
    rstate_o,
    narrow_o,
    post_o,
    skip_o,
    run_s,
    grun_s,
    ahead_s,
    behind_s,
    gated_s,
    dgn_s,
    spread_s,
    matrix_s,
    held_s,
    slope_s,
    norm_s,
    gain_s,
    narrow_s,
    post_s,
):
    seq = pl.program_id(0)
    step = pl.program_id(1)
    block = pl.num_programs(1) - 1 - step
    length = len_ref[seq]

    @pl.when((seq == 0) & (step == 0))
    def _():
        narrow_s[...] = jnp.zeros_like(narrow_s)
        post_s[...] = jnp.zeros_like(post_s)
        skip_o[...] = jnp.zeros_like(skip_o)
        spread_vectors(gain_s, post_ref, CONV + 2)

    @pl.when(step == 0)
    def _():
        run_s[...] = jnp.zeros_like(run_s)
        grun_s[...] = jnp.zeros_like(grun_s)

    @pl.when(block * BLOCK >= length)
    def _():
        result_o[...] = tok_ref[...]
        dgate_o[...] = jnp.zeros_like(dgate_o)

    @pl.when(block * BLOCK < length)
    def _():
        rows_i, cols_i = iotas((SPAN, SPAN))
        lower = rows_i < cols_i
        upper = rows_i > cols_i
        lane = lax.broadcasted_iota(jnp.int32, (1, SPAN), 1)
        place = block * BLOCK + lax.broadcasted_iota(jnp.int32, (BLOCK, 1), 0)
        inside = place < length
        slope_s[...] = jnp.where(inside, cot_ref[0].astype(f32), 0.0).astype(bf16)
        dgn_s[...] = mm_nt(narrow_ref[...], slope_s[...])
        zero = jnp.zeros((64, SPAN), bf16)

        def span_scores(cols):
            fi = act_ref[0, INNER : INNER + 64, cols]
            fo = act_ref[0, INNER + 64 : INNER + 128, cols]
            ri = act_ref[0, INNER + 128 : INNER + 192, cols]
            ro = act_ref[0, INNER + 192 : INNER + 256, cols]
            return fi, fo, ri, ro

        def fold(value):
            return jnp.sum(value.reshape(8, 8, SPAN), axis=0)

        def forward_span(sub):
            cols = slice(sub * SPAN, (sub + 1) * SPAN)
            fcum = rows_ref[0, 96:120, cols]
            rcum = rows_ref[0, 120:144, cols]
            columns = cols_ref[0, cols, :]
            out_f = rows_ref[0, 144:168, cols]
            out_r = rows_ref[0, 168:192, cols]
            decay = rows_ref[0, 168:192, sub * SPAN : sub * SPAN + 1]
            fi, fo, ri, ro = span_scores(cols)
            ahead_scores = jnp.where(lower, mm_tn(fi, fo), 0.0)
            behind_scores = jnp.where(upper, mm_tn(ri, ro), 0.0)
            fo = fo.astype(f32)
            ro = ro.astype(f32)
            squares = jnp.zeros((8, SPAN), f32)
            dots = jnp.zeros((8, SPAN), f32)
            for h in range(HEADS):
                rows = slice(h * 64, (h + 1) * 64)
                power = jnp.where(
                    lower,
                    fcum[h : h + 1] - columns[:, h : h + 1],
                    rcum[h : h + 1] - columns[:, HEADS + h : HEADS + h + 1],
                )
                spread = jnp.exp2(power)
                spread_s[sub, h] = spread.astype(bf16)
                low = (spread * ahead_scores).astype(bf16)
                high = (spread * behind_scores).astype(bf16)
                out_low = (fo * out_f[h : h + 1]).astype(bf16)
                out_high = (ro * out_r[h : h + 1]).astype(bf16)
                matrix_s[sub, h, :SPAN] = low
                matrix_s[sub, h, SPAN : 2 * SPAN] = high
                matrix_s[sub, h, 2 * SPAN : 2 * SPAN + 64] = out_low
                matrix_s[sub, h, 2 * SPAN + 64 :] = out_high
                matrix = jnp.concatenate(
                    [
                        jnp.concatenate([low, out_low, zero], axis=0),
                        jnp.concatenate([high, zero, out_high], axis=0),
                    ],
                    axis=1,
                )
                state = state_ref[0, sub, rows, :].astype(f32)
                run = run_s[rows, :]
                rstate_o[0, sub, rows, :] = run.astype(bf16)
                held = jnp.where(lane < 64, state, run).astype(bf16)
                held_s[sub, rows, :] = held
                run_s[rows, :] = run * decay[h : h + 1] + state
                values = act_ref[0, rows, cols]
                pair = mm(jnp.concatenate([values, held], axis=1), matrix)
                ahead = pair[:, :SPAN]
                behind = pair[:, SPAN:]
                ahead_s[rows, cols] = ahead
                behind_s[rows, cols] = behind
                mixed = ahead + behind + skip_ref[h] * values.astype(f32)
                gate = gate_ref[0, rows, cols].astype(f32)
                gated = mixed * (gate * sigmoid(gate))
                gated_s[rows, cols] = gated
                squares = squares + fold(gated * gated)
                dots = dots + fold(gated * gain_s[rows, :] * dgn_s[rows, cols])
            rs = lax.rsqrt(jnp.sum(squares, axis=0, keepdims=True) * (1.0 / INNER) + EPS)
            pull = rs * rs * rs * (jnp.sum(dots, axis=0, keepdims=True) * (1.0 / INNER))
            norm_s[:1, cols] = rs
            norm_s[1:2, cols] = pull

        for sub in reversed(range(SUBS)):
            forward_span(sub)
        rs = norm_s[:1, :]

        def norm_rows(i, _):
            r = pl.ds(pl.multiple_of(i * 32, 32), 32)
            kept = gated_s[r, :] * rs
            gain = gain_s[r, :]
            dgate_o[0, r, :] = (kept * jnp.concatenate([gain, gain], axis=1)).astype(bf16)
            product = kept * dgn_s[r, :]
            post_s[r, :] += product[:, :SPAN] + product[:, SPAN:]
            return None

        lax.fori_loop(0, INNER // 32, norm_rows, None, unroll=8)
        gnormed = dgate_o[0]
        branch = mm_tn(narrow_ref[...], gnormed).T
        result_o[0] = (tok_ref[0].astype(f32) + jnp.where(inside, branch, 0.0)).astype(bf16)
        narrow_s[...] += mm(gnormed, slope_s[...])

        def backward_span(sub):
            cols = slice(sub * SPAN, (sub + 1) * SPAN)
            out_f = rows_ref[0, 144:168, cols]
            out_r = rows_ref[0, 168:192, cols]
            decay = rows_ref[0, 144:168, (sub + 1) * SPAN - 1 : (sub + 1) * SPAN]
            fi, fo, ri, ro = span_scores(cols)
            rs = norm_s[:1, cols]
            pull = norm_s[1:2, cols]
            dscores = jnp.zeros((SPAN, SPAN), f32)
            dfo = jnp.zeros((64, SPAN), f32)
            dro = jnp.zeros((64, SPAN), f32)

            def down(value):
                return jnp.sum(value, axis=0, keepdims=True)

            for h in range(HEADS):
                rows = slice(h * 64, (h + 1) * 64)
                gate = gate_ref[0, rows, cols].astype(f32)
                sig = sigmoid(gate)
                values = act_ref[0, rows, cols]
                values32 = values.astype(f32)
                ahead = ahead_s[rows, cols]
                behind = behind_s[rows, cols]
                mixed = ahead + behind + skip_ref[h] * values32
                dgated = rs * (gain_s[rows, :] * dgn_s[rows, cols]) - gated_s[rows, cols] * pull
                dmixed = dgated * (gate * sig)
                dgate = dgated * mixed * (sig * (1.0 + gate * (1.0 - sig)))
                dgate_o[0, rows, cols] = dgate.astype(bf16)
                skip_o[h : h + 1, :] += down(dmixed * values32)
                dm = dmixed.astype(bf16)
                dm32 = dm.astype(f32)
                held = held_s[sub, rows, :]
                grad = mm_tn(jnp.concatenate([values, held], axis=1), dm)
                dscores = dscores + grad[:SPAN] * spread_s[sub, h].astype(f32)
                dfo = dfo + grad[SPAN : SPAN + 64] * out_f[h : h + 1]
                dro = dro + grad[SPAN + 64 :] * out_r[h : h + 1]
                dall = mm_nt(dm, matrix_s[sub, h])
                dlow = dall[:, :SPAN]
                dhigh = dall[:, SPAN : 2 * SPAN]
                dheld = dall[:, 2 * SPAN :]
                dval_o[0, rows, cols] = (dlow + dhigh + skip_ref[h] * dmixed).astype(bf16)
                run = grun_s[rows, :]
                dstate_o[0, sub, rows, :] = jnp.where(lane < 64, run, dheld).astype(bf16)
                grun_s[rows, :] = run * decay[h : h + 1] + dheld
                sums_o[0, h : h + 1, cols] = down(dm32 * ahead)
                sums_o[0, HEADS + h : HEADS + h + 1, cols] = down(dm32 * behind)
                sums_o[0, 2 * HEADS + h : 2 * HEADS + h + 1, cols] = down(values32 * dlow)
                sums_o[0, 3 * HEADS + h : 3 * HEADS + h + 1, cols] = down(values32 * dhigh)
                sums_o[0, 4 * HEADS + h : 4 * HEADS + h + 1, cols] = decay[h : h + 1] * down(
                    jnp.where(lane < 64, run * held.astype(f32), 0.0)
                )
            low = jnp.where(lower, dscores, 0.0).astype(bf16)
            high = jnp.where(upper, dscores, 0.0).astype(bf16)
            dio_o[0, 0:64, cols] = mm_nt(fo, low)
            dio_o[0, 64:128, cols] = dfo + mm(fi, low)
            dio_o[0, 128:192, cols] = mm_nt(ro, high)
            dio_o[0, 192:256, cols] = dro + mm(ri, high)

        for sub in reversed(range(SUBS)):
            backward_span(sub)

    @pl.when((seq == pl.num_programs(0) - 1) & (step == pl.num_programs(1) - 1))
    def _():
        post_o[...] = lane_sums(post_s[...])
        halves, shards, rows = narrow_o.shape[0] * SPAN // D, *narrow_o.shape[1:3]
        for unit in range(narrow_o.shape[0]):
            half, tile = divmod(unit, D // SPAN)
            for s in range(shards):
                start = (s * halves + half) * rows
                narrow_o[unit, s] = narrow_s[
                    start : start + rows, tile * SPAN : (tile + 1) * SPAN
                ].astype(bf16)


def leave_kernel(
    len_ref,
    filt_ref,
    act_ref,
    fin_ref,
    rows_ref,
    dval_ref,
    dio_ref,
    sums_ref,
    dstate_ref,
    rstate_ref,
    decay_ref,
    skip_ref,
    dfilt_o,
    draw_o,
    lines_o,
    heads_o,
    grun_s,
    near_s,
    dact_s,
    last_s,
    offset_s,
    taps_s,
    bias_s,
    decay_s,
    rate_s,
    ends_s,
    ahead_s,
    behind_s,
):
    seq = pl.program_id(0)
    block = pl.program_id(1)
    length = len_ref[seq]

    @pl.when((seq == 0) & (block == 0))
    def _():
        offset_s[...] = jnp.zeros_like(offset_s)
        taps_s[...] = jnp.zeros_like(taps_s)
        bias_s[...] = jnp.zeros_like(bias_s)
        decay_s[...] = jnp.zeros_like(decay_s)
        rate_s[...] = rate_columns(decay_ref) * (1.0 / LOG2E)
        same = span_matrix(lambda r, c: r == r)
        ahead_s[:BLOCK] = span_matrix(lambda r, c: r >= c)
        ahead_s[BLOCK : 2 * BLOCK] = span_matrix(lambda r, c: r < c)
        ahead_s[2 * BLOCK :] = same
        behind_s[:BLOCK] = span_matrix(lambda r, c: r <= c)
        behind_s[BLOCK : 2 * BLOCK] = span_matrix(lambda r, c: r > c)
        behind_s[2 * BLOCK :] = same

    @pl.when(block == 0)
    def _():
        grun_s[...] = jnp.zeros_like(grun_s)
        last_s[...] = jnp.zeros_like(last_s)

    @pl.when(block * BLOCK >= length)
    def _():
        draw_o[...] = jnp.zeros_like(draw_o)

    @pl.when(block * BLOCK < length)
    def _():
        lane = lax.broadcasted_iota(jnp.int32, (1, SPAN), 1)

        place = block * BLOCK + lax.broadcasted_iota(jnp.int32, (1, BLOCK), 1)
        mask = (place < length).astype(f32)

        def filter_rows(i):
            r = slice(i * 32, (i + 1) * 32)
            filt = filt_ref[0, r, :].astype(f32)
            sig = sigmoid(filt)
            dact = dact_s[r, :]
            if i < INNER // 32:
                dact = dact * mask
            dfilt = dact * (sig * (1.0 + filt * (1.0 - sig)))
            dfilt_o[0, r, :] = dfilt.astype(bf16)
            offset_s[r, :] += dfilt[:, :SPAN] + dfilt[:, SPAN:]
            fin = fin_ref[0, r, :]
            w = jnp.concatenate([last_s[r, :], fin], axis=1)
            last_s[r, :] = fin[:, SPAN:]
            product = dfilt * fin.astype(f32)
            taps_s[3, r, :] += product[:, :SPAN] + product[:, SPAN:]
            for lag in range(1, CONV):
                product = dfilt * pltpu.roll(w, lag, 1)[:, SPAN:].astype(f32)
                taps_s[3 - lag, r, :] += product[:, :SPAN] + product[:, SPAN:]

        def span(sub):
            cols = slice(sub * SPAN, (sub + 1) * SPAN)
            tail_f = rows_ref[0, 192:216, cols]
            tail_r = rows_ref[0, 216:240, cols]
            decay = rows_ref[0, 168:192, sub * SPAN : sub * SPAN + 1]
            fi = act_ref[0, INNER : INNER + 64, cols].astype(f32)
            ri = act_ref[0, INNER + 128 : INNER + 192, cols].astype(f32)
            dfi = jnp.zeros((64, SPAN), f32)
            dri = jnp.zeros((64, SPAN), f32)
            for h in range(HEADS):
                rows = slice(h * 64, (h + 1) * 64)
                weighted = jnp.concatenate(
                    [
                        (fi * tail_f[h : h + 1]).astype(bf16),
                        (ri * tail_r[h : h + 1]).astype(bf16),
                    ],
                    axis=0,
                )
                dstate = dstate_ref[0, sub, rows, :].astype(f32)
                run = grun_s[rows, :]
                dfresh = jnp.where(lane < 64, dstate, run).astype(bf16)
                near_s[h : h + 1, cols] = decay[h : h + 1] * jnp.sum(
                    jnp.where(lane < 64, 0.0, run * rstate_ref[0, sub, rows, :].astype(f32)),
                    axis=0,
                    keepdims=True,
                )
                grun_s[rows, :] = run * decay[h : h + 1] + dstate
                values = act_ref[0, rows, cols]
                dact_s[rows, cols] = dval_ref[0, rows, cols].astype(f32) + mm(dfresh, weighted)
                dweighted = mm_tn(dfresh, values)
                part_f = dweighted[:64] * tail_f[h : h + 1]
                part_r = dweighted[64:] * tail_r[h : h + 1]
                dfi = dfi + part_f
                dri = dri + part_r
                ends_s[h : h + 1, cols] = jnp.sum(part_f * fi, axis=0, keepdims=True)
                ends_s[HEADS + h : HEADS + h + 1, cols] = jnp.sum(
                    part_r * ri, axis=0, keepdims=True
                )
                if sub == SUBS - 1:
                    filter_rows(2 * h)
                    filter_rows(2 * h + 1)
            dact_s[INNER : INNER + 64, cols] = dio_ref[0, 0:64, cols] + dfi
            dact_s[INNER + 64 : INNER + 128, cols] = dio_ref[0, 64:128, cols]
            dact_s[INNER + 128 : INNER + 192, cols] = dio_ref[0, 128:192, cols] + dri
            dact_s[INNER + 192 : INNER + 256, cols] = dio_ref[0, 192:256, cols]

        for sub in range(SUBS):
            span(sub)
        for i in range(INNER // 32, CHANNELS // 32):
            filter_rows(i)
        col_f = sums_ref[0, 2 * HEADS : 3 * HEADS, :]
        col_r = sums_ref[0, 3 * HEADS : 4 * HEADS, :]
        ends_f = ends_s[:HEADS, :]
        ends_r = ends_s[HEADS:, :]
        dfa = exact_mm(
            jnp.concatenate(
                [sums_ref[0, :HEADS, :] - col_f, ends_f, sums_ref[0, 4 * HEADS :, :]], axis=1
            ),
            ahead_s[...],
        )
        dra = exact_mm(
            jnp.concatenate(
                [sums_ref[0, HEADS : 2 * HEADS, :] - col_r, ends_r, near_s[...]], axis=1
            ),
            behind_s[...],
        )
        sig = jax.nn.sigmoid(rows_ref[0, :48, :])
        steps = rows_ref[0, 48:96, :]
        rate = rate_s[:, :1]
        share = sig / jnp.maximum(steps, TINY)
        passed = jnp.concatenate([dfa, dra], axis=0) * rate
        draw = jnp.concatenate([col_f + ends_f, col_r + ends_r], axis=0) * share + passed * sig
        draw_o[0] = draw.astype(bf16)
        bias_s[...] += draw[:, :SPAN] + draw[:, SPAN:]
        product = passed * steps
        decay_s[...] += product[:, :SPAN] + product[:, SPAN:]
    @pl.when((seq == pl.num_programs(0) - 1) & (block == pl.num_programs(1) - 1))
    def _():
        lines_o[...] = jnp.zeros_like(lines_o)
        heads_o[...] = jnp.zeros_like(heads_o)
        for k in range(CONV):
            lines_o[k : k + 1, :] = lane_sums(taps_s[k])
        lines_o[CONV : CONV + 1, :] = lane_sums(offset_s[...])
        heads_o[:1, : 2 * HEADS] = lane_sums(bias_s[...])
        heads_o[1:2, :HEADS] = lane_sums(decay_s[:HEADS] + decay_s[HEADS:])
        heads_o[2:3, :HEADS] = lane_sums(skip_ref[...])


def widen_kernel(
    len_ref,
    tok_ref,
    dgate_ref,
    dfilt_ref,
    next_ref,
    draw_ref,
    vectors_ref,
    lines_ref,
    post_ref,
    dfin_o,
    wide_o,
    small_o,
    taps_s,
    wide_s,
    time_s,
    pre_s,
    lines_s,
):
    seq = pl.program_id(0)
    block = pl.program_id(1)
    length = len_ref[seq]

    @pl.when((seq == 0) & (block == 0))
    def _():
        wide_s[...] = jnp.zeros_like(wide_s)
        time_s[...] = jnp.zeros_like(time_s)
        for k in range(CONV):
            spread_vectors(taps_s.at[k], vectors_ref, k)
        join_row(pre_s, vectors_ref, CONV + 1)

    @pl.when(block * BLOCK >= length)
    def _():
        dfin_o[...] = jnp.zeros_like(dfin_o)

    @pl.when(block * BLOCK < length)
    def _():
        tok = tok_ref[0].astype(f32)
        scale = lax.rsqrt(jnp.mean(tok * tok, axis=-1, keepdims=True) + EPS)
        normed = (tok * scale * pre_s[...]).astype(bf16)
        normed_t = normed.T
        beyond = (block + 1) * BLOCK < length

        def filter_rows(i):
            r = slice(i * 32, (i + 1) * 32)
            following = jnp.where(beyond, next_ref[0, r, :].astype(f32), 0.0).astype(bf16)
            now = dfilt_ref[0, r, :]
            w = jnp.concatenate([now, following], axis=1)
            twice = lambda k: jnp.concatenate([taps_s[k, r, :]] * 2, axis=1)
            acc = twice(3) * now.astype(f32)
            for lag in range(1, CONV):
                moved = pltpu.roll(w, BLOCK + SPAN - lag, 1)[:, :BLOCK].astype(f32)
                acc = acc + twice(3 - lag) * moved
            dfin_o[0, r, :] = acc.astype(bf16)

        groups = CHANNELS // 32
        done = 0
        for i in range(WIDE // 256):
            rows = slice(i * 256, (i + 1) * 256)
            if i < INNER // 256:
                right = dgate_ref[0, rows, :]
            else:
                right = dfin_o[0, i * 256 - INNER : (i + 1) * 256 - INNER, :]
            wide_s[:, rows] += mm_nt(normed_t, right)
            upto = min(groups, -(-groups * (i + 1) // (INNER // 256)))
            for j in range(done, upto):
                filter_rows(j)
            done = upto
        draw = draw_ref[0]
        time_s[...] += mm(draw, normed)

    @pl.when((seq == pl.num_programs(0) - 1) & (block == pl.num_programs(1) - 1))
    def _():
        tiles, shards, rows = wide_o.shape[:3]
        for s in range(shards):
            own = slice(s * rows, (s + 1) * rows)
            for unit in range(tiles):
                wide_o[unit, s] = wide_s[own, unit * SPAN : (unit + 1) * SPAN].astype(bf16)
            lines_s[...] = jnp.zeros_like(lines_s)
            time_rows = time_s[...]
            for start in range(0, 2 * HEADS, rows):
                size = min(rows, 2 * HEADS - start)
                lines_s[:size, start : start + rows] = time_rows[start : start + size, own]
            small_o[0, s] = lines_s[...].astype(bf16)
        vectors = [(lines_ref[k : k + 1, :], CHANNELS // shards) for k in range(CONV + 1)]
        vectors += [(post_ref[...], INNER // shards)]
        lines_s[...] = jnp.zeros_like(lines_s)
        for s in range(shards):
            line = 0
            for vector, width in vectors:
                for start in range(0, width, SPAN):
                    size = min(SPAN, width - start)
                    begin = s * width + start
                    lines_s[line : line + 1, :size] = vector[:, begin : begin + size]
                    line += 1
            small_o[1, s] = lines_s[...].astype(bf16)


def whole(shape):
    return pl.BlockSpec(
        shape, lambda s, c, *_: (0,) * len(shape), pipeline_mode=pl.Buffered(1)
    )


def layer(
    tokens, cotangent, lengths, wide, time, narrow, vectors, timestep_bias, decay_log, skip_gain
):
    count, length = tokens.shape[:2]
    shards = vectors.shape[0]
    rows = D // shards
    blocks = length // BLOCK
    spans = length // SPAN
    bias = timestep_bias[None]
    decay = decay_log[None]
    grid = (count, blocks)
    sds = jax.ShapeDtypeStruct

    def ahead(rows, width=BLOCK):
        return pl.BlockSpec((1, rows, width), lambda s, c, *_: (s, 0, c))

    def back(rows, width=BLOCK):
        return pl.BlockSpec((1, rows, width), lambda s, c, *_: (s, 0, blocks - 1 - c))

    def tall(reverse):
        if reverse:
            return pl.BlockSpec((1, BLOCK, D), lambda s, c, *_: (s, blocks - 1 - c, 0))
        return pl.BlockSpec((1, BLOCK, D), lambda s, c, *_: (s, c, 0))

    def states(reverse):
        if reverse:
            return pl.BlockSpec((1, SUBS, INNER, SPAN), lambda s, c, *_: (s, blocks - 1 - c, 0, 0))
        return pl.BlockSpec((1, SUBS, INNER, SPAN), lambda s, c, *_: (s, c, 0, 0))

    def turned(reverse):
        if reverse:
            return pl.BlockSpec((1, BLOCK, SPAN), lambda s, c, *_: (s, blocks - 1 - c, 0))
        return pl.BlockSpec((1, BLOCK, SPAN), lambda s, c, *_: (s, c, 0))

    params = pltpu.CompilerParams(
        dimension_semantics=("arbitrary", "arbitrary"), vmem_limit_bytes=VMEM_LIMIT
    )
    state_shape = sds((count, spans, INNER, SPAN), bf16)
    gate, fin, filt, act, step_rows, step_cols, state = pl.pallas_call(
        enter_kernel,
        grid_spec=pltpu.PrefetchScalarGridSpec(
            num_scalar_prefetch=1,
            grid=grid,
            in_specs=[
                tall(False), whole((D, WIDE)), whole(time.shape), whole(vectors.shape),
                whole((1, 48)), whole((1, HEADS)),
            ],
            out_specs=[
                ahead(INNER), ahead(CHANNELS), ahead(CHANNELS), ahead(CHANNELS), ahead(240), turned(False), states(False),
            ],
            scratch_shapes=[
                pltpu.VMEM((CHANNELS, SPAN), bf16),
                pltpu.VMEM((INNER, SPAN), f32),
                pltpu.VMEM((CONV + 1, CHANNELS, SPAN), f32),
                pltpu.VMEM((WIDE, D), bf16),
                pltpu.VMEM((48, D), f32),
                pltpu.VMEM((1, D), f32),
                pltpu.VMEM((48, SPAN), f32),
                pltpu.VMEM((48, BLOCK), f32),
                pltpu.VMEM((BLOCK, BLOCK), bf16),
                pltpu.VMEM((BLOCK, BLOCK), bf16),
            ],
        ),
        out_shape=[
            sds((count, INNER, length), bf16),
            sds((count, CHANNELS, length), bf16),
            sds((count, CHANNELS, length), bf16),
            sds((count, CHANNELS, length), bf16),
            sds((count, 240, length), f32),
            sds((count, length, SPAN), f32),
            state_shape,
        ],
        compiler_params=params,
        name="enter",
    )(lengths, tokens, wide, time, vectors, bias, decay)

    across = 2 * D // SPAN
    result, dgate, dval, dio, sums, dstate, rstate, narrow_grad, post_grad, skip_grad = pl.pallas_call(
        middle_kernel,
        grid_spec=pltpu.PrefetchScalarGridSpec(
            num_scalar_prefetch=1,
            grid=grid,
            in_specs=[
                pl.BlockSpec(memory_space=pltpu.SMEM),
                tall(True), tall(True), back(INNER), back(CHANNELS), back(240), turned(True), states(True),
                whole((INNER, D)), whole(vectors.shape),
            ],
            out_specs=[
                tall(True), back(INNER), back(INNER), back(256), back(120), states(True), states(True),
                whole((across, shards, rows, SPAN)), whole((1, INNER)), whole((HEADS, SPAN)),
            ],
            scratch_shapes=[
                pltpu.VMEM((INNER, SPAN), f32),
                pltpu.VMEM((INNER, SPAN), f32),
                pltpu.VMEM((INNER, BLOCK), f32),
                pltpu.VMEM((INNER, BLOCK), f32),
                pltpu.VMEM((INNER, BLOCK), f32),
                pltpu.VMEM((INNER, BLOCK), f32),
                pltpu.VMEM((SUBS, HEADS, SPAN, SPAN), bf16),
                pltpu.VMEM((SUBS, HEADS, 3 * SPAN, SPAN), bf16),
                pltpu.VMEM((SUBS, INNER, SPAN), bf16),
                pltpu.VMEM((BLOCK, D), bf16),
                pltpu.VMEM((8, BLOCK), f32),
                pltpu.VMEM((INNER, SPAN), f32),
                pltpu.VMEM((INNER, D), f32),
                pltpu.VMEM((INNER, SPAN), f32),
            ],
        ),
        out_shape=[
            sds((count, length, D), bf16),
            sds((count, INNER, length), bf16),
            sds((count, INNER, length), bf16),
            sds((count, 256, length), f32),
            sds((count, 120, length), f32),
            state_shape,
            state_shape,
            sds((across, shards, rows, SPAN), bf16),
            sds((1, INNER), f32),
            sds((HEADS, SPAN), f32),
        ],
        compiler_params=params,
        name="middle",
    )(lengths, skip_gain, tokens, cotangent, gate, act, step_rows, step_cols, state, narrow, vectors)

    dfilt, draw, lines, heads = pl.pallas_call(
        leave_kernel,
        grid_spec=pltpu.PrefetchScalarGridSpec(
            num_scalar_prefetch=1,
            grid=grid,
            in_specs=[
                ahead(CHANNELS), ahead(CHANNELS), ahead(CHANNELS), ahead(240), ahead(INNER), ahead(256), ahead(120),
                states(False), states(False), whole((1, HEADS)), whole((HEADS, SPAN)),
            ],
            out_specs=[
                ahead(CHANNELS), ahead(48), whole((8, CHANNELS)), whole((8, SPAN)),
            ],
            scratch_shapes=[
                pltpu.VMEM((INNER, SPAN), f32),
                pltpu.VMEM((HEADS, BLOCK), f32),
                pltpu.VMEM((CHANNELS, BLOCK), f32),
                pltpu.VMEM((CHANNELS, SPAN), bf16),
                pltpu.VMEM((CHANNELS, SPAN), f32),
                pltpu.VMEM((CONV, CHANNELS, SPAN), f32),
                pltpu.VMEM((48, SPAN), f32),
                pltpu.VMEM((48, SPAN), f32),
                pltpu.VMEM((48, SPAN), f32),
                pltpu.VMEM((48, BLOCK), f32),
                pltpu.VMEM((3 * BLOCK, BLOCK), bf16),
                pltpu.VMEM((3 * BLOCK, BLOCK), bf16),
            ],
        ),
        out_shape=[
            sds((count, CHANNELS, length), bf16),
            sds((count, 48, length), bf16),
            sds((8, CHANNELS), f32),
            sds((8, SPAN), f32),
        ],
        compiler_params=params,
        name="leave",
    )(lengths, filt, act, fin, step_rows, dval, dio, sums, dstate, rstate, decay, skip_grad)

    dfin, wide_grad, small_grad = pl.pallas_call(
        widen_kernel,
        grid_spec=pltpu.PrefetchScalarGridSpec(
            num_scalar_prefetch=1,
            grid=grid,
            in_specs=[
                tall(False), ahead(INNER), ahead(CHANNELS),
                pl.BlockSpec(
                    (1, CHANNELS, SPAN),
                    lambda s, c, *_: (s, 0, jnp.minimum(SUBS * (c + 1), spans - 1)),
                ),
                ahead(48),
                whole(vectors.shape),
                whole((8, CHANNELS)), whole((1, INNER)),
            ],
            out_specs=[
                ahead(CHANNELS), whole((WIDE // SPAN, shards, rows, SPAN)), whole((2, shards, rows, SPAN)),
            ],
            scratch_shapes=[
                pltpu.VMEM((CONV, CHANNELS, SPAN), f32),
                pltpu.VMEM((D, WIDE), f32),
                pltpu.VMEM((48, D), f32),
                pltpu.VMEM((1, D), f32),
                pltpu.VMEM((rows, SPAN), f32),
            ],
        ),
        out_shape=[
            sds((count, CHANNELS, length), bf16),
            sds((WIDE // SPAN, shards, rows, SPAN), bf16),
            sds((2, shards, rows, SPAN), bf16),
        ],
        compiler_params=params,
        name="widen",
    )(lengths, tokens, dgate, dfilt, dfilt, draw, vectors, lines, post_grad)
    return result, (dgate, dfin, draw), wide_grad, narrow_grad, small_grad, heads


def peer(rep, shard):
    return {"rep": rep, "shard": shard}


def remote(src, dst, send, recv, device):
    return pltpu.make_async_remote_copy(
        src_ref=src, dst_ref=dst, send_sem=send, recv_sem=recv,
        device_id=device, device_id_type=pl.DeviceIdType.MESH,
    )


def greet(devices):
    barrier = pltpu.get_barrier_semaphore()
    for device in devices:
        pl.semaphore_signal(barrier, inc=1, device_id=device, device_id_type=pl.DeviceIdType.MESH)
    pl.semaphore_wait(barrier, len(devices))


STRIDE = 2


def reduce_kernel(
    lines, wide,
    wide_ref, narrow_ref, small_ref, heads_ref,
    tok_ref, cot_ref, dgate_ref, dfin_ref, draw_ref, weight_ref, time_ref, vectors_ref,
    out_ref, heads_out_ref, slope_ref,
    own_s, near_s, sum_s, p1_s, q1_s, t0_s, t1_s, p2_s, q2_s, r_s, z_s,
    hc_s, hx_s, hy_s, hz_s,
    send_sem, recv_sem, hsend_sem, hrecv_sem, near_sem, arrive_sem, own_sem,
    heads_s, weight_s, turned_s, gain_s, total_s, tok_s, cot_s, dgate_s, dfin_s, draw_s, slope_s,
    in_sem, put_sem, weight_sem,
):
    piece, rows = out_ref.shape[3:5]
    sources = (wide_ref, narrow_ref, small_ref)
    rep = lax.axis_index("rep")
    shard = lax.axis_index("shard")
    core, x = lax.rem(rep, 2), lax.div(rep, 2)
    y, z = lax.rem(shard, 2), lax.div(shard, 2)
    sibling = peer(rep + 1 - 2 * core, shard)
    partner = peer(rep, shard + 1 - 2 * y)
    across = [peer(lax.rem(x + k, wide) * 2 + core, shard) for k in range(1, wide)]
    along = [peer(rep, lax.rem(z + k, lines) * 2 + y) for k in range(1, lines)]
    greet([sibling, partner, *across, *along])
    started = []
    used = [0, 0]

    def launch(src, dst, device, small=False):
        i = used[small]
        used[small] += 1
        pair = (hsend_sem, hrecv_sem) if small else (send_sem, recv_sem)
        copy = remote(src, dst, pair[0].at[i], pair[1].at[i], device)
        copy.start()
        started.append(copy)
        return copy

    def add(where, extents, dst, *srcs):
        flat = 1
        for extent in extents:
            flat *= extent
        for unit in range(*where):

            def body(i, _, unit=unit):
                place = []
                rest = i
                for extent in reversed(extents):
                    place.append(lax.rem(rest, extent))
                    rest = lax.div(rest, extent)
                place = tuple(reversed(place))
                total = None
                for ref, index in srcs:
                    term = ref[index(unit, *place)].astype(f32)
                    total = term if total is None else total + term
                ref, index = dst
                ref[index(unit, *place)] = total.astype(ref.dtype)
                return None

            lax.fori_loop(0, flat, body, None)

    def source(position, order, unit):
        j = (position * 2 + order) * piece + unit
        for ref in sources:
            if j < ref.shape[1]:
                return ref, j
            j -= ref.shape[1]
        return None, None

    def chunk(*where):
        units = pl.ds(where[0], where[1] - where[0])
        near = []
        own = []
        for position in range(wide):
            for order in range(2):
                for unit in range(*where):
                    ref, j = source(position, order, unit)
                    if ref is None:
                        continue
                    place = (position, order, unit)
                    i = (position * 2 + order) * piece + unit
                    copy = remote(
                        ref.at[1 - core, j], near_s.at[place], near_sem.at[i], arrive_sem.at[i], sibling
                    )
                    copy.start()
                    started.append(copy)
                    near.append((order, place, copy))
                    copy = pltpu.make_async_copy(ref.at[core, j], own_s.at[place], own_sem.at[i])
                    copy.start()
                    own.append((order, place, copy))
        yield
        for order in range(2):
            for position in range(wide):
                for unit in range(*where):
                    if source(position, order, unit)[0] is None:
                        sum_s[position, order, unit] = jnp.zeros(sum_s.shape[3:], bf16)
            for mine, theirs in zip(own, near):
                if mine[0] != order:
                    continue
                place = mine[1]
                mine[2].wait()
                theirs[2].wait_recv()
                add(
                    (place[2], place[2] + 1), (lines, 2),
                    (sum_s, lambda u, a, b, p=place: (*p, a, b)),
                    (own_s, lambda u, a, b, p=place: (*p, a, b)),
                    (near_s, lambda u, a, b, p=place: (*p, a, b)),
                )
            if order == 0:
                p1 = [
                    launch(sum_s.at[lax.rem(x + k, wide), 0, units], p1_s.at[k - 1, units], across[k - 1])
                    for k in range(1, wide)
                ]
            else:
                q1 = launch(sum_s.at[:, 1, units, :, 1 - y], q1_s.at[:, units], partner)
        yield
        for copy in p1:
            copy.wait_recv()
        add(
            where, (lines, 2),
            (t0_s, lambda u, a, b: (u, a, b)),
            (sum_s, lambda u, a, b: (x, 0, u, a, b)),
            *[(p1_s, lambda u, a, b, k=k: (k, u, a, b)) for k in range(wide - 1)],
        )
        p2 = launch(t0_s.at[units, :, 1 - y], p2_s.at[units], partner)
        q1.wait_recv()
        add(
            where, (wide, lines),
            (t1_s, lambda u, p, a: (p, u, a)),
            (sum_s, lambda u, p, a: (p, 1, u, a, y)),
            (q1_s, lambda u, p, a: (p, u, a)),
        )
        q2 = [
            launch(t1_s.at[lax.rem(x + k, wide), units], q2_s.at[k - 1, units], across[k - 1])
            for k in range(1, wide)
        ]
        yield
        p2.wait_recv()
        add(
            where, (lines,),
            (r_s, lambda u, a: (0, u, a)), (t0_s, lambda u, a: (u, a, y)), (p2_s, lambda u, a: (u, a)),
        )
        for copy in q2:
            copy.wait_recv()
        add(
            where, (lines,),
            (r_s, lambda u, a: (1, u, a)), (t1_s, lambda u, a: (x, u, a)),
            *[(q2_s, lambda u, a, k=k: (k, u, a)) for k in range(wide - 1)],
        )
        last = [
            launch(r_s.at[:, units, lax.rem(z + k, lines)], z_s.at[k - 1, :, units], along[k - 1])
            for k in range(1, lines)
        ]
        yield
        for copy in last:
            copy.wait_recv()
        add(
            where, (2,),
            (out_ref, lambda u, o: (core, x, o, u)), (r_s, lambda u, o: (o, u, z)),
            *[(z_s, lambda u, o, k=k: (k, o, u)) for k in range(lines - 1)],
        )
        mine = out_ref.at[core, x, :, units]
        shares = [launch(mine, mine, device) for device in across]
        yield
        for copy in shares:
            copy.wait_recv()
        half = out_ref.at[core, :, :, units]
        swap = launch(half, half, sibling)
        yield
        swap.wait_recv()
        yield

    blocks = tok_ref.shape[1] // BLOCK
    total_blocks = tok_ref.shape[0] * blocks

    def fetch(b):
        seq, block = divmod(b, blocks)
        slot = b % 2
        part = slice(block * BLOCK, (block + 1) * BLOCK)
        pairs = [
            (tok_ref.at[seq, part, :], tok_s.at[slot]),
            (cot_ref.at[seq, part, :], cot_s.at[slot]),
            (dgate_ref.at[seq, :, part], dgate_s.at[slot]),
            (dfin_ref.at[seq, :, part], dfin_s.at[slot]),
            (draw_ref.at[seq, :, part], draw_s.at[slot]),
        ]
        made = [pltpu.make_async_copy(src, dst, in_sem.at[slot, i]) for i, (src, dst) in enumerate(pairs)]
        for copy in made:
            copy.start()
        return made

    def token_gradient():
        weights = pltpu.make_async_copy(weight_ref, weight_s, weight_sem.at[0])
        weights.start()
        coming = fetch(0)
        join_row(gain_s, vectors_ref, CONV + 1)
        for s in range(time_ref.shape[0]):
            width = time_ref.shape[2]
            turned_s[:, s * width : (s + 1) * width] = time_ref[s].astype(f32)
        total_s[...] = jnp.zeros_like(total_s)
        put = []
        yield
        for b in range(total_blocks):
            slot = b % 2
            now = coming
            if b + 1 < total_blocks:
                coming = fetch(b + 1)
            for copy in now:
                copy.wait()
            if b == 0:
                weights.wait()
            if b >= 2:
                put[b - 2].wait()
            dnormed = (
                mm(weight_s[:, :INNER], dgate_s[slot])
                + mm(weight_s[:, INNER:], dfin_s[slot])
                + mm_tn(turned_s[...].astype(bf16), draw_s[slot])
            ).T
            tok = tok_s[slot].astype(f32)
            scale = lax.rsqrt(jnp.mean(tok * tok, axis=-1, keepdims=True) + EPS)
            product = dnormed * tok
            total_s[...] += jnp.sum((product * scale).reshape(BLOCK // 8, 8, D), axis=0)
            gain = gain_s[...]
            mean = jnp.mean(product * gain, axis=-1, keepdims=True)
            grad = scale * (gain * dnormed) - tok * (scale * scale * scale * mean)
            slope_s[slot] = (cot_s[slot].astype(f32) + grad).astype(bf16)
            seq, block = divmod(b, blocks)
            copy = pltpu.make_async_copy(
                slope_s.at[slot],
                slope_ref.at[seq, slice(block * BLOCK, (block + 1) * BLOCK), :],
                put_sem.at[slot],
            )
            copy.start()
            put.append(copy)
            yield
        for copy in put[-2:]:
            copy.wait()
        heads_s[:8, :] = heads_ref[...]
        heads_s[8:, :] = jnp.zeros((8, SPAN), f32)
        pre_sum = jnp.sum(total_s[...], axis=0, keepdims=True)
        for k in range(D // SPAN):
            heads_s[8 + k : 9 + k, :] = pre_sum[:, k * SPAN : (k + 1) * SPAN]
        yield

    def sum_heads():
        hc_s[core] = heads_s[...]
        head = launch(hc_s.at[core], hc_s.at[core], sibling, True)
        yield
        head.wait_recv()
        hx_s[x] = hc_s[0] + hc_s[1]
        heads = [launch(hx_s.at[x], hx_s.at[x], device, True) for device in across]
        yield
        for copy in heads:
            copy.wait_recv()
        total = hx_s[0]
        for k in range(1, wide):
            total = total + hx_s[k]
        hy_s[y] = total
        head = launch(hy_s.at[y], hy_s.at[y], partner, True)
        yield
        head.wait_recv()
        hz_s[z] = hy_s[0] + hy_s[1]
        heads = [launch(hz_s.at[z], hz_s.at[z], device, True) for device in along]
        yield
        for copy in heads:
            copy.wait_recv()
        total = hz_s[0]
        for k in range(1, lines):
            total = total + hz_s[k]
        heads_out_ref[...] = total
        yield

    works = [chunk(i, min(i + STRIDE, piece)) for i in range(0, piece, STRIDE)]
    stages = 7
    small_work = sum_heads()
    token_work = token_gradient()
    steps = total_blocks + 2
    early = 4
    for slot in range(max(len(works) + stages - 1, early + 5)):
        left = steps * (slot + 1) // early - steps * slot // early if slot < early else 0
        for g in range(len(works)):
            if 0 <= slot - g < stages:
                next(works[g])
                if left:
                    next(token_work)
                    left -= 1
        for _ in range(left):
            next(token_work)
        if early <= slot < early + 5:
            next(small_work)
    for copy in started:
        copy.wait_send()


def reduce_units(
    wide_units, narrow_units, small_units, heads, tokens, cotangent, parts, weight, time, vectors, wide, lines
):
    rows = wide_units.shape[2]
    halves = [a.reshape(2, -1, lines, 2, rows, SPAN) for a in (wide_units, narrow_units, small_units)]
    used = sum(a.shape[1] for a in halves)
    unit = -(-used // (2 * wide))
    piece = (rows, SPAN)
    chunks = -(-unit // STRIDE)
    copies = (3 * (wide - 1) + 3 + lines - 1) * chunks
    small = 1 + (wide - 1) + 1 + (lines - 1)
    others = max(wide - 1, 1)
    vmem = pl.BlockSpec(memory_space=pltpu.VMEM)
    hbm = pl.BlockSpec(memory_space=pl.ANY)
    return pl.pallas_call(
        partial(reduce_kernel, lines, wide),
        in_specs=[hbm, hbm, hbm, vmem] + [hbm] * 6 + [vmem, vmem],
        out_specs=[vmem, vmem, hbm],
        out_shape=[
            jax.ShapeDtypeStruct((2, wide, 2, unit, *piece), bf16),
            jax.ShapeDtypeStruct((16, SPAN), f32),
            jax.ShapeDtypeStruct(tokens.shape, bf16),
        ],
        scratch_shapes=[
            pltpu.VMEM((wide, 2, unit, lines, 2, *piece), bf16),
            pltpu.VMEM((wide, 2, unit, lines, 2, *piece), bf16),
            pltpu.VMEM((wide, 2, unit, lines, 2, *piece), bf16),
            pltpu.VMEM((others, unit, lines, 2, *piece), bf16),
            pltpu.VMEM((wide, unit, lines, *piece), bf16),
            pltpu.VMEM((unit, lines, 2, *piece), bf16),
            pltpu.VMEM((wide, unit, lines, *piece), bf16),
            pltpu.VMEM((unit, lines, *piece), bf16),
            pltpu.VMEM((others, unit, lines, *piece), bf16),
            pltpu.VMEM((2, unit, lines, *piece), bf16),
            pltpu.VMEM((lines - 1, 2, unit, *piece), bf16),
            pltpu.VMEM((2, 16, SPAN), f32),
            pltpu.VMEM((wide, 16, SPAN), f32),
            pltpu.VMEM((2, 16, SPAN), f32),
            pltpu.VMEM((lines, 16, SPAN), f32),
            pltpu.SemaphoreType.DMA((copies,)),
            pltpu.SemaphoreType.DMA((copies,)),
            pltpu.SemaphoreType.DMA((small,)),
            pltpu.SemaphoreType.DMA((small,)),
            pltpu.SemaphoreType.DMA((2 * wide * unit,)),
            pltpu.SemaphoreType.DMA((2 * wide * unit,)),
            pltpu.SemaphoreType.DMA((2 * wide * unit,)),
            pltpu.VMEM((16, SPAN), f32),
            pltpu.VMEM((D, WIDE), bf16),
            pltpu.VMEM((48, D), f32),
            pltpu.VMEM((1, D), f32),
            pltpu.VMEM((8, D), f32),
            pltpu.VMEM((2, BLOCK, D), bf16),
            pltpu.VMEM((2, BLOCK, D), bf16),
            pltpu.VMEM((2, INNER, BLOCK), bf16),
            pltpu.VMEM((2, CHANNELS, BLOCK), bf16),
            pltpu.VMEM((2, 48, BLOCK), bf16),
            pltpu.VMEM((2, BLOCK, D), bf16),
            pltpu.SemaphoreType.DMA((2, 5)),
            pltpu.SemaphoreType.DMA((2,)),
            pltpu.SemaphoreType.DMA((1,)),
        ],
        compiler_params=pltpu.CompilerParams(
            collective_id=1, has_side_effects=True, vmem_limit_bytes=VMEM_LIMIT
        ),
        name="reduce",
    )(*halves, heads, tokens, cotangent, *parts, weight, time, vectors)


def finish_kernel(
    wide, summed_ref, heads_ref, slope_ref,
    wide_o, time_o, narrow_o, taps_o, offset_o, pre_o, post_o, bias_o, decay_o, skip_o, slope_o, joined_s,
    hold_s,
    slope_sem,
):
    count, length = slope_ref.shape[:2]
    copies = []
    for s in range(count):
        for i in range(4):
            part = slice(i * length // 4, (i + 1) * length // 4)
            there = pltpu.make_async_copy(
                slope_ref.at[s, part, :], hold_s.at[s, part, :], slope_sem.at[0, s, i]
            )
            back = pltpu.make_async_copy(
                hold_s.at[s, part, :], slope_o.at[s, part, :], slope_sem.at[1, s, i]
            )
            there.start()
            copies.append((there, back))
    unit, rows = summed_ref.shape[3:5]
    tiles_wide = wide_o.shape[1] // SPAN // 2
    tiles_narrow = narrow_o.shape[1] // SPAN

    def read(core, j):
        block, i = divmod(j, unit)
        return summed_ref[core, block // 2, block % 2, i].astype(f32)

    for there, back in copies:
        there.wait()
        back.start()
    for core in range(2):
        for j in range(tiles_wide):
            column = (core * tiles_wide + j) * SPAN
            wide_o[:, column : column + SPAN] = read(core, j)
        for j in range(tiles_narrow):
            narrow_o[core * rows : (core + 1) * rows, j * SPAN : (j + 1) * SPAN] = read(
                core, tiles_wide + j
            )
    times = read(0, tiles_wide + tiles_narrow)
    for start in range(0, 2 * HEADS, rows):
        size = min(rows, 2 * HEADS - start)
        time_o[start : start + size, :] = times[:size, start : start + rows]
    vectors = read(1, tiles_wide + tiles_narrow)
    line = 0
    outs = [(taps_o, k) for k in range(CONV)] + [(offset_o, 0), (post_o, 0)]
    for out, k in outs:
        width = out.shape[1]
        for start in range(0, width, SPAN):
            size = min(SPAN, width - start)
            out[k : k + 1, start : start + size] = vectors[line : line + 1, :size]
            line += 1
    for k in range(D // SPAN):
        joined_s[:, k * SPAN : (k + 1) * SPAN] = heads_ref[8 + k : 9 + k, :]
    shard = lax.axis_index("shard")
    for s in range(D // rows):

        @pl.when(shard == s)
        def _(s=s):
            pre_o[...] = joined_s[:, s * rows : (s + 1) * rows]

    bias_o[...] = heads_ref[:1, : 2 * HEADS]
    decay_o[...] = heads_ref[1:2, :HEADS]
    skip_o[...] = heads_ref[2:3, :HEADS]
    for _, back in copies:
        back.wait()


def finish(summed, heads, slope, wide, rows, width):
    shapes = [
        (rows, WIDE), (2 * HEADS, rows), (2 * rows, D), (CONV, width), (1, width), (1, rows), (1, 2 * rows),
        (1, 2 * HEADS), (1, HEADS), (1, HEADS),
    ]
    vmem = pl.BlockSpec(memory_space=pltpu.VMEM)
    hbm = pl.BlockSpec(memory_space=pl.ANY)
    return pl.pallas_call(
        partial(finish_kernel, wide),
        in_specs=[vmem, vmem, hbm],
        out_specs=[vmem] * len(shapes) + [hbm],
        out_shape=[jax.ShapeDtypeStruct(shape, f32) for shape in shapes]
        + [jax.ShapeDtypeStruct(slope.shape, bf16)],
        scratch_shapes=[
            pltpu.VMEM((1, D), f32),
            pltpu.VMEM(slope.shape, bf16),
            pltpu.SemaphoreType.DMA((2, slope.shape[0], 4)),
        ],
        compiler_params=pltpu.CompilerParams(vmem_limit_bytes=VMEM_LIMIT),
        name="finish",
    )(summed, heads, slope)


def gather_kernel(lines, large, kinds, *refs):
    ins, outs = refs[:kinds], refs[kinds : 2 * kinds]
    send_sem, recv_sem, own_sem, small_send, small_recv, *holds = refs[2 * kinds :]
    rep = lax.axis_index("rep")
    shard = lax.axis_index("shard")
    shards = 2 * lines
    core, x = lax.rem(rep, 2), lax.div(rep, 2)
    odd = lax.rem(x, 2)
    y, z = lax.rem(shard, 2), lax.div(shard, 2)
    sibling = peer(rep + 1 - 2 * core, shard)
    across = peer((x + 1 - 2 * odd) * 2 + core, shard)
    partner = peer(rep, shard + 1 - 2 * y)
    has_up, has_down = z < lines - 1, z > 0
    up = peer(rep, jnp.minimum(z + 1, lines - 1) * 2 + y)
    down = peer(rep, jnp.maximum(z - 1, 0) * 2 + y)
    away = [lax.rem(shard + k, shards) for k in range(1, shards)]
    greet([sibling, across, *[peer(rep, other) for other in away]])

    near = [pltpu.make_async_copy(src, hold, own_sem.at[0, i]) for i, (src, hold) in enumerate(zip(ins, holds))]
    own = [
        pltpu.make_async_copy(hold, dst.at[shard], own_sem.at[1, i])
        for i, (hold, dst) in enumerate(zip(holds, outs))
    ]

    def place(group, part, ref, index, side):
        half = ref.shape[-1] // SPAN // 2
        thin = max(1, half * 5 // 13)
        thick = half - 2 * thin
        start = side * half
        if group:
            swap = odd if group == 1 else 1 - odd
            start = start + thick + swap * thin
        columns = pl.ds(pl.multiple_of(start * SPAN, SPAN), (thin if group else thick) * SPAN)
        return ref.at[:, columns] if index is None else ref.at[index, :, columns]

    def copies(way, group, index, device, mine=False, side=None, part=None):
        side = core if side is None else side
        return [
            remote(
                place(group, part, ins[part] if mine else outs[part], None if mine else index, side),
                place(group, part, outs[part], index, side),
                send_sem.at[way, group, part, index],
                recv_sem.at[way, 1 if way == 4 else group, part, index],
                device,
            )
            for part in (range(large) if part is None else (part,))
        ]

    def start(*args, **kw):
        for copy in copies(*args, **kw):
            copy.start()

    def arrive(*args, **kw):
        for copy in copies(*args, **kw):
            copy.wait_recv()

    def sent(*args, **kw):
        for copy in copies(*args, **kw):
            copy.wait_send()

    other = shard + 1 - 2 * y

    def index_of(line, side):
        return line * 2 + side

    for group in (1, 0):
        pl.when(has_up)(lambda group=group: start(1, group, shard, up, mine=True))
        pl.when(has_down)(lambda group=group: start(2, group, shard, down, mine=True))
        start(0, group, shard, partner, mine=True)
    for copy in near:
        copy.start()
    small = []
    for k, index in enumerate(away):
        for part in range(large, kinds):
            copy = remote(
                ins[part], outs[part].at[shard], small_send.at[part - large, k], small_recv.at[part - large, k],
                peer(rep, index),
            )
            copy.start()
            small.append(copy)

    for first, second in zip(near, own):
        first.wait()
        second.start()

    def line_step(k, group, part):
        def spread(index):
            start(0, group, index, partner, part=part)
            if group == 1:
                start(4, 1, index, across, part=part)
            start(3, group, index, sibling, part=part)

        def from_below():
            index = index_of(z - k, y)
            arrive(1, group, index, down, part=part)
            pl.when(has_up)(lambda: start(1, group, index, up, part=part))
            spread(index)

        def from_above():
            index = index_of(z + k, y)
            arrive(2, group, index, up, part=part)
            pl.when(has_down)(lambda: start(2, group, index, down, part=part))
            spread(index)

        pl.when(z - k >= 0)(from_below)
        pl.when(z + k < lines)(from_above)

    def take(group, part, index):
        arrive(0, group, index, partner, part=part)
        if group == 1:
            start(4, 1, index, across, part=part)
        start(3, group, index, sibling, part=part)

    def cross(part, index):
        arrive(4, 2, index, across, part=part)
        start(3, 2, index, sibling, part=part)

    def either(k, action, side):
        pl.when(z - k >= 0)(lambda: action(index_of(z - k, side)))
        if k:
            pl.when(z + k < lines)(lambda: action(index_of(z + k, side)))

    pieces = [(group, part) for group in (1, 0) for part in range(large)]
    for group, part in pieces:
        take(group, part, other)
    for k in range(1, lines):
        for group, part in pieces:
            line_step(k, group, part)
        if k > 1:
            for group, part in pieces:
                either(k - 1, partial(take, group, part), 1 - y)
    for group, part in pieces:
        either(lines - 1, partial(take, group, part), 1 - y)
    for part in range(large):
        either(0, partial(cross, part), 1 - y)
    for k in range(1, lines):
        for part in range(large):
            either(k, partial(cross, part), y)
            either(k, partial(cross, part), 1 - y)
    for index in range(shards):

        @pl.when(index != shard)
        def _(index=index):
            for group in range(3):
                arrive(3, group, index, sibling, side=1 - core)
                sent(3, group, index, sibling)
            sent(4, 1, index, across)

    for line in range(lines):
        for group in range(2):
            index = index_of(line, y)
            sent(0, group, index, partner)

            @pl.when((line <= z) & has_up)
            def _(group=group, index=index):
                sent(1, group, index, up)

            @pl.when((line >= z) & has_down)
            def _(group=group, index=index):
                sent(2, group, index, down)

    for copy in own:
        copy.wait()
    for copy in small:
        copy.wait_send()
    for k in range(1, shards):
        index = lax.rem(shard + shards - k, shards)
        for part in range(large, kinds):
            remote(
                ins[part], outs[part].at[index], small_send.at[part - large, k - 1],
                small_recv.at[part - large, k - 1], peer(rep, index),
            ).wait_recv()


def gather_weights(arrays, large, lines):
    shards = 2 * lines
    hbm = pl.BlockSpec(memory_space=pl.ANY)
    kinds = len(arrays)
    return pl.pallas_call(
        partial(gather_kernel, lines, large, kinds),
        in_specs=[hbm] * kinds,
        out_specs=[hbm] * kinds,
        out_shape=[jax.ShapeDtypeStruct((shards, *a.shape), a.dtype) for a in arrays],
        scratch_shapes=[
            pltpu.SemaphoreType.DMA((5, 3, large, shards)),
            pltpu.SemaphoreType.DMA((5, 3, large, shards)),
            pltpu.SemaphoreType.DMA((2, kinds)),
            pltpu.SemaphoreType.DMA((kinds - large, shards - 1)),
            pltpu.SemaphoreType.DMA((kinds - large, shards - 1)),
            *[pltpu.VMEM(a.shape, a.dtype) for a in arrays],
        ],
        compiler_params=pltpu.CompilerParams(collective_id=0, has_side_effects=True),
        name="gather",
    )(*arrays)


def local(
    tokens,
    cotangent,
    lengths,
    widen_weight,
    timestep_weight,
    narrow_weight,
    filter_weight,
    filter_offset,
    prenorm_gain,
    postnorm_gain,
    timestep_bias,
    decay_log,
    skip_gain,
):
    lines = lax.axis_size("shard") // 2
    wide = lax.axis_size("rep") // 2
    rows = widen_weight.shape[0]
    width = filter_weight.shape[1]
    own = jnp.concatenate(
        [filter_weight.reshape(-1), filter_offset, prenorm_gain, postnorm_gain]
    )
    widen, narrow, timestep, vectors = gather_weights(
        [widen_weight, narrow_weight, timestep_weight.T, own[None]], 2, lines
    )
    widen = widen.reshape(D, WIDE)
    result, parts, wide_grad, narrow_grad, small_grad, heads = layer(
        tokens, cotangent, lengths, widen, timestep, narrow.reshape(INNER, D),
        vectors, timestep_bias, decay_log, skip_gain,
    )
    summed, heads, slope = reduce_units(
        wide_grad, narrow_grad, small_grad, heads, tokens, cotangent, parts, widen, timestep, vectors, wide, lines
    )
    (
        widen_out, timestep_out, narrow_out, filter_out, offset_out, prenorm_out, postnorm_out,
        bias_out, decay_out, skip_out, slope,
    ) = finish(summed, heads, slope, wide, rows, width)
    return (
        result, slope, widen_out, timestep_out.T, narrow_out, filter_out,
        *[row.reshape(-1) for row in (offset_out, prenorm_out, postnorm_out, bias_out, decay_out, skip_out)],
    )


def solution(mesh):
    placed = (
        P(("rep", "shard"), None, None),
        P(("rep", "shard"), None, None),
        P(("rep", "shard")),
        P("shard", None),
        P("shard", None),
        P("shard", None),
        P(None, "shard"),
        P("shard"),
        P("shard"),
        P("shard"),
        P(),
        P(),
        P(),
    )
    return jax.shard_map(
        local,
        mesh=mesh,
        in_specs=placed,
        out_specs=(
            P(("rep", "shard"), None, None),
            P(("rep", "shard"), None, None),
            P("shard", None),
            P("shard", None),
            P("shard", None),
            P(None, "shard"),
            P("shard"),
            P("shard"),
            P("shard"),
            P(),
            P(),
            P(),
        ),
        check_vma=False,
    )
```
